32 devices in a mesh: dp: 16 (over z, x, core), tp: 2 (over y).
Axes of the slice: x: 2, y: 2, z: 4, core: 2. Of those that a mesh axis runs over, the one named last changes fastest.
Arguments:
- layer_input: bfloat16 [16, 1024, 512], P('dp', 'tp'), may hold values from -6 to 6
- memory: bfloat16 [16, 1024, 512], P('dp', 'tp'), may hold values from -6 to 6
- seg_lengths: int32 [16, 16], P('dp'), may hold values from 1 to 256, 1024 in all within a row
- expert_ids: int32 [16, 1], P('dp'), may hold values from 0 to 15
- ln_gains: float32 [3, 512], replicated, may hold values from 0.5 to 1.5
- w_qkv: bfloat16 [3, 512, 512], P(None, None, 'tp'), may hold values from -0.25 to 0.25
- w_out_self: bfloat16 [512, 512], P('tp'), may hold values from -0.75 to 0.75
- w_query_cross: bfloat16 [512, 512], P(None, 'tp'), may hold values from -0.25 to 0.25
- w_kv_cross: bfloat16 [2, 512, 512], P(None, None, 'tp'), may hold values from -0.25 to 0.25
- w_out_cross: bfloat16 [512, 512], P('tp'), may hold values from -6 to 6
- w_up: bfloat16 [16, 512, 2048], P(None, None, 'tp'), may hold values from -0.25 to 0.25
- w_down: bfloat16 [16, 2048, 512], P(None, 'tp'), may hold values from -0.125 to 0.125
- cotangent: bfloat16 [16, 1024, 512], P('dp', 'tp'), may hold values from -6 to 6
Outputs:
- layer_output: bfloat16 [16, 1024, 512], P('dp', 'tp')
- grad_input: float32 [16, 1024, 512], P('dp', 'tp')
- grad_memory: float32 [16, 1024, 512], P('dp', 'tp')
- grad_ln_gains: float32 [3, 512], P(None, 'dp')
- grad_w_qkv: float32 [3, 512, 512], P(None, 'dp', 'tp')
- grad_w_out_self: float32 [512, 512], P('tp', 'dp')
- grad_w_query_cross: float32 [512, 512], P('dp', 'tp')
- grad_w_kv_cross: float32 [2, 512, 512], P(None, 'dp', 'tp')
- grad_w_out_cross: float32 [512, 512], P('tp', 'dp')
- grad_w_up: float32 [16, 512, 2048], P(None, 'dp', 'tp')
- grad_w_down: float32 [16, 2048, 512], P(None, 'tp', 'dp')
The draws below stay inside these ranges and needn't reach their ends.
Inputs may be any that keep to these rules, and one draw needn't show every extreme that they name: `seg_lengths`: each row's lengths sum to 1024; the longest segment of every row has 256 tokens. `expert_ids`: every expert serves some row.
All inputs are finite; a program needn't handle non-finite values.
Results may differ from the reference program's by a relative error of at most 0.024.
Values may be sent and summed in bfloat16 or wider, within the bound.
A program may use at most 256 MiB of HBM per device.

```python
import math
import jax
import jax.numpy as jnp
import numpy as np
from jax import lax

D = 512
HEADS = 8
HEAD_DIM = 64
FF = 2048
EXPERTS = 16
LEN = 1024
MLEN = 1024
SEGS = 16
MOST_SEG = 256
ROWS = 16


def steps_of(stream_key, extent, split, low, top_value):
    level = 1.0
    for position, parts in split:
        steps = jax.random.uniform(jax.random.fold_in(jax.random.fold_in(stream_key, 6), position), (parts,), jnp.float32, low / len(split), top_value / len(split))
        level = level * jnp.repeat(jnp.exp(steps), extent[position] // parts).reshape((-1,) + (1,) * (len(extent) - 1 - position))
    return level


def picks_of(key, rows, number_of, top, lift):
    ranking = jax.random.permutation(jax.random.fold_in(key, 1), number_of)
    favour = ranking
    for power in range(3):
        favour = favour * favour // number_of
    favour = favour * lift // number_of
    tickets = jax.random.randint(jax.random.fold_in(key, 2), (rows, number_of), 0, 4096) + favour
    sure = jax.random.permutation(jax.random.fold_in(key, 3), rows)[jnp.arange(number_of) % rows]
    tickets = jnp.where(jnp.arange(rows)[:, None] == sure[None, :], 1 << 14, tickets)
    merit = tickets * number_of + jnp.arange(number_of)
    return lax.top_k(merit.astype(jnp.int32), top)[1].astype(jnp.int32)


def profile(count, total, limit, slope):
    weights = [(1 << 20) // math.isqrt(rank ** slope) + 1 for rank in range(2, count + 1)]
    surplus, holding = total - limit - (count - 1), [1] * (count - 1)
    while surplus > 0:
        free = [i for i in range(count - 1) if holding[i] < limit]
        pool, budget = sum([weights[i] for i in free]), surplus
        for i in free:
            extra = min(limit - holding[i], max(1, budget * weights[i] // pool), surplus)
            holding[i] = holding[i] + extra
            surplus = surplus - extra
    return np.array([limit] + holding)


def ragged_sizes(stream_key, amount, total, bound, slope):
    if amount == 2:
        one = jax.random.randint(stream_key, (), max(1, total - bound), min(bound, total - 1) + 1)
        return jnp.stack([one, total - one])
    sizes = jnp.asarray(profile(amount, total, bound, slope), jnp.int32)
    couples = (amount - 1) // 2
    source_of, receiver = sizes[1:1 + 2 * couples:2], sizes[2:2 + 2 * couples:2]
    room = jnp.minimum(source_of - 1, bound - receiver)
    moved = jax.random.randint(jax.random.fold_in(stream_key, 1), (couples,), 0, 1 << 20) % (room + 1)
    sizes = sizes.at[1:1 + 2 * couples:2].set(source_of - moved).at[2:2 + 2 * couples:2].set(receiver + moved)
    return sizes[jax.random.permutation(jax.random.fold_in(stream_key, 2), amount)]


def scatter_about(stream_key, shape, width, bound, shards=(), kind=jnp.bfloat16):
    drawn = width * jax.random.normal(stream_key, shape, jnp.float32)
    if shards:
        drawn = drawn * steps_of(stream_key, shape, shards, -0.22, 0.18)
    return jnp.clip(drawn, -bound, bound).astype(kind)


def setup_inputs(seed: int = 0) -> dict:
    key_of = jax.random.split(jax.random.key(seed), 14)
    layer_input = scatter_about(key_of[0], (ROWS, LEN, D), 1.0, 6.0, ((0, 16), (1, 2)))
    memory = scatter_about(key_of[1], (ROWS, MLEN, D), 1.0, 6.0, ((0, 16), (1, 2)))
    seg_lengths = jax.vmap(lambda own: ragged_sizes(own, SEGS, LEN, MOST_SEG, 2))(jax.random.split(key_of[2], ROWS)).reshape((ROWS, SEGS)).astype(jnp.int32)
    expert_ids = picks_of(key_of[3], ROWS, EXPERTS, 1, 0)
    ln_gains = jnp.clip(1.0 + 0.1 * jax.random.normal(key_of[4], (3, D), jnp.float32), 0.5, 1.5)
    w_qkv = scatter_about(key_of[5], (3, D, D), D ** -0.5, 0.25, ((2, 2),))
    w_out_self = scatter_about(key_of[6], (D, D), (D // 8) ** -0.5, 0.75, ((0, 2),))
    w_query_cross = scatter_about(key_of[7], (D, D), D ** -0.5, 0.25, ((1, 2),))
    w_kv_cross = scatter_about(key_of[8], (2, D, D), D ** -0.5, 0.25, ((2, 2),))
    w_out_cross = scatter_about(key_of[9], (D, D), (max(D * 2 // MLEN, 1)) ** -0.5, 6.0, ((0, 2),))
    w_up = scatter_about(key_of[10], (EXPERTS, D, FF), D ** -0.5, 0.25, ((2, 2),))
    w_down = scatter_about(key_of[11], (EXPERTS, FF, D), FF ** -0.5, 0.125, ((1, 2),))
    cotangent = scatter_about(key_of[12], (ROWS, LEN, D), 1.0, 6.0, ((0, 16), (1, 2)))
    return {"layer_input": layer_input, "memory": memory, "seg_lengths": seg_lengths, "expert_ids": expert_ids, "ln_gains": ln_gains, "w_qkv": w_qkv, "w_out_self": w_out_self, "w_query_cross": w_query_cross, "w_kv_cross": w_kv_cross, "w_out_cross": w_out_cross, "w_up": w_up, "w_down": w_down, "cotangent": cotangent}


@jax.custom_vjp
def low(v):
    return lax.optimization_barrier(v.astype(jnp.bfloat16)).astype(jnp.float32)

@jax.custom_vjp
def low_back(v):
    return v

def low_keep(v):
    return (low(v), None)

def low_pass(kept, grad):
    return (grad,)

def back_keep(v):
    return (v, None)

def back_low(kept, grad):
    return (low(grad),)
low.defvjp(low_keep, low_pass)
low_back.defvjp(back_keep, back_low)
epsilon = 1e-05
highest = lax.Precision.HIGHEST

def layer_norm(values, gain):
    centered = values - lax.optimization_barrier(jnp.mean(values, axis=-1, keepdims=True))
    spread = lax.optimization_barrier(jnp.mean(centered * centered, axis=-1, keepdims=True))
    return centered * lax.rsqrt(spread + epsilon) * gain

def segment_mask(lengths, length):
    seg_ends = jnp.cumsum(lengths, dtype=jnp.int32)
    places = jnp.arange(length, dtype=jnp.int32)
    labels = lax.optimization_barrier(jnp.sum((places[:, None] >= seg_ends[None, :]).astype(jnp.int32), axis=1))
    return (labels[:, None] == labels[None, :]) & (places[:, None] >= places[None, :])

def project(values, weight):
    return jnp.dot(values, weight, precision=highest)

def attention(queries, key_rows, value_rows, allowed):
    q_heads = queries.reshape(queries.shape[0], HEADS, HEAD_DIM)
    k_heads = key_rows.reshape(key_rows.shape[0], HEADS, HEAD_DIM)
    v_heads = value_rows.reshape(value_rows.shape[0], HEADS, HEAD_DIM)
    scores = low_back(jnp.einsum('qhd,khd->hqk', q_heads, k_heads, precision=highest) * HEAD_DIM ** (-0.5))
    if allowed is not None:
        scores = jnp.where(allowed[None], scores, -1e+30)
    row_max = lax.optimization_barrier(jnp.max(scores, axis=-1, keepdims=True))
    weights = jnp.exp(scores - row_max)
    row_probs = weights / lax.optimization_barrier(jnp.sum(weights, axis=-1, keepdims=True))
    heads_out = jnp.einsum('hqk,khd->qhd', low(row_probs), v_heads, precision=highest)
    return low_back(low(heads_out.reshape(queries.shape[0], HEADS * HEAD_DIM)))

def row_layer(items, weights):
    row_input, memory_row, lengths, expert = items
    ln_gains, w_qkv, w_out_self, w_query_cross, w_kv_cross, w_out_cross, w_up, w_down = weights
    normed = low(layer_norm(row_input, ln_gains[0]))
    queries = low_back(low(project(normed, w_qkv[0])))
    key_rows = low_back(low(project(normed, w_qkv[1])))
    value_rows = low_back(low(project(normed, w_qkv[2])))
    heads_self = attention(queries, key_rows, value_rows, segment_mask(lengths, row_input.shape[0]))
    state_one = row_input + low_back(project(heads_self, w_out_self))
    normed = low(layer_norm(state_one, ln_gains[1]))
    queries = low_back(low(project(normed, w_query_cross)))
    key_rows = low_back(low(project(memory_row, w_kv_cross[0])))
    value_rows = low_back(low(project(memory_row, w_kv_cross[1])))
    heads_cross = attention(queries, key_rows, value_rows, None)
    state_two = state_one + low_back(project(heads_cross, w_out_cross))
    normed = low(layer_norm(state_two, ln_gains[2]))
    pre_act = low_back(project(normed, w_up[expert]))
    hidden = low(jax.nn.gelu(pre_act, approximate=False))
    return state_two + low_back(project(hidden, w_down[expert]))

def reference(layer_input, memory, seg_lengths, expert_ids, ln_gains, w_qkv, w_out_self, w_query_cross, w_kv_cross, w_out_cross, w_up, w_down, cotangent):
    weights = tuple((tensor.astype(jnp.float32) for tensor in (ln_gains, w_qkv, w_out_self, w_query_cross, w_kv_cross, w_out_cross, w_up, w_down)))

    def forward(inputs, memories, params):

        def one_row(items):
            return row_layer(items, params)
        return lax.map(jax.checkpoint(one_row), (inputs, memories, seg_lengths, expert_ids[:, 0]))
    outputs, pullback = jax.vjp(forward, layer_input.astype(jnp.float32), memory.astype(jnp.float32), weights)
    grad_input, grad_memory, weight_grads = pullback(cotangent.astype(jnp.float32))
    return (outputs.astype(jnp.bfloat16), grad_input, grad_memory, weight_grads[0], weight_grads[1], weight_grads[2], weight_grads[3], weight_grads[4], weight_grads[5], weight_grads[6], weight_grads[7])
```

```python
import math
from functools import partial

import jax
import jax.numpy as jnp
from jax import lax
from jax.experimental import pallas as pl
from jax.experimental.pallas import tpu as pltpu
from jax.sharding import PartitionSpec as P

HEAD_DIM = 64


epsilon = 1e-05


def layer_norm(values, gain):
    centered = values - jnp.mean(values, axis=-1, keepdims=True)
    spread = jnp.mean(centered * centered, axis=-1, keepdims=True)
    return centered * lax.rsqrt(spread + epsilon) * gain


def norm_backward(state, gain, grad_normed, grad_state):
    unused, pullback = jax.vjp(layer_norm, state, gain)
    grad_values, grad_gain = pullback(grad_normed)
    return (grad_state + grad_values, grad_gain)


def segment_mask(lengths, length, count):
    seg_ends = jnp.cumsum(lengths, dtype=jnp.int32)
    places = jnp.arange(length, dtype=jnp.int32)
    labels = jnp.sum((places[:, None] >= seg_ends[None, :]).astype(jnp.int32), axis=1)
    row_places = jnp.arange(count, dtype=jnp.int32)
    return (labels[:, None] == labels[None, :]) & (row_places[:, None] >= places[None, :])


def to_heads(block):
    return block.reshape(block.shape[:-1] + (block.shape[-1] // HEAD_DIM, HEAD_DIM))


def softmax_rows(queries, key_rows, allowed):
    scores = jnp.einsum(
        "qhd,khd->hqk", queries, key_rows, preferred_element_type=jnp.float32
    ) * HEAD_DIM ** (-0.5)
    if allowed is not None:
        scores = jnp.where(allowed[None], scores, -1e30)
    row_max = jnp.max(scores, axis=-1, keepdims=True)
    weights = jnp.exp(scores - row_max)
    return weights / jnp.sum(weights, axis=-1, keepdims=True)


def attend_both(queries, key_rows, value_rows, allowed, grad_heads):
    row_probs = softmax_rows(queries, key_rows, allowed)
    probs_low = row_probs.astype(jnp.bfloat16)
    heads_out = jnp.einsum(
        "hqk,khd->qhd", probs_low, value_rows, preferred_element_type=jnp.float32
    ).astype(jnp.bfloat16)
    grad_probs = jnp.einsum(
        "qhd,khd->hqk", grad_heads, value_rows, preferred_element_type=jnp.float32
    )
    inner_sum = jnp.sum(row_probs * grad_probs, axis=-1, keepdims=True)
    grad_scores = (row_probs * (grad_probs - inner_sum)).astype(jnp.bfloat16)
    grad_queries = jnp.einsum(
        "hqk,khd->qhd", grad_scores, key_rows, preferred_element_type=jnp.float32
    ) * HEAD_DIM ** (-0.5)
    grad_keys = jnp.einsum(
        "hqk,qhd->khd", grad_scores, queries, preferred_element_type=jnp.float32
    ) * HEAD_DIM ** (-0.5)
    grad_values = jnp.einsum(
        "hqk,qhd->khd", probs_low, grad_heads, preferred_element_type=jnp.float32
    )
    return (heads_out, grad_queries, grad_keys, grad_values)


def spread_tokens(normed):
    return lax.all_gather(normed, "tp", axis=1, tiled=True)


def sum_tokens(partial_out):
    return lax.psum_scatter(partial_out, "tp", scatter_dimension=1, tiled=True)


def gather_grads(grad_state):
    return lax.all_gather(grad_state.astype(jnp.bfloat16), "tp", axis=1, tiled=True)


def sum_grads(grad_normed):
    return lax.psum_scatter(grad_normed, "tp", scatter_dimension=1, tiled=True)


def self_partial(normed_all, seg_lengths, w_qkv, w_out_self):
    projected = jnp.einsum(
        "rld,cde->rcle", normed_all, w_qkv, preferred_element_type=jnp.float32
    ).astype(jnp.bfloat16)

    def one_row(items):
        row_proj, lengths = items
        split_heads = to_heads(row_proj)
        length = row_proj.shape[1]
        row_probs = softmax_rows(
            split_heads[0], split_heads[1], segment_mask(lengths, length, length)
        )
        heads_out = jnp.einsum(
            "hqk,khd->qhd",
            row_probs.astype(jnp.bfloat16),
            split_heads[2],
            preferred_element_type=jnp.float32,
        )
        return heads_out.reshape(row_proj.shape[1:]).astype(jnp.bfloat16)

    heads_all = lax.map(one_row, (projected, seg_lengths))
    return jnp.einsum("rle,ed->rld", heads_all, w_out_self, preferred_element_type=jnp.float32)


def self_backward(normed_all, seg_lengths, w_qkv, w_out_self, grad_branch):
    projected = jnp.einsum(
        "rld,cde->rcle", normed_all, w_qkv, preferred_element_type=jnp.float32
    ).astype(jnp.bfloat16)
    grad_heads = jnp.einsum(
        "rld,ed->rle", grad_branch, w_out_self, preferred_element_type=jnp.float32
    ).astype(jnp.bfloat16)

    def one_row(items):
        row_proj, lengths, row_grad = items
        split_heads = to_heads(row_proj)
        length = row_proj.shape[1]
        results = attend_both(
            split_heads[0],
            split_heads[1],
            split_heads[2],
            segment_mask(lengths, length, length),
            to_heads(row_grad),
        )
        return (
            results[0].reshape(length, -1),
            jnp.stack([piece.reshape(length, -1).astype(jnp.bfloat16) for piece in results[1:]]),
        )

    heads_all, grad_proj = lax.map(one_row, (projected, seg_lengths, grad_heads))
    grad_w_out = jnp.einsum(
        "rle,rld->ed", heads_all, grad_branch, preferred_element_type=jnp.float32
    )
    grad_w_qkv = jnp.einsum(
        "rld,rcle->cde", normed_all, grad_proj, preferred_element_type=jnp.float32
    )
    grad_normed = jnp.einsum("rcle,cde->rld", grad_proj, w_qkv, preferred_element_type=jnp.float32)
    return (grad_normed, grad_w_qkv, grad_w_out)


def cross_partial(normed_all, memory_all, w_query_cross, w_kv_cross, w_out_cross):
    queries = jnp.einsum(
        "rld,de->rle", normed_all, w_query_cross, preferred_element_type=jnp.float32
    ).astype(jnp.bfloat16)
    key_value = jnp.einsum(
        "rmd,cde->rcme", memory_all, w_kv_cross, preferred_element_type=jnp.float32
    ).astype(jnp.bfloat16)

    def one_row(items):
        row_query, row_kv = items
        split_kv = to_heads(row_kv)
        row_probs = softmax_rows(to_heads(row_query), split_kv[0], None)
        heads_out = jnp.einsum(
            "hqk,khd->qhd",
            row_probs.astype(jnp.bfloat16),
            split_kv[1],
            preferred_element_type=jnp.float32,
        )
        return heads_out.reshape(row_query.shape).astype(jnp.bfloat16)

    heads_all = lax.map(one_row, (queries, key_value))
    return jnp.einsum("rle,ed->rld", heads_all, w_out_cross, preferred_element_type=jnp.float32)


def cross_core(normed_all, memory_all, w_query_cross, w_kv_cross, w_out_cross, grad_branch):
    queries = jnp.einsum(
        "rld,de->rle", normed_all, w_query_cross, preferred_element_type=jnp.float32
    ).astype(jnp.bfloat16)
    key_value = jnp.einsum(
        "rmd,cde->rcme", memory_all, w_kv_cross, preferred_element_type=jnp.float32
    ).astype(jnp.bfloat16)
    grad_heads = jnp.einsum(
        "rld,ed->rle", grad_branch, w_out_cross, preferred_element_type=jnp.float32
    ).astype(jnp.bfloat16)

    def one_row(items):
        row_query, row_kv, row_grad = items
        split_kv = to_heads(row_kv)
        query_count = row_query.shape[0]
        memory_count = row_kv.shape[1]
        results = attend_both(
            to_heads(row_query), split_kv[0], split_kv[1], None, to_heads(row_grad)
        )
        grad_kv = jnp.stack(
            [results[2].reshape(memory_count, -1), results[3].reshape(memory_count, -1)]
        )
        return (results[0].reshape(query_count, -1), results[1].reshape(query_count, -1), grad_kv)

    heads_all, grad_queries, grad_kv = lax.map(one_row, (queries, key_value, grad_heads))
    grad_w_out = jnp.einsum(
        "rle,rld->ed", heads_all, grad_branch, preferred_element_type=jnp.float32
    )
    return (grad_queries, grad_kv, grad_w_out)


def cross_backward(normed_all, memory_all, w_query_cross, w_kv_cross, w_out_cross, grad_branch):
    grad_queries, grad_kv, grad_w_out = cross_core(
        normed_all, memory_all, w_query_cross, w_kv_cross, w_out_cross, grad_branch
    )
    grad_queries = grad_queries.astype(jnp.bfloat16)
    grad_kv = grad_kv.astype(jnp.bfloat16)
    grad_w_query = jnp.einsum(
        "rld,rle->de", normed_all, grad_queries, preferred_element_type=jnp.float32
    )
    grad_w_kv = jnp.einsum("rmd,rcme->cde", memory_all, grad_kv, preferred_element_type=jnp.float32)
    grad_normed = jnp.einsum(
        "rle,de->rld", grad_queries, w_query_cross, preferred_element_type=jnp.float32
    )
    grad_memory = jnp.einsum(
        "rcme,cde->rmd", grad_kv, w_kv_cross, preferred_element_type=jnp.float32
    )
    return (grad_normed, grad_memory, grad_w_query, grad_w_kv, grad_w_out)


def expert_rows(weights, expert):
    return lax.dynamic_index_in_dim(weights, expert, 0, keepdims=False)


def ffn_partial(normed_all, expert_ids, w_up, w_down):

    def one_row(items):
        normed_row, expert = items
        pre_act = jnp.dot(normed_row, expert_rows(w_up, expert), preferred_element_type=jnp.float32)
        hidden = jax.nn.gelu(pre_act, approximate=False).astype(jnp.bfloat16)
        return jnp.dot(hidden, expert_rows(w_down, expert), preferred_element_type=jnp.float32)

    return lax.map(one_row, (normed_all, expert_ids[:, 0]))


def ffn_backward(normed_all, expert_ids, w_up, w_down, grad_branch):

    def one_row(items):
        normed_row, expert, grad_row = items
        up_rows = expert_rows(w_up, expert)
        down_rows = expert_rows(w_down, expert)
        pre_act = jnp.dot(normed_row, up_rows, preferred_element_type=jnp.float32)
        activated, gelu_back = jax.vjp(partial(jax.nn.gelu, approximate=False), pre_act)
        hidden = activated.astype(jnp.bfloat16)
        grad_hidden = lax.dot_general(
            grad_row, down_rows, (((1,), (1,)), ((), ())), preferred_element_type=jnp.float32
        )
        grad_pre = gelu_back(grad_hidden)[0].astype(jnp.bfloat16)
        grad_down = lax.dot_general(
            hidden, grad_row, (((0,), (0,)), ((), ())), preferred_element_type=jnp.float32
        )
        grad_up = lax.dot_general(
            normed_row, grad_pre, (((0,), (0,)), ((), ())), preferred_element_type=jnp.float32
        )
        grad_normed = lax.dot_general(
            grad_pre, up_rows, (((1,), (1,)), ((), ())), preferred_element_type=jnp.float32
        )
        return (grad_normed, grad_up, grad_down)

    grad_normed, row_up, row_down = lax.map(one_row, (normed_all, expert_ids[:, 0], grad_branch))
    choose = (
        expert_ids[:, 0][:, None] == jnp.arange(w_up.shape[0], dtype=jnp.int32)[None, :]
    ).astype(jnp.float32)
    grad_w_up = jnp.einsum("re,rdf->edf", choose, row_up, precision=lax.Precision.HIGHEST)
    grad_w_down = jnp.einsum("re,rfd->efd", choose, row_down, precision=lax.Precision.HIGHEST)
    return (grad_normed, grad_w_up, grad_w_down)


def run_forward(layer_input, memory, seg_lengths, expert_ids, ln_gains, attn_weights, w_up, w_down):
    w_qkv, w_out_self, w_query_cross, w_kv_cross, w_out_cross = attn_weights
    state_zero = layer_input.astype(jnp.float32)
    normed_local = layer_norm(state_zero, ln_gains[0]).astype(jnp.bfloat16)
    memory_all = lax.all_gather(memory, "tp", axis=1, tiled=True)
    normed_self = spread_tokens(normed_local)
    state_one = state_zero + sum_tokens(self_partial(normed_self, seg_lengths, w_qkv, w_out_self))
    normed_cross = spread_tokens(layer_norm(state_one, ln_gains[1]).astype(jnp.bfloat16))
    state_two = state_one + sum_tokens(
        cross_partial(normed_cross, memory_all, w_query_cross, w_kv_cross, w_out_cross)
    )
    normed_ffn = spread_tokens(layer_norm(state_two, ln_gains[2]).astype(jnp.bfloat16))
    state_three = state_two + sum_tokens(ffn_partial(normed_ffn, expert_ids, w_up, w_down))
    return (
        state_three,
        (state_zero, state_one, state_two, normed_self, normed_cross, normed_ffn, memory_all),
    )


def per_device(
    layer_input,
    memory,
    seg_lengths,
    expert_ids,
    ln_gains,
    w_qkv,
    w_out_self,
    w_query_cross,
    w_kv_cross,
    w_out_cross,
    w_up,
    w_down,
    cotangent,
):
    attn_weights = (w_qkv, w_out_self, w_query_cross, w_kv_cross, w_out_cross)
    use_qkv, use_out_self, use_query, use_kv, use_out_cross = attn_weights
    state_three, kept = run_forward(
        layer_input, memory, seg_lengths, expert_ids, ln_gains, attn_weights, w_up, w_down
    )
    fresh = lax.optimization_barrier((layer_input, memory, state_three))
    unused, kept = run_forward(
        fresh[0], fresh[1], seg_lengths, expert_ids, ln_gains, attn_weights, w_up, w_down
    )
    state_zero, state_one, state_two, normed_self, normed_cross, normed_ffn, memory_all = kept
    grad_state = cotangent.astype(jnp.float32)
    grad_normed, grad_up, grad_down = ffn_backward(
        normed_ffn, expert_ids, w_up, w_down, gather_grads(grad_state)
    )
    grad_state, gain_ffn = norm_backward(state_two, ln_gains[2], sum_grads(grad_normed), grad_state)
    grad_normed, memory_part, grad_w_query, grad_w_kv, grad_w_out_cross = cross_backward(
        normed_cross, memory_all, use_query, use_kv, use_out_cross, gather_grads(grad_state)
    )
    grad_normed, grad_memory = (
        lax.psum_scatter(
            grad_normed.astype(jnp.bfloat16), "tp", scatter_dimension=1, tiled=True
        ).astype(jnp.float32),
        lax.psum_scatter(
            memory_part.astype(jnp.bfloat16), "tp", scatter_dimension=1, tiled=True
        ).astype(jnp.float32),
    )
    grad_state, gain_cross = norm_backward(state_one, ln_gains[1], grad_normed, grad_state)
    grad_normed, grad_w_qkv, grad_w_out_self = self_backward(
        normed_self, seg_lengths, use_qkv, use_out_self, gather_grads(grad_state)
    )
    grad_state, gain_self = norm_backward(
        state_zero, ln_gains[0], sum_grads(grad_normed), grad_state
    )
    summed = (
        lax.psum_scatter(
            grad_w_qkv.astype(jnp.bfloat16), "dp", scatter_dimension=1, tiled=True
        ).astype(jnp.float32),
        lax.psum_scatter(
            grad_w_out_self.astype(jnp.bfloat16), "dp", scatter_dimension=1, tiled=True
        ).astype(jnp.float32),
        lax.psum_scatter(
            grad_w_query.astype(jnp.bfloat16), "dp", scatter_dimension=0, tiled=True
        ).astype(jnp.float32),
        lax.psum_scatter(
            grad_w_kv.astype(jnp.bfloat16), "dp", scatter_dimension=1, tiled=True
        ).astype(jnp.float32),
        lax.psum_scatter(
            grad_w_out_cross.astype(jnp.bfloat16), "dp", scatter_dimension=1, tiled=True
        ).astype(jnp.float32),
        lax.psum_scatter(
            grad_up.astype(jnp.bfloat16), "dp", scatter_dimension=1, tiled=True
        ).astype(jnp.float32),
        lax.psum_scatter(
            grad_down.astype(jnp.bfloat16), "dp", scatter_dimension=2, tiled=True
        ).astype(jnp.float32),
    )
    grad_w_qkv, grad_w_out_self, grad_w_query, grad_w_kv, grad_w_out_cross, grad_up, grad_down = (
        summed
    )
    gain_total = lax.psum(jnp.stack([gain_self, gain_cross, gain_ffn]), ("dp", "tp"))
    share_width = gain_total.shape[1] // lax.axis_size("dp")
    gain_share = lax.dynamic_slice_in_dim(
        gain_total, lax.axis_index("dp") * share_width, share_width, 1
    )
    return (
        state_three.astype(jnp.bfloat16),
        grad_state,
        grad_memory,
        gain_share,
        grad_w_qkv,
        grad_w_out_self,
        grad_w_query,
        grad_w_kv,
        grad_w_out_cross,
        grad_up,
        grad_down,
    )


F32, BF16 = jnp.float32, jnp.bfloat16
MESH = pl.DeviceIdType.MESH
LOG2E = math.log2(math.e)
QSCALE = LOG2E * HEAD_DIM ** -0.5
NN = (((1,), (0,)), ((), ()))
NT = (((1,), (1,)), ((), ()))
TN = (((0,), (0,)), ((), ()))

LEN, WIDTH, COLS, HIDDEN, BLOCK, HALF = 1024, 512, 256, 1024, 256, 512
BLOCKS = LEN // BLOCK


def dot(left, right, dims=NN):
    return lax.dot_general(left, right, dims, preferred_element_type=F32)


def head_mask(block, side):
    lanes = lax.broadcasted_iota(jnp.int32, block.shape, 1)
    keep = (lanes >= HEAD_DIM) if side else (lanes < HEAD_DIM)
    return jnp.where(keep, block, jnp.zeros_like(block))


def window_bias(key_at, query_at, keys, queries, starts):
    key_place = key_at + lax.broadcasted_iota(jnp.int32, (keys, queries), 0)
    query_place = query_at + lax.broadcasted_iota(jnp.int32, (keys, queries), 1)
    return jnp.where((key_place >= starts) & (key_place <= query_place), 0.0, -1e30)


def attend_block(qs, k, vt, ht, lse, q_at, q_len, k_at, k_len, bias):
    for h in range(4):
        lanes = slice((h // 2) * 128, (h // 2) * 128 + 128)
        rows = slice(h * 64, h * 64 + 64)
        keys = head_mask(k[pl.ds(k_at, k_len), lanes], h % 2)
        s = dot(keys, qs[pl.ds(q_at, q_len), lanes], NT)
        if bias is not None:
            s = s + bias
        top = jnp.max(s, axis=0, keepdims=True)
        p = jnp.exp2(s - top)
        total = jnp.sum(p, axis=0, keepdims=True)
        out = dot(vt[rows, pl.ds(k_at, k_len)], p.astype(BF16)) * (1.0 / total)
        ht[rows, pl.ds(q_at, q_len)] = out.astype(BF16)
        lse[h:h + 1, pl.ds(q_at, q_len)] = top + jnp.log2(total)


def attend_back_block(qs, k, v, kt, gh, lse, inner, dqt, dk, dv, k_at, k_len, q_at, q_len, bias):
    for pair in range(2):
        lanes = slice(pair * 128, pair * 128 + 128)
        sum_k, sum_v = None, None
        qp = qs[pl.ds(q_at, q_len), lanes]
        gp = gh[pl.ds(q_at, q_len), lanes]
        for side in range(2):
            h = pair * 2 + side
            rows = slice(h * 64, h * 64 + 64)
            keys = head_mask(k[pl.ds(k_at, k_len), lanes], side)
            vals = head_mask(v[pl.ds(k_at, k_len), lanes], side)
            s = dot(keys, qp, NT)
            if bias is not None:
                s = s + bias
            p = jnp.exp2(s - lse[h:h + 1, pl.ds(q_at, q_len)])
            dp = dot(vals, gp, NT)
            ds = (p * (dp - inner[h:h + 1, pl.ds(q_at, q_len)])).astype(BF16)
            part_v = dot(p.astype(BF16), head_mask(gp, side))
            part_k = dot(ds, head_mask(qp, side))
            sum_v = part_v if sum_v is None else sum_v + part_v
            sum_k = part_k if sum_k is None else sum_k + part_k
            dqt[rows, pl.ds(q_at, q_len)] += dot(kt[rows, pl.ds(k_at, k_len)], ds)
        dv[pl.ds(k_at, k_len), lanes] = sum_v.astype(BF16)
        dk[pl.ds(k_at, k_len), lanes] = (sum_k * math.log(2.0)).astype(BF16)


def gelu_parts(pre):
    gauss = jnp.exp2(pre * pre * (-0.5 * LOG2E))
    t = 1.0 / (1.0 + (0.3275911 / math.sqrt(2.0)) * jnp.abs(pre))
    poly = t * (0.254829592 * 0.5 + t * (-0.284496736 * 0.5 + t * (
        1.421413741 * 0.5 + t * (-1.453152027 * 0.5 + t * (1.061405429 * 0.5)))))
    tail = poly * gauss
    phi = jnp.where(pre >= 0, 1.0 - tail, tail)
    return phi, phi + pre * (gauss * (1.0 / math.sqrt(2.0 * math.pi)))


def normalise(x):
    c = x - jnp.mean(x, axis=-1, keepdims=True)
    r = lax.rsqrt(jnp.mean(c * c, axis=-1, keepdims=True) + epsilon)
    return c * r, r


def norm_back(state, gain, grad):
    xhat, r = normalise(state)
    y = grad * gain
    m1 = jnp.mean(y, axis=-1, keepdims=True)
    m2 = jnp.mean(y * xhat, axis=-1, keepdims=True)
    return r * (y - m1 - xhat * m2), jnp.sum(grad * xhat, axis=0, keepdims=True)


def block_rows(i):
    return pl.ds(pl.multiple_of(i * BLOCK, BLOCK), BLOCK)


def each(count, body):
    def step(i, carry):
        body(i)
        return carry

    lax.fori_loop(0, count, step, 0)


def layer_kernel(
    n_dp,
    lens, expert, gains, x_in, mem_in, cot_in, wqkv_in, wos_in, wq_in, wkv_in, woc_in, up_in, down_in,
    lo_out, gi_out, gm_out, eu_out, ed_out, a1_out, a2_out, g_out,
    x, mem, cot, wqkv, wos, wq, wkv, woc, up, down, starts,
    s1, s2, gs, n0, n1, n2, q0, k0, v0, q1, k1, v1, kt0, vt0, kt1, vt1, ht0, ht1, lse0, lse1, inner,
    gb, gh, dqt, dq, dk, dv, hid, gpre, nt, eu, ed, a1, a2,
    snd, rcv, sndh, rcvh, leaving, half_out, gain_sum, g_send,
    y_send, y_recv, c_send, c_recv, x_send, x_recv, h_send, h_recv, sc_send, sc_recv, g_ssem, g_rsem, o_send, o_recv,
):
    d, t = lax.axis_index("dp"), lax.axis_index("tp")
    c = lax.rem(d, 2)
    k2 = d - c
    row = k2 + t
    lin = d * 2 + t
    n_all = n_dp * 2
    diag = (k2 + 1 - c, 1 - t)
    sib = (k2 + 1 - c, t)
    swaps = c != t
    stays = c == t

    def remote(src, dst, ssem, rsem, to):
        return pltpu.make_async_remote_copy(
            src_ref=src, dst_ref=dst, send_sem=ssem, recv_sem=rsem, device_id=to, device_id_type=MESH)

    own = pl.ds(pl.multiple_of(c * HALF, HALF), HALF)
    other = pl.ds(pl.multiple_of((1 - c) * HALF, HALF), HALF)
    theirs = pl.ds(pl.multiple_of(t * HALF, HALF), HALF)

    brought = [
        (x_in, lambda p: x.at[p]), (wqkv_in, wqkv), (wos_in, wos), (mem_in, lambda p: mem.at[p]), (wq_in, wq),
        (wkv_in, wkv), (woc_in, woc), (up_in, up), (down_in, down), (cot_in, lambda p: cot.at[p]),
    ]
    X, WQKV, WOS, MEM, WQ, WKV, WOC, UP, DOWN, COT = range(10)

    def bring(n, place):
        src, dst = brought[n]
        dst = dst(place) if callable(dst) else dst
        return (lambda: remote(src, dst, y_send.at[n], y_recv.at[n], diag),
                lambda: pltpu.make_async_copy(src, dst, y_recv.at[n]))

    def start_bring(n):
        far, near = bring(n, theirs)

        @pl.when(swaps)
        def _():
            far().start()

    def start_near(n):
        far, near = bring(n, own)

        @pl.when(stays)
        def _():
            near().start()

    def wait_bring(n):
        far, near = bring(n, own)

        @pl.when(swaps)
        def _():
            far().wait_recv()

        @pl.when(stays)
        def _():
            near().wait()

    def share(n, buf):
        return remote(buf.at[own], buf.at[own], c_send.at[n], c_recv.at[n], sib)

    def share_starts():
        return remote(starts, starts, c_send.at[3], c_recv.at[3], sib)

    for n in (X, WQKV, MEM, COT, WOS, WQ, WKV, WOC, UP, DOWN):
        start_near(n)
    barrier = pltpu.get_barrier_semaphore()

    def greet(i):
        to = lax.rem(lin + 1 + i, n_all)
        pl.semaphore_signal(barrier, inc=1, device_id=(lax.div(to, 2), lax.rem(to, 2)), device_id_type=MESH)

    each(n_all - 1, greet)

    @pl.when(stays)
    def _():
        places = lax.broadcasted_iota(jnp.int32, (8, LEN), 1)
        start, level = jnp.int32(0), jnp.zeros((8, LEN), jnp.int32)
        for s in range(lens.shape[1]):
            level = jnp.where(places >= start, start, level)
            start = start + lens[0, s]
        starts[...] = level

    pl.semaphore_wait(barrier, n_all - 1)
    for n in range(10):
        start_bring(n)

    @pl.when(stays)
    def _():
        share_starts().start()

    def wait_near(n):
        near = bring(n, own)[1]

        @pl.when(stays)
        def _():
            near().wait()

    def wait_swapped(n):
        far = bring(n, own)[0]

        @pl.when(swaps)
        def _():
            far().wait_recv()

    wait_bring(X)
    share(0, x).start()

    @pl.when(stays)
    def _():
        wait_near(MEM)
        share(1, mem).start()
        wait_near(COT)
        share(2, cot).start()

    def self_project(i):
        r = block_rows(i)
        xhat, _ = normalise(x[r, :].astype(F32))
        nn = (xhat * gains[0:1, :]).astype(BF16)
        n0[r, :] = nn
        q0[r, :] = (dot(nn, wqkv[0]) * QSCALE).astype(BF16)
        k0[r, :] = dot(nn, wqkv[1]).astype(BF16)
        v0[r, :] = dot(nn, wqkv[2]).astype(BF16)

    wait_bring(WQKV)
    each(2, lambda i: self_project(c * 2 + i))
    share(0, x).wait_recv()
    each(2, lambda i: self_project((1 - c) * 2 + i))
    kt0[...] = k0[...].T
    vt0[...] = v0[...].T

    @pl.when(swaps)
    def _():
        share_starts().wait_recv()

    wait_bring(WOS)

    def exchange(e, i):
        r = block_rows(i)
        return remote(snd.at[e, r], rcv.at[e, r], x_send.at[e, i], x_recv.at[e, i], sib)

    def self_out(i):
        r = block_rows(i)
        snd[0, r, :] = dot(ht0[:, r], wos[...], TN).astype(BF16)
        exchange(0, i).start()

    attend_block(q0, k0, vt0, ht0, lse0, 0, 256, 0, 256, window_bias(0, 0, 256, 256, starts[0:1, 0:256]))
    self_out(0)

    def self_block(j):
        i = j + 1
        q_at = pl.multiple_of(i * 256, 256)
        k_at = pl.multiple_of(j * 256, 256)
        attend_block(q0, k0, vt0, ht0, lse0, q_at, 256, k_at, 512,
                     window_bias(k_at, q_at, 512, 256, starts[0:1, pl.ds(q_at, 256)]))
        self_out(i)

    each(3, self_block)

    wait_swapped(MEM)

    @pl.when(swaps)
    def _():
        share(1, mem).start()

    wait_bring(WKV)

    def memory_project(i):
        r = block_rows(i)
        k1[r, :] = dot(mem[r, :], wkv[0]).astype(BF16)
        v1[r, :] = dot(mem[r, :], wkv[1]).astype(BF16)

    each(2, lambda i: memory_project(c * 2 + i))
    share(1, mem).wait_recv()
    each(2, lambda i: memory_project((1 - c) * 2 + i))
    kt1[...] = k1[...].T
    vt1[...] = v1[...].T
    wait_bring(WQ)
    wait_bring(WOC)

    def cross_block(i):
        r = block_rows(i)
        exchange(0, i).wait_recv()
        state = x[r, :].astype(F32) + (snd[0, r, :].astype(F32) + rcv[0, r, :].astype(F32))
        s1[r, :] = state
        xhat, _ = normalise(state)
        nn = (xhat * gains[1:2, :]).astype(BF16)
        n1[r, :] = nn
        q1[r, :] = (dot(nn, wq[...]) * QSCALE).astype(BF16)
        attend_block(q1, k1, vt1, ht1, lse1, pl.multiple_of(i * 256, 256), 256, 0, LEN, None)
        snd[1, r, :] = dot(ht1[:, r], woc[...], TN).astype(BF16)
        exchange(1, i).start()

    each(BLOCKS, cross_block)

    wait_bring(UP)
    wait_bring(DOWN)
    wait_swapped(COT)

    @pl.when(swaps)
    def _():
        share(2, cot).start()

    share(2, cot).wait_recv()

    def half_exchange(e, i):
        r = block_rows(i)
        return remote(sndh.at[e, r], rcvh.at[e, r], h_send.at[e, i], h_recv.at[e, i], sib)

    def expert_block(i):
        r = block_rows(i)
        exchange(1, i).wait_recv()
        state = s1[r, :] + (snd[1, r, :].astype(F32) + rcv[1, r, :].astype(F32))
        s2[r, :] = state
        xhat, _ = normalise(state)
        nn = (xhat * gains[2:3, :]).astype(BF16)
        n2[r, :] = nn
        for f in range(2):
            cols = slice(f * 512, f * 512 + 512)
            pre = dot(nn, up[:, cols])
            phi, slope = gelu_parts(pre)
            hid[r, cols] = (pre * phi).astype(BF16)
            gpre[r, cols] = (dot(cot[r, :], down[cols, :], NT) * slope).astype(BF16)
        snd[2, r, :] = dot(gpre[r, :], up[...], NT).astype(BF16)
        exchange(2, i).start()
        part = dot(hid[r, :], down[...])
        mine = lax.div(i, 2) == c
        low = lax.rem(i, 2)
        rl = block_rows(low)

        @pl.when(mine)
        def _():
            half_out[rl, :] = s2[r, :] + part

        @pl.when(jnp.logical_not(mine))
        def _():
            sndh[0, rl, :] = part.astype(BF16)
            half_exchange(0, low).start()

    each(BLOCKS, expert_block)

    def scatter(n, buf, out, action):
        def one(s):
            to = lax.rem(d + s, n_dp)
            src = buf.at[pl.ds(pl.multiple_of(to * 32, 32), 32)]
            action(remote(src, out.at[row], sc_send.at[n, s], sc_recv.at[n, row], (to, c)))

        src = buf.at[pl.ds(pl.multiple_of(d * 32, 32), 32)]

        @pl.when(stays)
        def _():
            if action is begin:
                pltpu.make_async_copy(src, out.at[row], sc_recv.at[n, row]).start()

        @pl.when(swaps)
        def _():
            action(remote(src, out.at[row], sc_send.at[n, 0], sc_recv.at[n, row], (d, c)))

        each(n_dp - 1, lambda s: one(s + 1))

    def begin(copy):
        copy.start()

    def finish_send(copy):
        copy.wait_send()

    def collect(n, buf, out):
        def one(i):
            @pl.when(stays & (i == row))
            def _():
                pltpu.make_async_copy(buf.at[pl.ds(0, 32)], out.at[i], sc_recv.at[n, i]).wait()

            @pl.when(jnp.logical_not(stays & (i == row)))
            def _():
                remote(buf.at[pl.ds(0, 32)], out.at[i], sc_send.at[n, 0], sc_recv.at[n, i], diag).wait_recv()

        each(n_dp, one)

    def quarter(i):
        return pl.ds(pl.multiple_of(i * 256, 256), 256)

    nt[...] = n2[...].T

    def up_grads(i):
        eu[:, quarter(i)] = dot(nt[...], gpre[:, quarter(i)]).astype(BF16)

    each(HIDDEN // 256, up_grads)
    scatter(0, eu, eu_out, begin)
    nt[...] = cot[...].T

    def down_grads(i):
        ed[:, quarter(i)] = dot(nt[...], hid[:, quarter(i)]).astype(BF16)

    each(HIDDEN // 256, down_grads)
    scatter(1, ed, ed_out, begin)

    gain_sum[...] = jnp.zeros_like(gain_sum)

    def branch_block(n, i, e, state, base, ht, w_out):
        r = block_rows(i)
        exchange(e, i).wait_recv()
        grad = snd[e, r, :].astype(F32) + rcv[e, r, :].astype(F32)
        step, share_gain = norm_back(state[r, :], gains[n:n + 1, :], grad)
        total = base[r, :].astype(F32) + step
        gs[r, :] = total
        low = total.astype(BF16)
        gb[r, :] = low
        gain_sum[n:n + 1, :] += jnp.where(lax.div(i, 2) == c, share_gain, 0.0)
        gh[r, :] = dot(low, w_out[...], NT).astype(BF16)
        ght = dot(w_out[...], low, NT).astype(BF16).astype(F32)
        prod = ght * ht[:, r].astype(F32)
        for h in range(4):
            inner[h:h + 1, r] = jnp.sum(prod[h * 64:h * 64 + 64], axis=0, keepdims=True)

    each(BLOCKS, lambda i: branch_block(2, i, 2, s2, cot, ht1, woc))
    dqt[...] = jnp.zeros_like(dqt)

    def cross_back(i):
        at = pl.multiple_of(i * 256, 256)
        attend_back_block(q1, k1, v1, kt1, gh, lse1, inner, dqt, dk, dv, at, 256, 0, LEN, None)

    each(BLOCKS, cross_back)
    dq[...] = (dqt[...] * HEAD_DIM ** -0.5).astype(BF16).T

    def cross_grads(i):
        r = block_rows(i)
        snd[3, r, :] = dot(dq[r, :], wq[...], NT).astype(BF16)
        exchange(3, i).start()

    each(BLOCKS, cross_grads)

    def memory_grads(i):
        r = block_rows(i)
        part = dot(dk[r, :], wkv[0], NT) + dot(dv[r, :], wkv[1], NT)
        mine = lax.div(i, 2) == c
        low = lax.rem(i, 2)
        rl = block_rows(low)

        @pl.when(mine)
        def _():
            half_out[pl.ds(pl.multiple_of(HALF + low * BLOCK, BLOCK), BLOCK), :] = part

        @pl.when(jnp.logical_not(mine))
        def _():
            sndh[1, rl, :] = part.astype(BF16)
            half_exchange(1, low).start()

    each(BLOCKS, memory_grads)
    a1[:, 0:256] = dot(ht1[...], gb[...]).T.astype(BF16)
    nt[...] = n1[...].T
    a1[:, 256:512] = dot(nt[...], dq[...]).astype(BF16)
    nt[...] = mem[...].T
    a1[:, 512:768] = dot(nt[...], dk[...]).astype(BF16)
    a1[:, 768:1024] = dot(nt[...], dv[...]).astype(BF16)
    scatter(2, a1, a1_out, begin)

    def leave(n, out):
        buf = leaving.at[n]
        return (lambda: remote(buf, out, o_send.at[n], o_recv.at[n], diag),
                lambda: pltpu.make_async_copy(buf, out, o_recv.at[n]))

    def start_leave(n, out):
        far, near = leave(n, out)

        @pl.when(swaps)
        def _():
            far().start()

        @pl.when(stays)
        def _():
            near().start()

    def wait_leave(n, out):
        far, near = leave(n, out)

        @pl.when(swaps)
        def _():
            far().wait()

        @pl.when(stays)
        def _():
            near().wait()

    for n in range(2):
        for low in range(2):
            half_exchange(n, low).wait_recv()
            r = pl.ds(low * BLOCK, BLOCK)
            whole = half_out[pl.ds(n * HALF + low * BLOCK, BLOCK), :] + rcvh[n, r, :].astype(F32)
            leaving[n, r, :] = whole.astype(BF16)
        start_leave(n, (lo_out, gm_out)[n])

    each(BLOCKS, lambda i: branch_block(1, i, 3, s1, gs, ht0, wos))
    dqt[...] = jnp.zeros_like(dqt)

    def self_back(i):
        at = pl.multiple_of(i * 256, 256)
        attend_back_block(q0, k0, v0, kt0, gh, lse0, inner, dqt, dk, dv, at, 256, at, 512,
                          window_bias(at, at, 256, 512, starts[0:1, pl.ds(at, 512)]))

    each(BLOCKS - 1, self_back)
    attend_back_block(q0, k0, v0, kt0, gh, lse0, inner, dqt, dk, dv, 768, 256, 768, 256,
                      window_bias(768, 768, 256, 256, starts[0:1, 768:1024]))
    dq[...] = (dqt[...] * HEAD_DIM ** -0.5).astype(BF16).T

    nt[...] = n0[...].T
    a2[:, 0:256] = dot(ht0[...], gb[...]).T.astype(BF16)
    a2[:, 256:512] = dot(nt[...], dq[...]).astype(BF16)
    a2[:, 512:768] = dot(nt[...], dk[...]).astype(BF16)
    a2[:, 768:1024] = dot(nt[...], dv[...]).astype(BF16)
    scatter(3, a2, a2_out, begin)

    def input_grads(i):
        r = block_rows(i)
        return dot(dq[r, :], wqkv[0], NT) + dot(dk[r, :], wqkv[1], NT) + dot(dv[r, :], wqkv[2], NT)

    def input_send(low):
        rl = block_rows(low)
        sndh[2, rl, :] = input_grads((1 - c) * 2 + low).astype(BF16)
        half_exchange(2, low).start()

    each(2, input_send)

    def input_keep(low):
        half_out[block_rows(low), :] = input_grads(c * 2 + low)

    each(2, input_keep)

    def input_done(low):
        half_exchange(2, low).wait_recv()
        rl = block_rows(low)
        r = block_rows(c * 2 + low)
        grad = half_out[rl, :] + rcvh[2, rl, :].astype(F32)
        step, share_gain = norm_back(x[r, :].astype(F32), gains[0:1, :], grad)
        gain_sum[0:1, :] += share_gain
        leaving[2, rl, :] = (gs[r, :] + step).astype(BF16)

    each(2, input_done)
    start_leave(2, gi_out)

    number = jnp.full((1, 128), expert[0, 0].astype(F32))
    for j in range(n_dp):
        turned = gain_sum[...] if j == 0 else pltpu.roll(gain_sum[...], (WIDTH - 32 * j) % WIDTH, 1)
        g_send[j] = turned[:, :128]
        g_send[j, 3:4, :] = number

    def gain_copy(s):
        to = lax.rem(lin + s, n_all)
        to_dp = lax.div(to, 2)
        return remote(g_send.at[to_dp], g_out.at[lin], g_ssem.at[s], g_rsem.at[lin], (to_dp, lax.rem(to, 2)))

    each(n_all - 1, lambda s: gain_copy(s + 1).start())
    keep_gain = pltpu.make_async_copy(g_send.at[d], g_out.at[lin], g_rsem.at[lin])
    keep_gain.start()

    wait_leave(0, lo_out)
    wait_leave(1, gm_out)
    wait_leave(2, gi_out)
    for n, (buf, out) in enumerate(((eu, eu_out), (ed, ed_out), (a1, a1_out), (a2, a2_out))):
        collect(n, buf, out)
        scatter(n, buf, out, finish_send)
    keep_gain.wait()

    def gain_wait(s):
        gain_copy(s + 1).wait_send()
        who = lax.rem(lin + s + 1, n_all)
        remote(g_send.at[0], g_out.at[who], g_ssem.at[0], g_rsem.at[who], diag).wait_recv()

    each(n_all - 1, gain_wait)

    @pl.when(swaps)
    def _():
        for n in range(10):
            bring(n, theirs)[0]().wait_send()

    for n, buf in enumerate((x, mem, cot)):
        share(n, buf).wait_send()

    @pl.when(stays)
    def _():
        share_starts().wait_send()

    for e in range(4):
        each(BLOCKS, lambda i: exchange(e, i).wait_send())
    for e in range(3):
        each(2, lambda i: half_exchange(e, i).wait_send())


def paired_layer(n_dp, lens, expert, gains, *arrays):
    bf = lambda *shape: pltpu.VMEM(shape, BF16)
    fl = lambda *shape: pltpu.VMEM(shape, F32)
    dma = lambda *shape: pltpu.SemaphoreType.DMA(shape)
    tokens = bf(LEN, WIDTH)
    heads = bf(LEN, COLS)
    turned = bf(COLS, LEN)
    grads = bf(WIDTH, HIDDEN)
    shares = jax.ShapeDtypeStruct((n_dp, 32, HIDDEN), BF16)
    half = jax.ShapeDtypeStruct((HALF, WIDTH), BF16)
    any_place = pl.BlockSpec(memory_space=pl.ANY)
    return pl.pallas_call(
        partial(layer_kernel, n_dp),
        out_shape=(half, half, half, shares, shares, shares, shares,
                   jax.ShapeDtypeStruct((2 * n_dp, 8, 128), F32)),
        in_specs=[pl.BlockSpec(memory_space=pltpu.SMEM)] * 2 + [pl.BlockSpec(memory_space=pltpu.VMEM)] + [any_place] * 10,
        out_specs=(any_place,) * 8,
        scratch_shapes=[
            tokens, tokens, tokens, bf(3, WIDTH, COLS), bf(COLS, WIDTH), bf(WIDTH, COLS), bf(2, WIDTH, COLS),
            bf(COLS, WIDTH), bf(WIDTH, HIDDEN), bf(HIDDEN, WIDTH), pltpu.VMEM((8, LEN), jnp.int32),
            fl(LEN, WIDTH), fl(LEN, WIDTH), fl(LEN, WIDTH), tokens, tokens, tokens,
            heads, heads, heads, heads, heads, heads, turned, turned, turned, turned, turned, turned,
            fl(8, LEN), fl(8, LEN), fl(8, LEN),
            tokens, heads, fl(COLS, LEN), heads, heads, heads, bf(LEN, HIDDEN), bf(LEN, HIDDEN), bf(WIDTH, LEN),
            grads, grads, grads, grads,
            bf(4, LEN, WIDTH), bf(4, LEN, WIDTH), bf(3, HALF, WIDTH), bf(3, HALF, WIDTH), bf(3, HALF, WIDTH),
            fl(LEN, WIDTH), fl(8, WIDTH), fl(n_dp, 8, 128),
            dma(10), dma(10), dma(4), dma(4), dma(4, 4), dma(4, 4), dma(3, 2), dma(3, 2),
            dma(4, n_dp), dma(4, n_dp), dma(2 * n_dp), dma(2 * n_dp), dma(3), dma(3),
        ],
        compiler_params=pltpu.CompilerParams(
            collective_id=0, has_side_effects=True, vmem_limit_bytes=VMEM_BYTES),
        cost_estimate=pl.CostEstimate(flops=20 * 10**9, bytes_accessed=20 * 2**20, transcendentals=0),
    )(lens, expert, gains, *arrays)


VMEM_BYTES = 63 * 2**20


def per_device_paired(
    layer_input, memory, seg_lengths, expert_ids, ln_gains, w_qkv, w_out_self, w_query_cross, w_kv_cross,
    w_out_cross, w_up, w_down, cotangent,
):
    n_dp = lax.axis_size("dp")
    experts = w_up.shape[0]
    outs = paired_layer(
        n_dp, seg_lengths, expert_ids, ln_gains,
        layer_input[0], memory[0], cotangent[0], w_qkv, w_out_self, w_query_cross, w_kv_cross, w_out_cross,
        expert_rows(w_up, expert_ids[0, 0]), expert_rows(w_down, expert_ids[0, 0]),
    )
    layer_output, grad_input, grad_memory, up_rows, down_rows, cross_rows, self_rows, gain_rows = outs
    served = gain_rows[0::2, 3, 0].astype(jnp.int32)
    order = jnp.argmax(
        (served[None, :] == jnp.arange(experts, dtype=jnp.int32)[:, None]).astype(jnp.int32), axis=1)
    grad_up = jnp.take(up_rows, order, axis=0).astype(F32)
    grad_down = jnp.swapaxes(jnp.take(down_rows, order, axis=0).astype(F32), 1, 2)
    cross = jnp.sum(cross_rows.astype(F32), axis=0)
    own = jnp.sum(self_rows.astype(F32), axis=0)
    gain_share = jnp.sum(gain_rows, axis=0)[:3, :32]
    return (
        layer_output[None],
        grad_input.astype(F32)[None],
        grad_memory.astype(F32)[None],
        gain_share,
        jnp.stack([own[:, 256:512], own[:, 512:768], own[:, 768:1024]]),
        own[:, 0:256].T,
        cross[:, 256:512],
        jnp.stack([cross[:, 512:768], cross[:, 768:1024]]),
        cross[:, 0:256].T,
        grad_up,
        grad_down,
    )


def fits_pairs(mesh, layer_input, seg_lengths, w_up):
    return (
        mesh.shape["tp"] == 2
        and mesh.shape["dp"] == 16
        and layer_input.shape == (mesh.shape["dp"], LEN, WIDTH)
        and w_up.shape == (mesh.shape["dp"], WIDTH, 2 * HIDDEN)
    )


def solution(mesh):
    in_specs = (
        P("dp", "tp", None),
        P("dp", "tp", None),
        P("dp", None),
        P("dp", None),
        P(),
        P(None, None, "tp"),
        P("tp", None),
        P(None, "tp"),
        P(None, None, "tp"),
        P("tp", None),
        P(None, None, "tp"),
        P(None, "tp", None),
        P("dp", "tp", None),
    )
    out_specs = (
        P("dp", "tp", None),
        P("dp", "tp", None),
        P("dp", "tp", None),
        P(None, "dp"),
        P(None, "dp", "tp"),
        P("tp", "dp"),
        P("dp", "tp"),
        P(None, "dp", "tp"),
        P("tp", "dp"),
        P(None, "dp", "tp"),
        P(None, "tp", "dp"),
    )

    def run(*args):
        layer_input, seg_lengths, w_up = args[0], args[2], args[10]
        paired = fits_pairs(mesh, layer_input, seg_lengths, w_up)
        return jax.shard_map(
            per_device_paired if paired else per_device,
            mesh=mesh, in_specs=in_specs, out_specs=out_specs, check_vma=False,
        )(*args)

    return run
```

```python
import math
from functools import partial

import jax
import jax.numpy as jnp
from jax import lax
from jax.experimental import pallas as pl
from jax.experimental.pallas import tpu as pltpu
from jax.sharding import PartitionSpec as P

HEAD_DIM = 64


epsilon = 1e-05


def layer_norm(values, gain):
    centered = values - jnp.mean(values, axis=-1, keepdims=True)
    spread = jnp.mean(centered * centered, axis=-1, keepdims=True)
    return centered * lax.rsqrt(spread + epsilon) * gain


def norm_backward(state, gain, grad_normed, grad_state):
    unused, pullback = jax.vjp(layer_norm, state, gain)
    grad_values, grad_gain = pullback(grad_normed)
    return (grad_state + grad_values, grad_gain)


def segment_mask(lengths, length, count):
    seg_ends = jnp.cumsum(lengths, dtype=jnp.int32)
    places = jnp.arange(length, dtype=jnp.int32)
    labels = jnp.sum((places[:, None] >= seg_ends[None, :]).astype(jnp.int32), axis=1)
    row_places = jnp.arange(count, dtype=jnp.int32)
    return (labels[:, None] == labels[None, :]) & (row_places[:, None] >= places[None, :])


def to_heads(block):
    return block.reshape(block.shape[:-1] + (block.shape[-1] // HEAD_DIM, HEAD_DIM))


def softmax_rows(queries, key_rows, allowed):
    scores = jnp.einsum(
        "qhd,khd->hqk", queries, key_rows, preferred_element_type=jnp.float32
    ) * HEAD_DIM ** (-0.5)
    if allowed is not None:
        scores = jnp.where(allowed[None], scores, -1e30)
    row_max = jnp.max(scores, axis=-1, keepdims=True)
    weights = jnp.exp(scores - row_max)
    return weights / jnp.sum(weights, axis=-1, keepdims=True)


def attend_both(queries, key_rows, value_rows, allowed, grad_heads):
    row_probs = softmax_rows(queries, key_rows, allowed)
    probs_low = row_probs.astype(jnp.bfloat16)
    heads_out = jnp.einsum(
        "hqk,khd->qhd", probs_low, value_rows, preferred_element_type=jnp.float32
    ).astype(jnp.bfloat16)
    grad_probs = jnp.einsum(
        "qhd,khd->hqk", grad_heads, value_rows, preferred_element_type=jnp.float32
    )
    inner_sum = jnp.sum(row_probs * grad_probs, axis=-1, keepdims=True)
    grad_scores = (row_probs * (grad_probs - inner_sum)).astype(jnp.bfloat16)
    grad_queries = jnp.einsum(
        "hqk,khd->qhd", grad_scores, key_rows, preferred_element_type=jnp.float32
    ) * HEAD_DIM ** (-0.5)
    grad_keys = jnp.einsum(
        "hqk,qhd->khd", grad_scores, queries, preferred_element_type=jnp.float32
    ) * HEAD_DIM ** (-0.5)
    grad_values = jnp.einsum(
        "hqk,qhd->khd", probs_low, grad_heads, preferred_element_type=jnp.float32
    )
    return (heads_out, grad_queries, grad_keys, grad_values)


def spread_tokens(normed):
    return lax.all_gather(normed, "tp", axis=1, tiled=True)


def sum_tokens(partial_out):
    return lax.psum_scatter(partial_out, "tp", scatter_dimension=1, tiled=True)


def gather_grads(grad_state):
    return lax.all_gather(grad_state.astype(jnp.bfloat16), "tp", axis=1, tiled=True)


def sum_grads(grad_normed):
    return lax.psum_scatter(grad_normed, "tp", scatter_dimension=1, tiled=True)


def self_partial(normed_all, seg_lengths, w_qkv, w_out_self):
    projected = jnp.einsum(
        "rld,cde->rcle", normed_all, w_qkv, preferred_element_type=jnp.float32
    ).astype(jnp.bfloat16)

    def one_row(items):
        row_proj, lengths = items
        split_heads = to_heads(row_proj)
        length = row_proj.shape[1]
        row_probs = softmax_rows(
            split_heads[0], split_heads[1], segment_mask(lengths, length, length)
        )
        heads_out = jnp.einsum(
            "hqk,khd->qhd",
            row_probs.astype(jnp.bfloat16),
            split_heads[2],
            preferred_element_type=jnp.float32,
        )
        return heads_out.reshape(row_proj.shape[1:]).astype(jnp.bfloat16)

    heads_all = lax.map(one_row, (projected, seg_lengths))
    return jnp.einsum("rle,ed->rld", heads_all, w_out_self, preferred_element_type=jnp.float32)


def self_backward(normed_all, seg_lengths, w_qkv, w_out_self, grad_branch):
    projected = jnp.einsum(
        "rld,cde->rcle", normed_all, w_qkv, preferred_element_type=jnp.float32
    ).astype(jnp.bfloat16)
    grad_heads = jnp.einsum(
        "rld,ed->rle", grad_branch, w_out_self, preferred_element_type=jnp.float32
    ).astype(jnp.bfloat16)

    def one_row(items):
        row_proj, lengths, row_grad = items
        split_heads = to_heads(row_proj)
        length = row_proj.shape[1]
        results = attend_both(
            split_heads[0],
            split_heads[1],
            split_heads[2],
            segment_mask(lengths, length, length),
            to_heads(row_grad),
        )
        return (
            results[0].reshape(length, -1),
            jnp.stack([piece.reshape(length, -1).astype(jnp.bfloat16) for piece in results[1:]]),
        )

    heads_all, grad_proj = lax.map(one_row, (projected, seg_lengths, grad_heads))
    grad_w_out = jnp.einsum(
        "rle,rld->ed", heads_all, grad_branch, preferred_element_type=jnp.float32
    )
    grad_w_qkv = jnp.einsum(
        "rld,rcle->cde", normed_all, grad_proj, preferred_element_type=jnp.float32
    )
    grad_normed = jnp.einsum("rcle,cde->rld", grad_proj, w_qkv, preferred_element_type=jnp.float32)
    return (grad_normed, grad_w_qkv, grad_w_out)


def cross_partial(normed_all, memory_all, w_query_cross, w_kv_cross, w_out_cross):
    queries = jnp.einsum(
        "rld,de->rle", normed_all, w_query_cross, preferred_element_type=jnp.float32
    ).astype(jnp.bfloat16)
    key_value = jnp.einsum(
        "rmd,cde->rcme", memory_all, w_kv_cross, preferred_element_type=jnp.float32
    ).astype(jnp.bfloat16)

    def one_row(items):
        row_query, row_kv = items
        split_kv = to_heads(row_kv)
        row_probs = softmax_rows(to_heads(row_query), split_kv[0], None)
        heads_out = jnp.einsum(
            "hqk,khd->qhd",
            row_probs.astype(jnp.bfloat16),
            split_kv[1],
            preferred_element_type=jnp.float32,
        )
        return heads_out.reshape(row_query.shape).astype(jnp.bfloat16)

    heads_all = lax.map(one_row, (queries, key_value))
    return jnp.einsum("rle,ed->rld", heads_all, w_out_cross, preferred_element_type=jnp.float32)


def cross_core(normed_all, memory_all, w_query_cross, w_kv_cross, w_out_cross, grad_branch):
    queries = jnp.einsum(
        "rld,de->rle", normed_all, w_query_cross, preferred_element_type=jnp.float32
    ).astype(jnp.bfloat16)
    key_value = jnp.einsum(
        "rmd,cde->rcme", memory_all, w_kv_cross, preferred_element_type=jnp.float32
    ).astype(jnp.bfloat16)
    grad_heads = jnp.einsum(
        "rld,ed->rle", grad_branch, w_out_cross, preferred_element_type=jnp.float32
    ).astype(jnp.bfloat16)

    def one_row(items):
        row_query, row_kv, row_grad = items
        split_kv = to_heads(row_kv)
        query_count = row_query.shape[0]
        memory_count = row_kv.shape[1]
        results = attend_both(
            to_heads(row_query), split_kv[0], split_kv[1], None, to_heads(row_grad)
        )
        grad_kv = jnp.stack(
            [results[2].reshape(memory_count, -1), results[3].reshape(memory_count, -1)]
        )
        return (results[0].reshape(query_count, -1), results[1].reshape(query_count, -1), grad_kv)

    heads_all, grad_queries, grad_kv = lax.map(one_row, (queries, key_value, grad_heads))
    grad_w_out = jnp.einsum(
        "rle,rld->ed", heads_all, grad_branch, preferred_element_type=jnp.float32
    )
    return (grad_queries, grad_kv, grad_w_out)


def cross_backward(normed_all, memory_all, w_query_cross, w_kv_cross, w_out_cross, grad_branch):
    grad_queries, grad_kv, grad_w_out = cross_core(
        normed_all, memory_all, w_query_cross, w_kv_cross, w_out_cross, grad_branch
    )
    grad_queries = grad_queries.astype(jnp.bfloat16)
    grad_kv = grad_kv.astype(jnp.bfloat16)
    grad_w_query = jnp.einsum(
        "rld,rle->de", normed_all, grad_queries, preferred_element_type=jnp.float32
    )
    grad_w_kv = jnp.einsum("rmd,rcme->cde", memory_all, grad_kv, preferred_element_type=jnp.float32)
    grad_normed = jnp.einsum(
        "rle,de->rld", grad_queries, w_query_cross, preferred_element_type=jnp.float32
    )
    grad_memory = jnp.einsum(
        "rcme,cde->rmd", grad_kv, w_kv_cross, preferred_element_type=jnp.float32
    )
    return (grad_normed, grad_memory, grad_w_query, grad_w_kv, grad_w_out)


def expert_rows(weights, expert):
    return lax.dynamic_index_in_dim(weights, expert, 0, keepdims=False)


def ffn_partial(normed_all, expert_ids, w_up, w_down):

    def one_row(items):
        normed_row, expert = items
        pre_act = jnp.dot(normed_row, expert_rows(w_up, expert), preferred_element_type=jnp.float32)
        hidden = jax.nn.gelu(pre_act, approximate=False).astype(jnp.bfloat16)
        return jnp.dot(hidden, expert_rows(w_down, expert), preferred_element_type=jnp.float32)

    return lax.map(one_row, (normed_all, expert_ids[:, 0]))


def ffn_backward(normed_all, expert_ids, w_up, w_down, grad_branch):

    def one_row(items):
        normed_row, expert, grad_row = items
        up_rows = expert_rows(w_up, expert)
        down_rows = expert_rows(w_down, expert)
        pre_act = jnp.dot(normed_row, up_rows, preferred_element_type=jnp.float32)
        activated, gelu_back = jax.vjp(partial(jax.nn.gelu, approximate=False), pre_act)
        hidden = activated.astype(jnp.bfloat16)
        grad_hidden = lax.dot_general(
            grad_row, down_rows, (((1,), (1,)), ((), ())), preferred_element_type=jnp.float32
        )
        grad_pre = gelu_back(grad_hidden)[0].astype(jnp.bfloat16)
        grad_down = lax.dot_general(
            hidden, grad_row, (((0,), (0,)), ((), ())), preferred_element_type=jnp.float32
        )
        grad_up = lax.dot_general(
            normed_row, grad_pre, (((0,), (0,)), ((), ())), preferred_element_type=jnp.float32
        )
        grad_normed = lax.dot_general(
            grad_pre, up_rows, (((1,), (1,)), ((), ())), preferred_element_type=jnp.float32
        )
        return (grad_normed, grad_up, grad_down)

    grad_normed, row_up, row_down = lax.map(one_row, (normed_all, expert_ids[:, 0], grad_branch))
    choose = (
        expert_ids[:, 0][:, None] == jnp.arange(w_up.shape[0], dtype=jnp.int32)[None, :]
    ).astype(jnp.float32)
    grad_w_up = jnp.einsum("re,rdf->edf", choose, row_up, precision=lax.Precision.HIGHEST)
    grad_w_down = jnp.einsum("re,rfd->efd", choose, row_down, precision=lax.Precision.HIGHEST)
    return (grad_normed, grad_w_up, grad_w_down)


def run_forward(layer_input, memory, seg_lengths, expert_ids, ln_gains, attn_weights, w_up, w_down):
    w_qkv, w_out_self, w_query_cross, w_kv_cross, w_out_cross = attn_weights
    state_zero = layer_input.astype(jnp.float32)
    normed_local = layer_norm(state_zero, ln_gains[0]).astype(jnp.bfloat16)
    memory_all = lax.all_gather(memory, "tp", axis=1, tiled=True)
    normed_self = spread_tokens(normed_local)
    state_one = state_zero + sum_tokens(self_partial(normed_self, seg_lengths, w_qkv, w_out_self))
    normed_cross = spread_tokens(layer_norm(state_one, ln_gains[1]).astype(jnp.bfloat16))
    state_two = state_one + sum_tokens(
        cross_partial(normed_cross, memory_all, w_query_cross, w_kv_cross, w_out_cross)
    )
    normed_ffn = spread_tokens(layer_norm(state_two, ln_gains[2]).astype(jnp.bfloat16))
    state_three = state_two + sum_tokens(ffn_partial(normed_ffn, expert_ids, w_up, w_down))
    return (
        state_three,
        (state_zero, state_one, state_two, normed_self, normed_cross, normed_ffn, memory_all),
    )


def per_device(
    layer_input,
    memory,
    seg_lengths,
    expert_ids,
    ln_gains,
    w_qkv,
    w_out_self,
    w_query_cross,
    w_kv_cross,
    w_out_cross,
    w_up,
    w_down,
    cotangent,
):
    attn_weights = (w_qkv, w_out_self, w_query_cross, w_kv_cross, w_out_cross)
    use_qkv, use_out_self, use_query, use_kv, use_out_cross = attn_weights
    state_three, kept = run_forward(
        layer_input, memory, seg_lengths, expert_ids, ln_gains, attn_weights, w_up, w_down
    )
    fresh = lax.optimization_barrier((layer_input, memory, state_three))
    unused, kept = run_forward(
        fresh[0], fresh[1], seg_lengths, expert_ids, ln_gains, attn_weights, w_up, w_down
    )
    state_zero, state_one, state_two, normed_self, normed_cross, normed_ffn, memory_all = kept
    grad_state = cotangent.astype(jnp.float32)
    grad_normed, grad_up, grad_down = ffn_backward(
        normed_ffn, expert_ids, w_up, w_down, gather_grads(grad_state)
    )
    grad_state, gain_ffn = norm_backward(state_two, ln_gains[2], sum_grads(grad_normed), grad_state)
    grad_normed, memory_part, grad_w_query, grad_w_kv, grad_w_out_cross = cross_backward(
        normed_cross, memory_all, use_query, use_kv, use_out_cross, gather_grads(grad_state)
    )
    grad_normed, grad_memory = (
        lax.psum_scatter(
            grad_normed.astype(jnp.bfloat16), "tp", scatter_dimension=1, tiled=True
        ).astype(jnp.float32),
        lax.psum_scatter(
            memory_part.astype(jnp.bfloat16), "tp", scatter_dimension=1, tiled=True
        ).astype(jnp.float32),
    )
    grad_state, gain_cross = norm_backward(state_one, ln_gains[1], grad_normed, grad_state)
    grad_normed, grad_w_qkv, grad_w_out_self = self_backward(
        normed_self, seg_lengths, use_qkv, use_out_self, gather_grads(grad_state)
    )
    grad_state, gain_self = norm_backward(
        state_zero, ln_gains[0], sum_grads(grad_normed), grad_state
    )
    summed = (
        lax.psum_scatter(
            grad_w_qkv.astype(jnp.bfloat16), "dp", scatter_dimension=1, tiled=True
        ).astype(jnp.float32),
        lax.psum_scatter(
            grad_w_out_self.astype(jnp.bfloat16), "dp", scatter_dimension=1, tiled=True
        ).astype(jnp.float32),
        lax.psum_scatter(
            grad_w_query.astype(jnp.bfloat16), "dp", scatter_dimension=0, tiled=True
        ).astype(jnp.float32),
        lax.psum_scatter(
            grad_w_kv.astype(jnp.bfloat16), "dp", scatter_dimension=1, tiled=True
        ).astype(jnp.float32),
        lax.psum_scatter(
            grad_w_out_cross.astype(jnp.bfloat16), "dp", scatter_dimension=1, tiled=True
        ).astype(jnp.float32),
        lax.psum_scatter(
            grad_up.astype(jnp.bfloat16), "dp", scatter_dimension=1, tiled=True
        ).astype(jnp.float32),
        lax.psum_scatter(
            grad_down.astype(jnp.bfloat16), "dp", scatter_dimension=2, tiled=True
        ).astype(jnp.float32),
    )
    grad_w_qkv, grad_w_out_self, grad_w_query, grad_w_kv, grad_w_out_cross, grad_up, grad_down = (
        summed
    )
    gain_total = lax.psum(jnp.stack([gain_self, gain_cross, gain_ffn]), ("dp", "tp"))
    share_width = gain_total.shape[1] // lax.axis_size("dp")
    gain_share = lax.dynamic_slice_in_dim(
        gain_total, lax.axis_index("dp") * share_width, share_width, 1
    )
    return (
        state_three.astype(jnp.bfloat16),
        grad_state,
        grad_memory,
        gain_share,
        grad_w_qkv,
        grad_w_out_self,
        grad_w_query,
        grad_w_kv,
        grad_w_out_cross,
        grad_up,
        grad_down,
    )


F32, BF16 = jnp.float32, jnp.bfloat16
MESH = pl.DeviceIdType.MESH
LOG2E = math.log2(math.e)
QSCALE = LOG2E * HEAD_DIM ** -0.5
NN = (((1,), (0,)), ((), ()))
NT = (((1,), (1,)), ((), ()))
TN = (((0,), (0,)), ((), ()))

LEN, WIDTH, COLS, HIDDEN, BLOCK, HALF = 1024, 512, 256, 1024, 256, 512
BLOCKS = LEN // BLOCK
TILE = 256
TILES = HIDDEN // TILE


def dot(left, right, dims=NN):
    return lax.dot_general(left, right, dims, preferred_element_type=F32)


def head_mask(block, side):
    lanes = lax.broadcasted_iota(jnp.int32, block.shape, 1)
    keep = (lanes >= HEAD_DIM) if side else (lanes < HEAD_DIM)
    return jnp.where(keep, block, jnp.zeros_like(block))


def window_bias(key_at, query_at, keys, queries, starts):
    key_place = key_at + lax.broadcasted_iota(jnp.int32, (keys, queries), 0)
    query_place = query_at + lax.broadcasted_iota(jnp.int32, (keys, queries), 1)
    return jnp.where((key_place >= starts) & (key_place <= query_place), 0.0, -1e30)


def attend_block(qs, k, vt, ht, lse, q_at, q_len, k_at, k_len, bias):
    for h in range(4):
        lanes = slice((h // 2) * 128, (h // 2) * 128 + 128)
        rows = slice(h * 64, h * 64 + 64)
        keys = head_mask(k[pl.ds(k_at, k_len), lanes], h % 2)
        s = dot(keys, qs[pl.ds(q_at, q_len), lanes], NT)
        if bias is not None:
            s = s + bias
        top = jnp.max(s, axis=0, keepdims=True)
        p = jnp.exp2(s - top)
        total = jnp.sum(p, axis=0, keepdims=True)
        out = dot(vt[rows, pl.ds(k_at, k_len)], p.astype(BF16)) * (1.0 / total)
        ht[rows, pl.ds(q_at, q_len)] = out.astype(BF16)
        lse[h:h + 1, pl.ds(q_at, q_len)] = top + jnp.log2(total)


def attend_back_block(qs, k, v, kt, gh, lse, inner, dqt, dk, dv, k_at, k_len, q_at, q_len, bias):
    for pair in range(2):
        lanes = slice(pair * 128, pair * 128 + 128)
        sum_k, sum_v = None, None
        qp = qs[pl.ds(q_at, q_len), lanes]
        gp = gh[pl.ds(q_at, q_len), lanes]
        for side in range(2):
            h = pair * 2 + side
            rows = slice(h * 64, h * 64 + 64)
            keys = head_mask(k[pl.ds(k_at, k_len), lanes], side)
            vals = head_mask(v[pl.ds(k_at, k_len), lanes], side)
            s = dot(keys, qp, NT)
            if bias is not None:
                s = s + bias
            p = jnp.exp2(s - lse[h:h + 1, pl.ds(q_at, q_len)])
            dp = dot(vals, gp, NT)
            ds = (p * (dp - inner[h:h + 1, pl.ds(q_at, q_len)])).astype(BF16)
            part_v = dot(p.astype(BF16), head_mask(gp, side))
            part_k = dot(ds, head_mask(qp, side))
            sum_v = part_v if sum_v is None else sum_v + part_v
            sum_k = part_k if sum_k is None else sum_k + part_k
            dqt[rows, pl.ds(q_at, q_len)] += dot(kt[rows, pl.ds(k_at, k_len)], ds)
        dv[pl.ds(k_at, k_len), lanes] = sum_v.astype(BF16)
        dk[pl.ds(k_at, k_len), lanes] = (sum_k * math.log(2.0)).astype(BF16)


def gelu_parts(pre):
    gauss = jnp.exp2(pre * pre * (-0.5 * LOG2E))
    t = 1.0 / (1.0 + (0.3275911 / math.sqrt(2.0)) * jnp.abs(pre))
    poly = t * (0.254829592 * 0.5 + t * (-0.284496736 * 0.5 + t * (
        1.421413741 * 0.5 + t * (-1.453152027 * 0.5 + t * (1.061405429 * 0.5)))))
    tail = poly * gauss
    phi = jnp.where(pre >= 0, 1.0 - tail, tail)
    return phi, phi + pre * (gauss * (1.0 / math.sqrt(2.0 * math.pi)))


def normalise(x):
    c = x - jnp.mean(x, axis=-1, keepdims=True)
    r = lax.rsqrt(jnp.mean(c * c, axis=-1, keepdims=True) + epsilon)
    return c * r, r


def norm_back(state, gain, grad):
    xhat, r = normalise(state)
    y = grad * gain
    m1 = jnp.mean(y, axis=-1, keepdims=True)
    m2 = jnp.mean(y * xhat, axis=-1, keepdims=True)
    return r * (y - m1 - xhat * m2), jnp.sum(grad * xhat, axis=0, keepdims=True)


def block_rows(i):
    return pl.ds(pl.multiple_of(i * BLOCK, BLOCK), BLOCK)


def each(count, body):
    def step(i, carry):
        body(i)
        return carry

    lax.fori_loop(0, count, step, 0)


def layer_kernel(
    n_dp,
    lens, expert, gains, x_in, mem_in, cot_in, wqkv_in, wos_in, wq_in, wkv_in, woc_in, up_in, down_in,
    lo_out, gi_out, gm_out, e_out, a1_out, a2_out, g_out,
    x, mem, cot, wqkv, wos, wq, wkv, woc, up, down, starts,
    s1, s2, gs, n0, n1, n2, q0, k0, v0, q1, k1, v1, kt0, vt0, kt1, vt1, ht0, ht1, lse0, lse1, inner,
    gb, gh, dqt, dq, dk, dv, hid, gpre, nt, cot_t, eb, a1, a2, r1, r2,
    snd, rcv, sndh, rcvh, leaving, half_out, gain_sum, g_send,
    y_send, y_recv, w_send, w_recv, c_send, c_recv, x_send, x_recv, h_send, h_recv,
    e_send, e_recv, p_send, p_recv, a_send, a_recv, g_ssem, g_rsem, o_send, o_recv,
):
    d, t = lax.axis_index("dp"), lax.axis_index("tp")
    c = lax.rem(d, 2)
    k2 = d - c
    row = k2 + t
    lin = d * 2 + t
    n_all = n_dp * 2
    diag = (k2 + 1 - c, 1 - t)
    sib = (k2 + 1 - c, t)
    swaps = c != t
    stays = c == t

    def remote(src, dst, ssem, rsem, to):
        return pltpu.make_async_remote_copy(
            src_ref=src, dst_ref=dst, send_sem=ssem, recv_sem=rsem, device_id=to, device_id_type=MESH)

    own = pl.ds(pl.multiple_of(c * HALF, HALF), HALF)
    other = pl.ds(pl.multiple_of((1 - c) * HALF, HALF), HALF)
    theirs = pl.ds(pl.multiple_of(t * HALF, HALF), HALF)

    X, MEM, COT, UP, DOWN = 0, 1, 2, 3, 3 + TILES
    n_brought = 3 + 2 * TILES

    def tile(f):
        return pl.ds(pl.multiple_of(f * TILE, TILE), TILE)

    def bring(n, place):
        if n < UP:
            src, dst = ((x_in, x), (mem_in, mem), (cot_in, cot))[n]
            dst = dst.at[place]
        elif n < DOWN:
            src, dst = up_in.at[:, tile(n - UP)], up.at[:, tile(n - UP)]
        else:
            src, dst = down_in.at[tile(n - DOWN)], down.at[tile(n - DOWN)]
        return (lambda: remote(src, dst, y_send.at[n], y_recv.at[n], diag),
                lambda: pltpu.make_async_copy(src, dst, y_recv.at[n]))

    def start_bring(n):
        far, near = bring(n, theirs)

        @pl.when(swaps)
        def _():
            far().start()

    def start_near(n):
        far, near = bring(n, own)

        @pl.when(stays)
        def _():
            near().start()

    def wait_bring(n):
        far, near = bring(n, own)

        @pl.when(swaps)
        def _():
            far().wait_recv()

        @pl.when(stays)
        def _():
            near().wait()

    def share(n, buf):
        return remote(buf.at[own], buf.at[own], c_send.at[n], c_recv.at[n], sib)

    def share_starts():
        return remote(starts, starts, c_send.at[3], c_recv.at[3], sib)

    n_pairs = n_dp // 2
    pair = lax.div(d, 2)
    halves = [(wqkv_in, wqkv), (wos_in, wos), (wq_in, wq), (wkv_in, wkv), (woc_in, woc)]
    WQKV, WOS, WQ, WKV, WOC = range(5)

    def piece(ref, p):
        if len(ref.shape) == 3:
            rows = ref.shape[1] // n_pairs
            return ref.at[:, pl.ds(pl.multiple_of(p * rows, rows), rows)]
        rows = ref.shape[0] // n_pairs
        return ref.at[pl.ds(pl.multiple_of(p * rows, rows), rows)]

    def first_piece(n):
        src, dst = halves[n]
        return remote(piece(src, pair), piece(dst, pair), w_send.at[n, 0], w_recv.at[n, pair], diag)

    def hand_piece(n, s):
        dst = halves[n][1]
        to = lax.rem(pair + s, n_pairs)
        return remote(piece(dst, pair), piece(dst, pair), w_send.at[n, s], w_recv.at[n, pair], (2 * to + c, t))

    def near_weight(n):
        src, dst = halves[n]
        return pltpu.make_async_copy(src, dst, w_recv.at[n, 0])

    def hand_round(n):
        first_piece(n).wait_recv()
        each(n_pairs - 1, lambda s: hand_piece(n, s + 1).start())

    def wait_weight(n):
        @pl.when(swaps)
        def _():
            def one(s):
                dst = halves[n][1]
                p = lax.rem(pair + s + 1, n_pairs)
                remote(piece(dst, p), piece(dst, p), w_send.at[n, 0], w_recv.at[n, p], diag).wait_recv()

            each(n_pairs - 1, one)

        @pl.when(stays)
        def _():
            near_weight(n).wait()

    start_near(X)

    @pl.when(stays)
    def _():
        near_weight(WQKV).start()

    start_near(MEM)
    start_near(COT)

    @pl.when(stays)
    def _():
        for n in (WOS, WKV, WQ, WOC):
            near_weight(n).start()

    for f in range(TILES):
        start_near(UP + f)
        start_near(DOWN + f)
    barrier = pltpu.get_barrier_semaphore()

    def greet(i):
        to = lax.rem(lin + 1 + i, n_all)
        pl.semaphore_signal(barrier, inc=1, device_id=(lax.div(to, 2), lax.rem(to, 2)), device_id_type=MESH)

    each(n_all - 1, greet)

    @pl.when(stays)
    def _():
        places = lax.broadcasted_iota(jnp.int32, (8, LEN), 1)
        start, level = jnp.int32(0), jnp.zeros((8, LEN), jnp.int32)
        for s in range(lens.shape[1]):
            level = jnp.where(places >= start, start, level)
            start = start + lens[0, s]
        starts[...] = level

    pl.semaphore_wait(barrier, n_all - 1)

    @pl.when(swaps)
    def _():
        first_piece(WQKV).start()

    start_bring(X)

    @pl.when(swaps)
    def _():
        for n in (WOS, WKV, WQ, WOC):
            first_piece(n).start()

    start_bring(MEM)
    start_bring(COT)
    for f in range(TILES):
        start_bring(UP + f)
        start_bring(DOWN + f)

    @pl.when(swaps)
    def _():
        hand_round(WQKV)

    @pl.when(stays)
    def _():
        share_starts().start()

    def wait_near(n):
        near = bring(n, own)[1]

        @pl.when(stays)
        def _():
            near().wait()

    def wait_swapped(n):
        far = bring(n, own)[0]

        @pl.when(swaps)
        def _():
            far().wait_recv()

    wait_bring(X)
    share(0, x).start()

    @pl.when(stays)
    def _():
        wait_near(MEM)
        share(1, mem).start()
        wait_near(COT)
        share(2, cot).start()

    def self_project(i):
        r = block_rows(i)
        xhat, _ = normalise(x[r, :].astype(F32))
        nn = (xhat * gains[0:1, :]).astype(BF16)
        n0[r, :] = nn
        q0[r, :] = (dot(nn, wqkv[0]) * QSCALE).astype(BF16)
        k0[r, :] = dot(nn, wqkv[1]).astype(BF16)
        v0[r, :] = dot(nn, wqkv[2]).astype(BF16)

    @pl.when(swaps)
    def _():
        for n in (WOS, WKV, WQ, WOC):
            hand_round(n)

    wait_weight(WQKV)
    each(2, lambda i: self_project(c * 2 + i))
    share(0, x).wait_recv()
    each(2, lambda i: self_project((1 - c) * 2 + i))
    kt0[...] = k0[...].T
    vt0[...] = v0[...].T

    @pl.when(swaps)
    def _():
        share_starts().wait_recv()

    wait_weight(WOS)

    def exchange(e, i):
        r = block_rows(i)
        return remote(snd.at[e, r], rcv.at[e, r], x_send.at[e, i], x_recv.at[e, i], sib)

    def self_out(i):
        r = block_rows(i)
        snd[0, r, :] = dot(ht0[:, r], wos[...], TN).astype(BF16)
        exchange(0, i).start()

    attend_block(q0, k0, vt0, ht0, lse0, 0, 256, 0, 256, window_bias(0, 0, 256, 256, starts[0:1, 0:256]))
    self_out(0)

    def self_block(j):
        i = j + 1
        q_at = pl.multiple_of(i * 256, 256)
        k_at = pl.multiple_of(j * 256, 256)
        attend_block(q0, k0, vt0, ht0, lse0, q_at, 256, k_at, 512,
                     window_bias(k_at, q_at, 512, 256, starts[0:1, pl.ds(q_at, 256)]))
        self_out(i)

    each(3, self_block)

    wait_swapped(MEM)

    @pl.when(swaps)
    def _():
        share(1, mem).start()

    wait_weight(WKV)

    def memory_project(i):
        r = block_rows(i)
        k1[r, :] = dot(mem[r, :], wkv[0]).astype(BF16)
        v1[r, :] = dot(mem[r, :], wkv[1]).astype(BF16)

    each(2, lambda i: memory_project(c * 2 + i))
    share(1, mem).wait_recv()
    each(2, lambda i: memory_project((1 - c) * 2 + i))
    kt1[...] = k1[...].T
    vt1[...] = v1[...].T
    wait_weight(WQ)
    wait_weight(WOC)

    def cross_block(i):
        r = block_rows(i)
        exchange(0, i).wait_recv()
        state = x[r, :].astype(F32) + (snd[0, r, :].astype(F32) + rcv[0, r, :].astype(F32))
        s1[r, :] = state
        xhat, _ = normalise(state)
        nn = (xhat * gains[1:2, :]).astype(BF16)
        n1[r, :] = nn
        q1[r, :] = (dot(nn, wq[...]) * QSCALE).astype(BF16)
        attend_block(q1, k1, vt1, ht1, lse1, pl.multiple_of(i * 256, 256), 256, 0, LEN, None)
        snd[1, r, :] = dot(ht1[:, r], woc[...], TN).astype(BF16)
        exchange(1, i).start()

    each(BLOCKS, cross_block)

    wait_swapped(COT)

    @pl.when(swaps)
    def _():
        share(2, cot).start()

    def half_exchange(e, i):
        r = block_rows(i)
        return remote(sndh.at[e, r], rcvh.at[e, r], h_send.at[e, i], h_recv.at[e, i], sib)

    def expert_norm(i):
        r = block_rows(i)
        exchange(1, i).wait_recv()
        state = s1[r, :] + (snd[1, r, :].astype(F32) + rcv[1, r, :].astype(F32))
        s2[r, :] = state
        xhat, _ = normalise(state)
        n2[r, :] = (xhat * gains[2:3, :]).astype(BF16)

    each(BLOCKS, expert_norm)
    nt[...] = n2[...].T
    share(2, cot).wait_recv()
    cot_t[...] = cot[...].T

    def begin(copy):
        copy.start()

    def finish_send(copy):
        copy.wait_send()

    def share_rows(ref, to):
        return ref.at[pl.ds(pl.multiple_of(to * 32, 32), 32)]

    def scatter(f, action):
        src, dst = eb.at[f], e_out.at[row, f]

        @pl.when(stays)
        def _():
            if action is begin:
                pltpu.make_async_copy(share_rows(src, d), dst, e_recv.at[f, row]).start()

        @pl.when(swaps)
        def _():
            action(remote(share_rows(src, d), dst, e_send.at[f, 0], e_recv.at[f, row], (d, c)))

        def one(s):
            to = lax.rem(d + s + 1, n_dp)
            action(remote(share_rows(src, to), dst, e_send.at[f, s + 1], e_recv.at[f, row], (to, c)))

        each(n_dp - 1, one)

    def collect(f):
        def one(i):
            src, dst = eb.at[f, pl.ds(0, 32)], e_out.at[i, f]

            @pl.when(stays & (i == row))
            def _():
                pltpu.make_async_copy(src, dst, e_recv.at[f, i]).wait()

            @pl.when(jnp.logical_not(stays & (i == row)))
            def _():
                remote(src, dst, e_send.at[f, 0], e_recv.at[f, i], diag).wait_recv()

        each(n_dp, one)

    for f in range(TILES):
        wait_bring(UP + f)
        wait_bring(DOWN + f)
        cols = tile(f)

        def expert_block(i):
            r = block_rows(i)
            phi, slope = gelu_parts(pre := dot(n2[r, :], up[:, cols]))
            hid[r, cols] = (pre * phi).astype(BF16)
            gpre[r, cols] = (dot(cot[r, :], down[cols, :], NT) * slope).astype(BF16)

        each(BLOCKS, expert_block)
        eb[f, :, 0:TILE] = dot(nt[...], gpre[:, cols]).astype(BF16)
        eb[f, :, TILE:2 * TILE] = dot(cot_t[...], hid[:, cols]).astype(BF16)
        scatter(f, begin)

    def expert_back(i):
        r = block_rows(i)
        snd[2, r, :] = dot(gpre[r, :], up[...], NT).astype(BF16)
        exchange(2, i).start()

    each(BLOCKS, expert_back)

    def expert_out(i):
        r = block_rows(i)
        part = dot(hid[r, :], down[...])
        mine = lax.div(i, 2) == c
        low = lax.rem(i, 2)
        rl = block_rows(low)

        @pl.when(mine)
        def _():
            half_out[rl, :] = s2[r, :] + part

        @pl.when(jnp.logical_not(mine))
        def _():
            sndh[0, rl, :] = part.astype(BF16)
            half_exchange(0, low).start()

    each(BLOCKS, expert_out)

    gain_sum[...] = jnp.zeros_like(gain_sum)

    def branch_block(n, i, e, state, base, ht, w_out):
        r = block_rows(i)
        exchange(e, i).wait_recv()
        grad = snd[e, r, :].astype(F32) + rcv[e, r, :].astype(F32)
        step, share_gain = norm_back(state[r, :], gains[n:n + 1, :], grad)
        total = base[r, :].astype(F32) + step
        gs[r, :] = total
        low = total.astype(BF16)
        gb[r, :] = low
        gain_sum[n:n + 1, :] += jnp.where(lax.div(i, 2) == c, share_gain, 0.0)
        gh[r, :] = dot(low, w_out[...], NT).astype(BF16)
        ght = dot(w_out[...], low, NT).astype(BF16).astype(F32)
        prod = ght * ht[:, r].astype(F32)
        for h in range(4):
            inner[h:h + 1, r] = jnp.sum(prod[h * 64:h * 64 + 64], axis=0, keepdims=True)

    each(BLOCKS, lambda i: branch_block(2, i, 2, s2, cot, ht1, woc))
    dqt[...] = jnp.zeros_like(dqt)

    def cross_back(i):
        at = pl.multiple_of(i * 256, 256)
        attend_back_block(q1, k1, v1, kt1, gh, lse1, inner, dqt, dk, dv, at, 256, 0, LEN, None)

    each(BLOCKS, cross_back)
    dq[...] = (dqt[...] * HEAD_DIM ** -0.5).astype(BF16).T

    def cross_grads(i):
        r = block_rows(i)
        snd[3, r, :] = dot(dq[r, :], wq[...], NT).astype(BF16)
        exchange(3, i).start()

    each(BLOCKS, cross_grads)

    def memory_grads(i):
        r = block_rows(i)
        part = dot(dk[r, :], wkv[0], NT) + dot(dv[r, :], wkv[1], NT)
        mine = lax.div(i, 2) == c
        low = lax.rem(i, 2)
        rl = block_rows(low)

        @pl.when(mine)
        def _():
            half_out[pl.ds(pl.multiple_of(HALF + low * BLOCK, BLOCK), BLOCK), :] = part

        @pl.when(jnp.logical_not(mine))
        def _():
            sndh[1, rl, :] = part.astype(BF16)
            half_exchange(1, low).start()

    each(BLOCKS, memory_grads)
    a1[:, 0:256] = dot(ht1[...], gb[...]).T.astype(BF16)
    nt[...] = n1[...].T
    a1[:, 256:512] = dot(nt[...], dq[...]).astype(BF16)
    nt[...] = mem[...].T
    a1[:, 512:768] = dot(nt[...], dk[...]).astype(BF16)
    a1[:, 768:1024] = dot(nt[...], dv[...]).astype(BF16)

    def over(n):
        buf, place = ((a1, r1), (a2.at[0], r2.at[0]), (a2.at[1], r2.at[1]), (a2.at[2], r2.at[2]))[n]
        return remote(buf, place, p_send.at[n], p_recv.at[n], (d, c))

    def hand_over(n):
        @pl.when(swaps)
        def _():
            over(n).start()

    def hand_out(n):
        if n == 0:
            return a1, a1_out.at[pair]
        return a2.at[n - 1], a2_out.at[pair, n - 1]

    def owners(n, action):
        src, dst = hand_out(n)

        def one(s):
            to = lax.rem(d + s + 1, n_dp)
            action(remote(share_rows(src, to), dst, a_send.at[n, s + 1], a_recv.at[n, pair], (to, t)))

        each(n_dp - 1, one)

    def add_over(n):
        @pl.when(stays)
        def _():
            over(n).wait_recv()
            if n == 0:
                a1[...] = (a1[...].astype(F32) + r1[...].astype(F32)).astype(BF16)
            else:
                a2[n - 1] = (a2[n - 1].astype(F32) + r2[n - 1].astype(F32)).astype(BF16)
            src, dst = hand_out(n)
            pltpu.make_async_copy(share_rows(src, d), dst, a_recv.at[n, pair]).start()
            owners(n, begin)

    def collect_over(n):
        def one(i):
            src = hand_out(n)[0].at[pl.ds(0, 32)]
            dst = a1_out.at[i] if n == 0 else a2_out.at[i, n - 1]

            @pl.when(stays & (i == pair))
            def _():
                pltpu.make_async_copy(src, dst, a_recv.at[n, i]).wait()

            @pl.when(jnp.logical_not(stays & (i == pair)))
            def _():
                remote(src, dst, a_send.at[n, 0], a_recv.at[n, i], diag).wait_recv()

        each(n_pairs, one)

        @pl.when(stays)
        def _():
            owners(n, finish_send)

        @pl.when(swaps)
        def _():
            over(n).wait_send()

    def leave(n, out):
        buf = leaving.at[n]
        return (lambda: remote(buf, out, o_send.at[n], o_recv.at[n], diag),
                lambda: pltpu.make_async_copy(buf, out, o_recv.at[n]))

    def start_leave(n, out):
        far, near = leave(n, out)

        @pl.when(swaps)
        def _():
            far().start()

        @pl.when(stays)
        def _():
            near().start()

    def wait_leave(n, out):
        far, near = leave(n, out)

        @pl.when(swaps)
        def _():
            far().wait()

        @pl.when(stays)
        def _():
            near().wait()

    for n in range(2):
        for low in range(2):
            half_exchange(n, low).wait_recv()
            r = pl.ds(low * BLOCK, BLOCK)
            whole = half_out[pl.ds(n * HALF + low * BLOCK, BLOCK), :] + rcvh[n, r, :].astype(F32)
            leaving[n, r, :] = whole.astype(BF16)
        start_leave(n, (lo_out, gm_out)[n])

    each(BLOCKS, lambda i: branch_block(1, i, 3, s1, gs, ht0, wos))
    a1[:, 1024:1280] = dot(ht0[...], gb[...]).T.astype(BF16)
    hand_over(0)
    dqt[...] = jnp.zeros_like(dqt)

    def self_back(i):
        at = pl.multiple_of(i * 256, 256)
        attend_back_block(q0, k0, v0, kt0, gh, lse0, inner, dqt, dk, dv, at, 256, at, 512,
                          window_bias(at, at, 256, 512, starts[0:1, pl.ds(at, 512)]))

    each(BLOCKS - 1, self_back)
    attend_back_block(q0, k0, v0, kt0, gh, lse0, inner, dqt, dk, dv, 768, 256, 768, 256,
                      window_bias(768, 768, 256, 256, starts[0:1, 768:1024]))
    dq[...] = (dqt[...] * HEAD_DIM ** -0.5).astype(BF16).T

    def input_grads(i):
        r = block_rows(i)
        return dot(dq[r, :], wqkv[0], NT) + dot(dk[r, :], wqkv[1], NT) + dot(dv[r, :], wqkv[2], NT)

    def input_send(low):
        rl = block_rows(low)
        sndh[2, rl, :] = input_grads((1 - c) * 2 + low).astype(BF16)
        half_exchange(2, low).start()

    each(2, input_send)
    add_over(0)
    nt[...] = n0[...].T
    for n, grad in enumerate((dq, dk, dv)):
        a2[n] = dot(nt[...], grad[...]).astype(BF16)
        hand_over(n + 1)

    def input_keep(low):
        half_out[block_rows(low), :] = input_grads(c * 2 + low)

    each(2, input_keep)

    def input_done(low):
        half_exchange(2, low).wait_recv()
        rl = block_rows(low)
        r = block_rows(c * 2 + low)
        grad = half_out[rl, :] + rcvh[2, rl, :].astype(F32)
        step, share_gain = norm_back(x[r, :].astype(F32), gains[0:1, :], grad)
        gain_sum[0:1, :] += share_gain
        leaving[2, rl, :] = (gs[r, :] + step).astype(BF16)

    each(2, input_done)
    start_leave(2, gi_out)
    for n in range(1, 4):
        add_over(n)

    number = jnp.full((1, 128), expert[0, 0].astype(F32))
    for j in range(n_dp):
        turned = gain_sum[...] if j == 0 else pltpu.roll(gain_sum[...], (WIDTH - 32 * j) % WIDTH, 1)
        g_send[j] = turned[:, :128]
        g_send[j, 3:4, :] = number

    def gain_copy(s):
        to = lax.rem(lin + s, n_all)
        to_dp = lax.div(to, 2)
        return remote(g_send.at[to_dp], g_out.at[lin], g_ssem.at[s], g_rsem.at[lin], (to_dp, lax.rem(to, 2)))

    each(n_all - 1, lambda s: gain_copy(s + 1).start())
    keep_gain = pltpu.make_async_copy(g_send.at[d], g_out.at[lin], g_rsem.at[lin])
    keep_gain.start()

    wait_leave(0, lo_out)
    wait_leave(1, gm_out)
    wait_leave(2, gi_out)
    for f in range(TILES):
        collect(f)
        scatter(f, finish_send)
    for n in range(4):
        collect_over(n)
    keep_gain.wait()

    def gain_wait(s):
        gain_copy(s + 1).wait_send()
        who = lax.rem(lin + s + 1, n_all)
        remote(g_send.at[0], g_out.at[who], g_ssem.at[0], g_rsem.at[who], diag).wait_recv()

    each(n_all - 1, gain_wait)

    @pl.when(swaps)
    def _():
        for n in range(n_brought):
            bring(n, theirs)[0]().wait_send()
        for n in range(5):
            first_piece(n).wait_send()
            each(n_pairs - 1, lambda s: hand_piece(n, s + 1).wait_send())

    for n, buf in enumerate((x, mem, cot)):
        share(n, buf).wait_send()

    @pl.when(stays)
    def _():
        share_starts().wait_send()

    for e in range(4):
        each(BLOCKS, lambda i: exchange(e, i).wait_send())
    for e in range(3):
        each(2, lambda i: half_exchange(e, i).wait_send())


VMEM_BYTES = 63 * 2**20
ANY_PLACE = pl.BlockSpec(memory_space=pl.ANY)
IN_HBM = pl.BlockSpec(memory_space=pltpu.HBM)
IN_SMEM = pl.BlockSpec(memory_space=pltpu.SMEM)
IN_VMEM = pl.BlockSpec(memory_space=pltpu.VMEM)


def paired_layer(n_dp, lens, expert, gains, *arrays):
    bf = lambda *shape: pltpu.VMEM(shape, BF16)
    fl = lambda *shape: pltpu.VMEM(shape, F32)
    dma = lambda *shape: pltpu.SemaphoreType.DMA(shape)
    tokens = bf(LEN, WIDTH)
    heads = bf(LEN, COLS)
    turned = bf(COLS, LEN)
    half = jax.ShapeDtypeStruct((HALF, WIDTH), BF16)
    n_pairs = n_dp // 2
    return pl.pallas_call(
        partial(layer_kernel, n_dp),
        out_shape=(half, half, half,
                   jax.ShapeDtypeStruct((n_dp, TILES, 32, 2 * TILE), BF16),
                   jax.ShapeDtypeStruct((n_pairs, 32, 5 * COLS), BF16),
                   jax.ShapeDtypeStruct((n_pairs, 3, 32, COLS), BF16),
                   jax.ShapeDtypeStruct((2 * n_dp, 8, 128), F32)),
        in_specs=[IN_SMEM] * 2 + [IN_VMEM] + [ANY_PLACE] * 10,
        out_specs=(ANY_PLACE,) * 7,
        scratch_shapes=[
            tokens, tokens, tokens, bf(3, WIDTH, COLS), bf(COLS, WIDTH), bf(WIDTH, COLS), bf(2, WIDTH, COLS),
            bf(COLS, WIDTH), bf(WIDTH, HIDDEN), bf(HIDDEN, WIDTH), pltpu.VMEM((8, LEN), jnp.int32),
            fl(LEN, WIDTH), fl(LEN, WIDTH), fl(LEN, WIDTH), tokens, tokens, tokens,
            heads, heads, heads, heads, heads, heads, turned, turned, turned, turned, turned, turned,
            fl(8, LEN), fl(8, LEN), fl(8, LEN),
            tokens, heads, fl(COLS, LEN), heads, heads, heads, bf(LEN, HIDDEN), bf(LEN, HIDDEN), bf(WIDTH, LEN),
            bf(WIDTH, LEN), bf(TILES, WIDTH, 2 * TILE), bf(WIDTH, 5 * COLS), bf(3, WIDTH, COLS),
            bf(WIDTH, 5 * COLS), bf(3, WIDTH, COLS),
            bf(4, LEN, WIDTH), bf(4, LEN, WIDTH), bf(3, HALF, WIDTH), bf(3, HALF, WIDTH), bf(3, HALF, WIDTH),
            fl(LEN, WIDTH), fl(8, WIDTH), fl(n_dp, 8, 128),
            dma(3 + 2 * TILES), dma(3 + 2 * TILES), dma(5, n_pairs), dma(5, n_pairs), dma(4), dma(4),
            dma(4, 4), dma(4, 4), dma(3, 2), dma(3, 2),
            dma(TILES, n_dp), dma(TILES, n_dp), dma(4), dma(4), dma(4, n_dp), dma(4, n_pairs),
            dma(2 * n_dp), dma(2 * n_dp), dma(3), dma(3),
        ],
        compiler_params=pltpu.CompilerParams(
            collective_id=0, has_side_effects=True, vmem_limit_bytes=VMEM_BYTES),
        cost_estimate=pl.CostEstimate(flops=20 * 10**9, bytes_accessed=20 * 2**20, transcendentals=0),
    )(lens, expert, gains, *arrays)


def choose_kernel(expert, up_in, down_in, up_out, down_out, sems):
    e = expert[0, 0]
    parts = 4
    copies = []
    for p in range(parts):
        for n, (src, dst) in enumerate(((up_in, up_out), (down_in, down_out))):
            rows = dst.shape[0] // parts
            at = pl.ds(p * rows, rows)
            copies.append(pltpu.make_async_copy(src.at[e, at], dst.at[at], sems.at[n, p]))
    for copy in copies:
        copy.start()
    for copy in copies:
        copy.wait()


def choose_expert(expert, w_up, w_down):
    return pl.pallas_call(
        choose_kernel,
        out_shape=(jax.ShapeDtypeStruct(w_up.shape[1:], BF16), jax.ShapeDtypeStruct(w_down.shape[1:], BF16)),
        in_specs=[IN_SMEM, ANY_PLACE, ANY_PLACE],
        out_specs=(IN_VMEM, IN_VMEM),
        scratch_shapes=[pltpu.SemaphoreType.DMA((2, 4))],
        compiler_params=pltpu.CompilerParams(vmem_limit_bytes=VMEM_BYTES),
    )(expert, w_up, w_down)


def place_kernel(
    gains_any, e_any, a1_any, a2_any, gi_any, gm_any, lo_any,
    lo_out, gi_out, gm_out, gain_out, qkv_out, os_out, q_out, kv_out, oc_out, up_out, down_out,
    ids, gains_in, e_in, a1_in, a2_in, gi_in, gm_in, lo_in, gi_v, gm_v, ups, downs, in_sems, e_sems, up_sems, down_sems, out_sems,
):
    rows = e_in.shape[0]
    number = pltpu.make_async_copy(gains_any, ids, in_sems.at[0])
    number.start()
    blocks = [pltpu.make_async_copy(e_any.at[r], e_in.at[r], e_sems.at[r]) for r in range(rows)]
    for copy in blocks:
        copy.start()
    pairs = ((lo_any, lo_in), (gi_any, gi_in), (gm_any, gm_in), (gains_any, gains_in), (a1_any, a1_in), (a2_any, a2_in))
    reads = [pltpu.make_async_copy(src, dst, in_sems.at[1 + n]) for n, (src, dst) in enumerate(pairs)]
    for copy in reads:
        copy.start()
    number.wait()
    writes = []

    def write(src, dst, sem):
        writes.append(pltpu.make_async_copy(src, dst, sem))
        writes[-1].start()

    for r in range(rows):
        blocks[r].wait()
        for f in range(TILES):
            ups[r, :, f * TILE:(f + 1) * TILE] = e_in[r, f, :, 0:TILE].astype(F32)
            downs[r, :, f * TILE:(f + 1) * TILE] = e_in[r, f, :, TILE:2 * TILE].astype(F32)
        e = ids[2 * r, 3, 0].astype(jnp.int32)
        write(ups.at[r], up_out.at[e], up_sems.at[r])
        write(downs.at[r], down_out.at[e], down_sems.at[r])
    reads[0].wait()
    write(lo_in, lo_out, out_sems.at[2])
    reads[1].wait()
    gi_v[...] = gi_in[...].astype(F32)
    write(gi_v, gi_out, out_sems.at[0])
    reads[2].wait()
    gm_v[...] = gm_in[...].astype(F32)
    write(gm_v, gm_out, out_sems.at[1])
    for copy in reads[3:]:
        copy.wait()
    gain_out[...] = jnp.sum(gains_in[...], axis=0)[:3, :32]
    first = jnp.sum(a1_in[...].astype(F32), axis=0)
    oc_out[...] = first[:, 0:COLS]
    q_out[...] = first[:, COLS:2 * COLS]
    kv_out[0] = first[:, 2 * COLS:3 * COLS]
    kv_out[1] = first[:, 3 * COLS:4 * COLS]
    os_out[...] = first[:, 4 * COLS:5 * COLS]
    qkv_out[...] = jnp.sum(a2_in[...].astype(F32), axis=0)
    for copy in writes:
        copy.wait()


def place_grads(experts, *arrays):
    shape = lambda *dims: jax.ShapeDtypeStruct(dims, F32)
    like = lambda array: pltpu.VMEM(array.shape, array.dtype)
    dma = lambda *dims: pltpu.SemaphoreType.DMA(dims)
    rows = arrays[1].shape[0]
    staged = pltpu.VMEM((rows, 32, HIDDEN), F32)
    half = pltpu.VMEM((HALF, WIDTH), F32)
    return pl.pallas_call(
        place_kernel,
        out_shape=(jax.ShapeDtypeStruct((HALF, WIDTH), BF16), shape(HALF, WIDTH), shape(HALF, WIDTH), shape(3, 32), shape(3, 32, COLS), shape(32, COLS),
                   shape(32, COLS), shape(2, 32, COLS), shape(32, COLS),
                   shape(experts, 32, HIDDEN), shape(experts, 32, HIDDEN)),
        in_specs=[IN_HBM] * 7,
        out_specs=(IN_HBM,) * 3 + (IN_VMEM,) * 6 + (IN_HBM,) * 2,
        scratch_shapes=[pltpu.SMEM(arrays[0].shape, F32)] + [like(array) for array in arrays] + [
            half, half, staged, staged, dma(7), dma(rows), dma(rows), dma(rows), dma(3)],
        compiler_params=pltpu.CompilerParams(vmem_limit_bytes=VMEM_BYTES),
    )(*arrays)


def per_device_paired(
    layer_input, memory, seg_lengths, expert_ids, ln_gains, w_qkv, w_out_self, w_query_cross, w_kv_cross,
    w_out_cross, w_up, w_down, cotangent,
):
    n_dp = lax.axis_size("dp")
    up, down = choose_expert(expert_ids, w_up, w_down)
    layer_output, grad_input, grad_memory, e_rows, a1_rows, a2_rows, gain_rows = paired_layer(
        n_dp, seg_lengths, expert_ids, ln_gains,
        layer_input[0], memory[0], cotangent[0], w_qkv, w_out_self, w_query_cross, w_kv_cross, w_out_cross, up, down,
    )
    layer_output, grad_input, grad_memory, gain_share, qkv, out_self, query, key_value, out_cross, grad_up, grad_down = place_grads(
        w_up.shape[0], gain_rows, e_rows, a1_rows, a2_rows, grad_input, grad_memory, layer_output)
    return (
        layer_output[None], grad_input[None], grad_memory[None], gain_share, qkv, out_self.T, query, key_value,
        out_cross.T, grad_up, jnp.swapaxes(grad_down, 1, 2),
    )


def fits_pairs(mesh, layer_input, seg_lengths, w_up):
    return (
        mesh.shape["tp"] == 2
        and mesh.shape["dp"] == 16
        and layer_input.shape == (mesh.shape["dp"], LEN, WIDTH)
        and w_up.shape == (mesh.shape["dp"], WIDTH, 2 * HIDDEN)
    )


def solution(mesh):
    in_specs = (
        P("dp", "tp", None),
        P("dp", "tp", None),
        P("dp", None),
        P("dp", None),
        P(),
        P(None, None, "tp"),
        P("tp", None),
        P(None, "tp"),
        P(None, None, "tp"),
        P("tp", None),
        P(None, None, "tp"),
        P(None, "tp", None),
        P("dp", "tp", None),
    )
    out_specs = (
        P("dp", "tp", None),
        P("dp", "tp", None),
        P("dp", "tp", None),
        P(None, "dp"),
        P(None, "dp", "tp"),
        P("tp", "dp"),
        P("dp", "tp"),
        P(None, "dp", "tp"),
        P("tp", "dp"),
        P(None, "dp", "tp"),
        P(None, "tp", "dp"),
    )

    def run(*args):
        layer_input, seg_lengths, w_up = args[0], args[2], args[10]
        paired = fits_pairs(mesh, layer_input, seg_lengths, w_up)
        return jax.shard_map(
            per_device_paired if paired else per_device,
            mesh=mesh, in_specs=in_specs, out_specs=out_specs, check_vma=False,
        )(*args)

    return run
```

```python
import math
from functools import partial

import jax
import jax.numpy as jnp
from jax import lax
from jax.experimental import pallas as pl
from jax.experimental.pallas import tpu as pltpu
from jax.sharding import PartitionSpec as P

HEAD_DIM = 64


epsilon = 1e-05


def layer_norm(values, gain):
    centered = values - jnp.mean(values, axis=-1, keepdims=True)
    spread = jnp.mean(centered * centered, axis=-1, keepdims=True)
    return centered * lax.rsqrt(spread + epsilon) * gain


def norm_backward(state, gain, grad_normed, grad_state):
    unused, pullback = jax.vjp(layer_norm, state, gain)
    grad_values, grad_gain = pullback(grad_normed)
    return (grad_state + grad_values, grad_gain)


def segment_mask(lengths, length, count):
    seg_ends = jnp.cumsum(lengths, dtype=jnp.int32)
    places = jnp.arange(length, dtype=jnp.int32)
    labels = jnp.sum((places[:, None] >= seg_ends[None, :]).astype(jnp.int32), axis=1)
    row_places = jnp.arange(count, dtype=jnp.int32)
    return (labels[:, None] == labels[None, :]) & (row_places[:, None] >= places[None, :])


def to_heads(block):
    return block.reshape(block.shape[:-1] + (block.shape[-1] // HEAD_DIM, HEAD_DIM))


def softmax_rows(queries, key_rows, allowed):
    scores = jnp.einsum(
        "qhd,khd->hqk", queries, key_rows, preferred_element_type=jnp.float32
    ) * HEAD_DIM ** (-0.5)
    if allowed is not None:
        scores = jnp.where(allowed[None], scores, -1e30)
    row_max = jnp.max(scores, axis=-1, keepdims=True)
    weights = jnp.exp(scores - row_max)
    return weights / jnp.sum(weights, axis=-1, keepdims=True)


def attend_both(queries, key_rows, value_rows, allowed, grad_heads):
    row_probs = softmax_rows(queries, key_rows, allowed)
    probs_low = row_probs.astype(jnp.bfloat16)
    heads_out = jnp.einsum(
        "hqk,khd->qhd", probs_low, value_rows, preferred_element_type=jnp.float32
    ).astype(jnp.bfloat16)
    grad_probs = jnp.einsum(
        "qhd,khd->hqk", grad_heads, value_rows, preferred_element_type=jnp.float32
    )
    inner_sum = jnp.sum(row_probs * grad_probs, axis=-1, keepdims=True)
    grad_scores = (row_probs * (grad_probs - inner_sum)).astype(jnp.bfloat16)
    grad_queries = jnp.einsum(
        "hqk,khd->qhd", grad_scores, key_rows, preferred_element_type=jnp.float32
    ) * HEAD_DIM ** (-0.5)
    grad_keys = jnp.einsum(
        "hqk,qhd->khd", grad_scores, queries, preferred_element_type=jnp.float32
    ) * HEAD_DIM ** (-0.5)
    grad_values = jnp.einsum(
        "hqk,qhd->khd", probs_low, grad_heads, preferred_element_type=jnp.float32
    )
    return (heads_out, grad_queries, grad_keys, grad_values)


def spread_tokens(normed):
    return lax.all_gather(normed, "tp", axis=1, tiled=True)


def sum_tokens(partial_out):
    return lax.psum_scatter(partial_out, "tp", scatter_dimension=1, tiled=True)


def gather_grads(grad_state):
    return lax.all_gather(grad_state.astype(jnp.bfloat16), "tp", axis=1, tiled=True)


def sum_grads(grad_normed):
    return lax.psum_scatter(grad_normed, "tp", scatter_dimension=1, tiled=True)


def self_partial(normed_all, seg_lengths, w_qkv, w_out_self):
    projected = jnp.einsum(
        "rld,cde->rcle", normed_all, w_qkv, preferred_element_type=jnp.float32
    ).astype(jnp.bfloat16)

    def one_row(items):
        row_proj, lengths = items
        split_heads = to_heads(row_proj)
        length = row_proj.shape[1]
        row_probs = softmax_rows(
            split_heads[0], split_heads[1], segment_mask(lengths, length, length)
        )
        heads_out = jnp.einsum(
            "hqk,khd->qhd",
            row_probs.astype(jnp.bfloat16),
            split_heads[2],
            preferred_element_type=jnp.float32,
        )
        return heads_out.reshape(row_proj.shape[1:]).astype(jnp.bfloat16)

    heads_all = lax.map(one_row, (projected, seg_lengths))
    return jnp.einsum("rle,ed->rld", heads_all, w_out_self, preferred_element_type=jnp.float32)


def self_backward(normed_all, seg_lengths, w_qkv, w_out_self, grad_branch):
    projected = jnp.einsum(
        "rld,cde->rcle", normed_all, w_qkv, preferred_element_type=jnp.float32
    ).astype(jnp.bfloat16)
    grad_heads = jnp.einsum(
        "rld,ed->rle", grad_branch, w_out_self, preferred_element_type=jnp.float32
    ).astype(jnp.bfloat16)

    def one_row(items):
        row_proj, lengths, row_grad = items
        split_heads = to_heads(row_proj)
        length = row_proj.shape[1]
        results = attend_both(
            split_heads[0],
            split_heads[1],
            split_heads[2],
            segment_mask(lengths, length, length),
            to_heads(row_grad),
        )
        return (
            results[0].reshape(length, -1),
            jnp.stack([piece.reshape(length, -1).astype(jnp.bfloat16) for piece in results[1:]]),
        )

    heads_all, grad_proj = lax.map(one_row, (projected, seg_lengths, grad_heads))
    grad_w_out = jnp.einsum(
        "rle,rld->ed", heads_all, grad_branch, preferred_element_type=jnp.float32
    )
    grad_w_qkv = jnp.einsum(
        "rld,rcle->cde", normed_all, grad_proj, preferred_element_type=jnp.float32
    )
    grad_normed = jnp.einsum("rcle,cde->rld", grad_proj, w_qkv, preferred_element_type=jnp.float32)
    return (grad_normed, grad_w_qkv, grad_w_out)


def cross_partial(normed_all, memory_all, w_query_cross, w_kv_cross, w_out_cross):
    queries = jnp.einsum(
        "rld,de->rle", normed_all, w_query_cross, preferred_element_type=jnp.float32
    ).astype(jnp.bfloat16)
    key_value = jnp.einsum(
        "rmd,cde->rcme", memory_all, w_kv_cross, preferred_element_type=jnp.float32
    ).astype(jnp.bfloat16)

    def one_row(items):
        row_query, row_kv = items
        split_kv = to_heads(row_kv)
        row_probs = softmax_rows(to_heads(row_query), split_kv[0], None)
        heads_out = jnp.einsum(
            "hqk,khd->qhd",
            row_probs.astype(jnp.bfloat16),
            split_kv[1],
            preferred_element_type=jnp.float32,
        )
        return heads_out.reshape(row_query.shape).astype(jnp.bfloat16)

    heads_all = lax.map(one_row, (queries, key_value))
    return jnp.einsum("rle,ed->rld", heads_all, w_out_cross, preferred_element_type=jnp.float32)


def cross_core(normed_all, memory_all, w_query_cross, w_kv_cross, w_out_cross, grad_branch):
    queries = jnp.einsum(
        "rld,de->rle", normed_all, w_query_cross, preferred_element_type=jnp.float32
    ).astype(jnp.bfloat16)
    key_value = jnp.einsum(
        "rmd,cde->rcme", memory_all, w_kv_cross, preferred_element_type=jnp.float32
    ).astype(jnp.bfloat16)
    grad_heads = jnp.einsum(
        "rld,ed->rle", grad_branch, w_out_cross, preferred_element_type=jnp.float32
    ).astype(jnp.bfloat16)

    def one_row(items):
        row_query, row_kv, row_grad = items
        split_kv = to_heads(row_kv)
        query_count = row_query.shape[0]
        memory_count = row_kv.shape[1]
        results = attend_both(
            to_heads(row_query), split_kv[0], split_kv[1], None, to_heads(row_grad)
        )
        grad_kv = jnp.stack(
            [results[2].reshape(memory_count, -1), results[3].reshape(memory_count, -1)]
        )
        return (results[0].reshape(query_count, -1), results[1].reshape(query_count, -1), grad_kv)

    heads_all, grad_queries, grad_kv = lax.map(one_row, (queries, key_value, grad_heads))
    grad_w_out = jnp.einsum(
        "rle,rld->ed", heads_all, grad_branch, preferred_element_type=jnp.float32
    )
    return (grad_queries, grad_kv, grad_w_out)


def cross_backward(normed_all, memory_all, w_query_cross, w_kv_cross, w_out_cross, grad_branch):
    grad_queries, grad_kv, grad_w_out = cross_core(
        normed_all, memory_all, w_query_cross, w_kv_cross, w_out_cross, grad_branch
    )
    grad_queries = grad_queries.astype(jnp.bfloat16)
    grad_kv = grad_kv.astype(jnp.bfloat16)
    grad_w_query = jnp.einsum(
        "rld,rle->de", normed_all, grad_queries, preferred_element_type=jnp.float32
    )
    grad_w_kv = jnp.einsum("rmd,rcme->cde", memory_all, grad_kv, preferred_element_type=jnp.float32)
    grad_normed = jnp.einsum(
        "rle,de->rld", grad_queries, w_query_cross, preferred_element_type=jnp.float32
    )
    grad_memory = jnp.einsum(
        "rcme,cde->rmd", grad_kv, w_kv_cross, preferred_element_type=jnp.float32
    )
    return (grad_normed, grad_memory, grad_w_query, grad_w_kv, grad_w_out)


def expert_rows(weights, expert):
    return lax.dynamic_index_in_dim(weights, expert, 0, keepdims=False)


def ffn_partial(normed_all, expert_ids, w_up, w_down):

    def one_row(items):
        normed_row, expert = items
        pre_act = jnp.dot(normed_row, expert_rows(w_up, expert), preferred_element_type=jnp.float32)
        hidden = jax.nn.gelu(pre_act, approximate=False).astype(jnp.bfloat16)
        return jnp.dot(hidden, expert_rows(w_down, expert), preferred_element_type=jnp.float32)

    return lax.map(one_row, (normed_all, expert_ids[:, 0]))


def ffn_backward(normed_all, expert_ids, w_up, w_down, grad_branch):

    def one_row(items):
        normed_row, expert, grad_row = items
        up_rows = expert_rows(w_up, expert)
        down_rows = expert_rows(w_down, expert)
        pre_act = jnp.dot(normed_row, up_rows, preferred_element_type=jnp.float32)
        activated, gelu_back = jax.vjp(partial(jax.nn.gelu, approximate=False), pre_act)
        hidden = activated.astype(jnp.bfloat16)
        grad_hidden = lax.dot_general(
            grad_row, down_rows, (((1,), (1,)), ((), ())), preferred_element_type=jnp.float32
        )
        grad_pre = gelu_back(grad_hidden)[0].astype(jnp.bfloat16)
        grad_down = lax.dot_general(
            hidden, grad_row, (((0,), (0,)), ((), ())), preferred_element_type=jnp.float32
        )
        grad_up = lax.dot_general(
            normed_row, grad_pre, (((0,), (0,)), ((), ())), preferred_element_type=jnp.float32
        )
        grad_normed = lax.dot_general(
            grad_pre, up_rows, (((1,), (1,)), ((), ())), preferred_element_type=jnp.float32
        )
        return (grad_normed, grad_up, grad_down)

    grad_normed, row_up, row_down = lax.map(one_row, (normed_all, expert_ids[:, 0], grad_branch))
    choose = (
        expert_ids[:, 0][:, None] == jnp.arange(w_up.shape[0], dtype=jnp.int32)[None, :]
    ).astype(jnp.float32)
    grad_w_up = jnp.einsum("re,rdf->edf", choose, row_up, precision=lax.Precision.HIGHEST)
    grad_w_down = jnp.einsum("re,rfd->efd", choose, row_down, precision=lax.Precision.HIGHEST)
    return (grad_normed, grad_w_up, grad_w_down)


def run_forward(layer_input, memory, seg_lengths, expert_ids, ln_gains, attn_weights, w_up, w_down):
    w_qkv, w_out_self, w_query_cross, w_kv_cross, w_out_cross = attn_weights
    state_zero = layer_input.astype(jnp.float32)
    normed_local = layer_norm(state_zero, ln_gains[0]).astype(jnp.bfloat16)
    memory_all = lax.all_gather(memory, "tp", axis=1, tiled=True)
    normed_self = spread_tokens(normed_local)
    state_one = state_zero + sum_tokens(self_partial(normed_self, seg_lengths, w_qkv, w_out_self))
    normed_cross = spread_tokens(layer_norm(state_one, ln_gains[1]).astype(jnp.bfloat16))
    state_two = state_one + sum_tokens(
        cross_partial(normed_cross, memory_all, w_query_cross, w_kv_cross, w_out_cross)
    )
    normed_ffn = spread_tokens(layer_norm(state_two, ln_gains[2]).astype(jnp.bfloat16))
    state_three = state_two + sum_tokens(ffn_partial(normed_ffn, expert_ids, w_up, w_down))
    return (
        state_three,
        (state_zero, state_one, state_two, normed_self, normed_cross, normed_ffn, memory_all),
    )


def per_device(
    layer_input,
    memory,
    seg_lengths,
    expert_ids,
    ln_gains,
    w_qkv,
    w_out_self,
    w_query_cross,
    w_kv_cross,
    w_out_cross,
    w_up,
    w_down,
    cotangent,
):
    attn_weights = (w_qkv, w_out_self, w_query_cross, w_kv_cross, w_out_cross)
    use_qkv, use_out_self, use_query, use_kv, use_out_cross = attn_weights
    state_three, kept = run_forward(
        layer_input, memory, seg_lengths, expert_ids, ln_gains, attn_weights, w_up, w_down
    )
    fresh = lax.optimization_barrier((layer_input, memory, state_three))
    unused, kept = run_forward(
        fresh[0], fresh[1], seg_lengths, expert_ids, ln_gains, attn_weights, w_up, w_down
    )
    state_zero, state_one, state_two, normed_self, normed_cross, normed_ffn, memory_all = kept
    grad_state = cotangent.astype(jnp.float32)
    grad_normed, grad_up, grad_down = ffn_backward(
        normed_ffn, expert_ids, w_up, w_down, gather_grads(grad_state)
    )
    grad_state, gain_ffn = norm_backward(state_two, ln_gains[2], sum_grads(grad_normed), grad_state)
    grad_normed, memory_part, grad_w_query, grad_w_kv, grad_w_out_cross = cross_backward(
        normed_cross, memory_all, use_query, use_kv, use_out_cross, gather_grads(grad_state)
    )
    grad_normed, grad_memory = (
        lax.psum_scatter(
            grad_normed.astype(jnp.bfloat16), "tp", scatter_dimension=1, tiled=True
        ).astype(jnp.float32),
        lax.psum_scatter(
            memory_part.astype(jnp.bfloat16), "tp", scatter_dimension=1, tiled=True
        ).astype(jnp.float32),
    )
    grad_state, gain_cross = norm_backward(state_one, ln_gains[1], grad_normed, grad_state)
    grad_normed, grad_w_qkv, grad_w_out_self = self_backward(
        normed_self, seg_lengths, use_qkv, use_out_self, gather_grads(grad_state)
    )
    grad_state, gain_self = norm_backward(
        state_zero, ln_gains[0], sum_grads(grad_normed), grad_state
    )
    summed = (
        lax.psum_scatter(
            grad_w_qkv.astype(jnp.bfloat16), "dp", scatter_dimension=1, tiled=True
        ).astype(jnp.float32),
        lax.psum_scatter(
            grad_w_out_self.astype(jnp.bfloat16), "dp", scatter_dimension=1, tiled=True
        ).astype(jnp.float32),
        lax.psum_scatter(
            grad_w_query.astype(jnp.bfloat16), "dp", scatter_dimension=0, tiled=True
        ).astype(jnp.float32),
        lax.psum_scatter(
            grad_w_kv.astype(jnp.bfloat16), "dp", scatter_dimension=1, tiled=True
        ).astype(jnp.float32),
        lax.psum_scatter(
            grad_w_out_cross.astype(jnp.bfloat16), "dp", scatter_dimension=1, tiled=True
        ).astype(jnp.float32),
        lax.psum_scatter(
            grad_up.astype(jnp.bfloat16), "dp", scatter_dimension=1, tiled=True
        ).astype(jnp.float32),
        lax.psum_scatter(
            grad_down.astype(jnp.bfloat16), "dp", scatter_dimension=2, tiled=True
        ).astype(jnp.float32),
    )
    grad_w_qkv, grad_w_out_self, grad_w_query, grad_w_kv, grad_w_out_cross, grad_up, grad_down = (
        summed
    )
    gain_total = lax.psum(jnp.stack([gain_self, gain_cross, gain_ffn]), ("dp", "tp"))
    share_width = gain_total.shape[1] // lax.axis_size("dp")
    gain_share = lax.dynamic_slice_in_dim(
        gain_total, lax.axis_index("dp") * share_width, share_width, 1
    )
    return (
        state_three.astype(jnp.bfloat16),
        grad_state,
        grad_memory,
        gain_share,
        grad_w_qkv,
        grad_w_out_self,
        grad_w_query,
        grad_w_kv,
        grad_w_out_cross,
        grad_up,
        grad_down,
    )


F32, BF16 = jnp.float32, jnp.bfloat16
MESH = pl.DeviceIdType.MESH
LOG2E = math.log2(math.e)
QSCALE = LOG2E * HEAD_DIM ** -0.5
NN = (((1,), (0,)), ((), ()))
NT = (((1,), (1,)), ((), ()))
TN = (((0,), (0,)), ((), ()))

LEN, WIDTH, COLS, HIDDEN, BLOCK, HALF = 1024, 512, 256, 1024, 256, 512
BLOCKS = LEN // BLOCK
TILE = 256
TILES = HIDDEN // TILE


def dot(left, right, dims=NN):
    return lax.dot_general(left, right, dims, preferred_element_type=F32)


def head_mask(block, side):
    lanes = lax.broadcasted_iota(jnp.int32, block.shape, 1)
    keep = (lanes >= HEAD_DIM) if side else (lanes < HEAD_DIM)
    return jnp.where(keep, block, jnp.zeros_like(block))


def window_bias(key_at, query_at, keys, queries, starts):
    key_place = key_at + lax.broadcasted_iota(jnp.int32, (keys, queries), 0)
    query_place = query_at + lax.broadcasted_iota(jnp.int32, (keys, queries), 1)
    return jnp.where((key_place >= starts) & (key_place <= query_place), 0.0, -1e30)


def add_up(total, part):
    return part if total is None else total + part


def attend(units, q, k, vt, kept, ht, inverse, q_len, k_len, chunk, before=None, after=None):
    def scores(unit):
        h, slot, q_at, k_at, bias = unit
        lanes = slice((h // 2) * 128, (h // 2) * 128 + 128)
        out, top = [], None
        queries = q[pl.ds(q_at, q_len), lanes]
        for j in range(0, k_len, chunk):
            s = dot(head_mask(k[pl.ds(k_at + j, chunk), lanes], h % 2), queries, NT)
            if bias is not None:
                s = s + bias[j:j + chunk]
            out.append(s)
            high = jnp.max(s.reshape(chunk // 8, 8, q_len), axis=0)
            top = high if top is None else jnp.maximum(top, high)
        return out, jnp.max(top, axis=0, keepdims=True)

    def values(unit, made):
        h, slot, q_at, k_at, bias = unit
        rows = slice(h * 64, h * 64 + 64)
        out, total = None, None
        for n, s in enumerate(made[0]):
            p = jnp.exp2(s - made[1])
            total = add_up(total, jnp.sum(p.reshape(chunk // 8, 8, q_len), axis=0))
            low = p.astype(BF16)
            kept[slot, n * chunk:(n + 1) * chunk, :] = low
            out = add_up(out, dot(vt[rows, pl.ds(k_at + n * chunk, chunk)], low))
        inv = 1.0 / jnp.sum(total, axis=0, keepdims=True)
        ht[rows, pl.ds(q_at, q_len)] = (out * inv).astype(BF16)
        inverse[h:h + 1, pl.ds(q_at, q_len)] = inv

    made = None
    for n, unit in enumerate(units):
        if n == 0:
            made = scores(unit)
        following = scores(units[n + 1]) if n + 1 < len(units) else None
        values(unit, made)
        made = following


def attend_back(units, v, kt, qt, gh, ght, kept, inner, inverse, dqt, dkt, dvt, q_len, k_len, chunk):
    def first(unit):
        h, slot, q_at, k_at = unit
        lanes = slice((h // 2) * 128, (h // 2) * 128 + 128)
        grads = gh[pl.ds(q_at, q_len), lanes]
        return [dot(head_mask(v[pl.ds(k_at + j, chunk), lanes], h % 2), grads, NT) for j in range(0, k_len, chunk)]

    def second(unit, made):
        h, slot, q_at, k_at = unit
        rows = slice(h * 64, h * 64 + 64)
        cols = pl.ds(q_at, q_len)
        shift = inner[h:h + 1, cols]
        part_q = None
        for n, dp in enumerate(made):
            at = pl.ds(k_at + n * chunk, chunk)
            p = kept[slot, n * chunk:(n + 1) * chunk, :]
            ds = (p.astype(F32) * (dp - shift)).astype(BF16)
            dvt[rows, at] += dot(ght[rows, cols], p, NT)
            dkt[rows, at] += dot(qt[rows, cols], ds, NT)
            part_q = add_up(part_q, dot(kt[rows, at], ds))
        dqt[rows, cols] = (part_q * (inverse[h:h + 1, cols] * HEAD_DIM ** -0.5)).astype(BF16)

    made = None
    for n, unit in enumerate(units):
        if n == 0:
            made = first(unit)
        following = first(units[n + 1]) if n + 1 < len(units) else None
        second(unit, made)
        made = following


def gelu_parts(pre):
    gauss = jnp.exp2(pre * pre * (-0.5 * LOG2E))
    t = 1.0 / (1.0 + (0.3275911 / math.sqrt(2.0)) * jnp.abs(pre))
    poly = t * (0.254829592 * 0.5 + t * (-0.284496736 * 0.5 + t * (
        1.421413741 * 0.5 + t * (-1.453152027 * 0.5 + t * (1.061405429 * 0.5)))))
    tail = poly * gauss
    phi = jnp.where(pre >= 0, 1.0 - tail, tail)
    return phi, phi + pre * (gauss * (1.0 / math.sqrt(2.0 * math.pi)))


def normalise(x):
    c = x - jnp.mean(x, axis=-1, keepdims=True)
    r = lax.rsqrt(jnp.mean(c * c, axis=-1, keepdims=True) + epsilon)
    return c * r, r


def norm_back(state, gain, grad):
    xhat, r = normalise(state)
    y = grad * gain
    m1 = jnp.mean(y, axis=-1, keepdims=True)
    m2 = jnp.mean(y * xhat, axis=-1, keepdims=True)
    return r * (y - m1 - xhat * m2), jnp.sum(grad * xhat, axis=0, keepdims=True)


def block_rows(i):
    return pl.ds(pl.multiple_of(i * BLOCK, BLOCK), BLOCK)


def each(count, body):
    def step(i, carry):
        body(i)
        return carry

    lax.fori_loop(0, count, step, 0)


def layer_kernel(
    n_dp,
    lens, expert, gains, x_in, mem_in, cot_in, wqkv_in, wos_in, wq_in, wkv_in, woc_in, up_in, down_in,
    lo_out, gi_out, gm_out, e_out, a0_out, a1_out, a2_out, g_out,
    x, mem, cot, wqkv, wos, wq, wkv, woc, up, down, starts,
    s1, s2, gs, n0, n1, n2, q0, k0, v0, q1, k1, v1, vt, ht0, ht1, inv0, inv1, inner,
    kept0, kept1, kept2, gb, dkt, dvt, work, nt, cot_t, eb, a0, a1, a2, ax0, ax1, ax2, ay0, ay1, ay2,
    snd, rcv, sndh, rcvh, leaving, half_out, gain_sum, g_send,
    y_send, y_recv, w_send, w_recv, c_send, c_recv, x_send, x_recv, h_send, h_recv,
    e_send, e_recv, p_send, p_recv, a_send, a_recv, g_ssem, g_rsem, o_send, o_recv,
):
    d, t = lax.axis_index("dp"), lax.axis_index("tp")
    c = lax.rem(d, 2)
    k2 = d - c
    row = k2 + t
    lin = d * 2 + t
    n_all = n_dp * 2
    diag = (k2 + 1 - c, 1 - t)
    sib = (k2 + 1 - c, t)
    swaps = c != t
    stays = c == t

    def remote(src, dst, ssem, rsem, to):
        return pltpu.make_async_remote_copy(
            src_ref=src, dst_ref=dst, send_sem=ssem, recv_sem=rsem, device_id=to, device_id_type=MESH)

    own = pl.ds(pl.multiple_of(c * HALF, HALF), HALF)
    other = pl.ds(pl.multiple_of((1 - c) * HALF, HALF), HALF)
    theirs = pl.ds(pl.multiple_of(t * HALF, HALF), HALF)

    X, MEM, COT, UP, DOWN = 0, 1, 2, 3, 3 + TILES
    n_brought = 3 + 2 * TILES

    def tile(f):
        return pl.ds(pl.multiple_of(f * TILE, TILE), TILE)

    def bring(n, place):
        if n < UP:
            src, dst = ((x_in, x), (mem_in, mem), (cot_in, cot))[n]
            dst = dst.at[place]
        elif n < DOWN:
            src, dst = up_in.at[:, tile(n - UP)], up.at[:, tile(n - UP)]
        else:
            src, dst = down_in.at[tile(n - DOWN)], down.at[tile(n - DOWN)]
        return (lambda: remote(src, dst, y_send.at[n], y_recv.at[n], diag),
                lambda: pltpu.make_async_copy(src, dst, y_recv.at[n]))

    def start_bring(n):
        far, near = bring(n, theirs)

        @pl.when(swaps)
        def _():
            far().start()

    def start_near(n):
        far, near = bring(n, own)

        @pl.when(stays)
        def _():
            near().start()

    def wait_bring(n):
        far, near = bring(n, own)

        @pl.when(swaps)
        def _():
            far().wait_recv()

        @pl.when(stays)
        def _():
            near().wait()

    def share(n, buf):
        return remote(buf.at[own], buf.at[own], c_send.at[n], c_recv.at[n], sib)

    def share_starts():
        return remote(starts, starts, c_send.at[3], c_recv.at[3], sib)

    n_pairs = n_dp // 2
    pair = lax.div(d, 2)
    halves = [(wqkv_in, wqkv), (wos_in, wos), (wq_in, wq), (wkv_in, wkv), (woc_in, woc)]
    WQKV, WOS, WQ, WKV, WOC = range(5)

    def piece(ref, p):
        if len(ref.shape) == 3:
            rows = ref.shape[1] // n_pairs
            return ref.at[:, pl.ds(pl.multiple_of(p * rows, rows), rows)]
        rows = ref.shape[0] // n_pairs
        return ref.at[pl.ds(pl.multiple_of(p * rows, rows), rows)]

    def first_piece(n):
        src, dst = halves[n]
        return remote(piece(src, pair), piece(dst, pair), w_send.at[n, 0], w_recv.at[n, pair], diag)

    def hand_piece(n, s):
        dst = halves[n][1]
        to = lax.rem(pair + s, n_pairs)
        return remote(piece(dst, pair), piece(dst, pair), w_send.at[n, s], w_recv.at[n, pair], (2 * to + c, t))

    def near_weight(n):
        src, dst = halves[n]
        return pltpu.make_async_copy(src, dst, w_recv.at[n, 0])

    def hand_round(n):
        first_piece(n).wait_recv()
        each(n_pairs - 1, lambda s: hand_piece(n, s + 1).start())

    def wait_weight(n):
        @pl.when(swaps)
        def _():
            def one(s):
                dst = halves[n][1]
                p = lax.rem(pair + s + 1, n_pairs)
                remote(piece(dst, p), piece(dst, p), w_send.at[n, 0], w_recv.at[n, p], diag).wait_recv()

            each(n_pairs - 1, one)

        @pl.when(stays)
        def _():
            near_weight(n).wait()

    start_near(X)

    @pl.when(stays)
    def _():
        near_weight(WQKV).start()

    start_near(MEM)
    start_near(COT)

    @pl.when(stays)
    def _():
        for n in (WOS, WKV, WQ, WOC):
            near_weight(n).start()

    for f in range(TILES):
        start_near(UP + f)
        start_near(DOWN + f)
    barrier = pltpu.get_barrier_semaphore()

    def greet(i):
        to = lax.rem(lin + 1 + i, n_all)
        pl.semaphore_signal(barrier, inc=1, device_id=(lax.div(to, 2), lax.rem(to, 2)), device_id_type=MESH)

    each(n_all - 1, greet)

    @pl.when(stays)
    def _():
        places = lax.broadcasted_iota(jnp.int32, (8, LEN), 1)
        start, level = jnp.int32(0), jnp.zeros((8, LEN), jnp.int32)
        for s in range(lens.shape[1]):
            level = jnp.where(places >= start, start, level)
            start = start + lens[0, s]
        starts[...] = level

    pl.semaphore_wait(barrier, n_all - 1)

    @pl.when(swaps)
    def _():
        first_piece(WQKV).start()

    start_bring(X)

    @pl.when(swaps)
    def _():
        for n in (WOS, WKV, WQ, WOC):
            first_piece(n).start()

    start_bring(MEM)
    start_bring(COT)
    for f in range(TILES):
        start_bring(UP + f)
        start_bring(DOWN + f)

    @pl.when(swaps)
    def _():
        hand_round(WQKV)

    @pl.when(stays)
    def _():
        share_starts().start()

    def wait_near(n):
        near = bring(n, own)[1]

        @pl.when(stays)
        def _():
            near().wait()

    def wait_swapped(n):
        far = bring(n, own)[0]

        @pl.when(swaps)
        def _():
            far().wait_recv()

    wait_bring(X)
    share(0, x).start()

    @pl.when(stays)
    def _():
        wait_near(MEM)
        share(1, mem).start()
        wait_near(COT)
        share(2, cot).start()

    def self_project(i):
        r = block_rows(i)
        xhat, _ = normalise(x[r, :].astype(F32))
        nn = (xhat * gains[0:1, :]).astype(BF16)
        n0[r, :] = nn
        q0[r, :] = (dot(nn, wqkv[0]) * QSCALE).astype(BF16)
        k0[r, :] = dot(nn, wqkv[1]).astype(BF16)
        v0[r, :] = dot(nn, wqkv[2]).astype(BF16)

    @pl.when(swaps)
    def _():
        for n in (WOS, WKV, WQ, WOC):
            hand_round(n)

    wait_weight(WQKV)
    each(2, lambda i: self_project(c * 2 + i))
    share(0, x).wait_recv()
    each(2, lambda i: self_project((1 - c) * 2 + i))
    vt[...] = v0[...].T

    @pl.when(swaps)
    def _():
        share_starts().wait_recv()

    wait_weight(WOS)

    def exchange(e, i):
        r = block_rows(i)
        return remote(snd.at[e % 2, r], rcv.at[e % 2, r], x_send.at[e, i], x_recv.at[e, i], sib)

    def out_of(e, i, ht, w_out):
        r = block_rows(i)
        snd[e % 2, r, :] = dot(ht[:, r], w_out[...], TN).astype(BF16)
        exchange(e, i).start()

    everything = range(4)
    first_bias = window_bias(0, 0, 256, 256, starts[0:1, 0:256])
    attend([(h, h, 0, 0, first_bias) for h in everything], q0, k0, vt, kept0, ht0, inv0, 256, 256, 256)
    out_of(0, 0, ht0, wos)

    def self_block(j):
        i = j + 1
        q_at = pl.multiple_of(i * 256, 256)
        k_at = pl.multiple_of(j * 256, 256)
        bias = window_bias(k_at, q_at, 512, 256, starts[0:1, pl.ds(q_at, 256)])
        attend([(h, j * 4 + h, q_at, k_at, bias) for h in everything], q0, k0, vt, kept1, ht0, inv0, 256, 512, 256)
        out_of(0, i, ht0, wos)

    each(BLOCKS - 1, self_block)

    wait_swapped(MEM)

    @pl.when(swaps)
    def _():
        share(1, mem).start()

    wait_weight(WKV)

    def memory_project(i):
        r = block_rows(i)
        k1[r, :] = dot(mem[r, :], wkv[0]).astype(BF16)
        v1[r, :] = dot(mem[r, :], wkv[1]).astype(BF16)

    each(2, lambda i: memory_project(c * 2 + i))
    share(1, mem).wait_recv()
    each(2, lambda i: memory_project((1 - c) * 2 + i))
    vt[...] = v1[...].T
    wait_weight(WQ)
    wait_weight(WOC)

    def cross_norm(i):
        r = block_rows(i)
        exchange(0, i).wait_recv()
        state = x[r, :].astype(F32) + (snd[0, r, :].astype(F32) + rcv[0, r, :].astype(F32))
        s1[r, :] = state
        xhat, _ = normalise(state)
        nn = (xhat * gains[1:2, :]).astype(BF16)
        n1[r, :] = nn
        q1[r, :] = (dot(nn, wq[...]) * QSCALE).astype(BF16)

    each(BLOCKS, cross_norm)

    def cross_pair(j):
        units = []
        for i in range(2):
            for h in everything:
                at = pl.multiple_of((j * 2 + i) * 256, 256)
                units.append((h, (j * 2 + i) * 4 + h, at, 0, None))
        attend(units, q1, k1, vt, kept2, ht1, inv1, 256, LEN, 256)
        out_of(1, j * 2, ht1, woc)
        out_of(1, j * 2 + 1, ht1, woc)

    each(BLOCKS // 2, cross_pair)

    wait_swapped(COT)

    @pl.when(swaps)
    def _():
        share(2, cot).start()

    def half_exchange(e, i):
        r = block_rows(i)
        return remote(sndh.at[e, r], rcvh.at[e, r], h_send.at[e, i], h_recv.at[e, i], sib)

    def expert_norm(i):
        r = block_rows(i)
        exchange(1, i).wait_recv()
        state = s1[r, :] + (snd[1, r, :].astype(F32) + rcv[1, r, :].astype(F32))
        s2[r, :] = state
        xhat, _ = normalise(state)
        n2[r, :] = (xhat * gains[2:3, :]).astype(BF16)

    each(BLOCKS, expert_norm)
    nt[...] = n2[...].T
    share(2, cot).wait_recv()
    cot_t[...] = cot[...].T

    def begin(copy):
        copy.start()

    def finish_send(copy):
        copy.wait_send()

    def share_rows(ref, to):
        return ref.at[pl.ds(pl.multiple_of(to * 32, 32), 32)]

    def scatter(f, action):
        src, dst = eb.at[f], e_out.at[row, f]

        @pl.when(stays)
        def _():
            if action is begin:
                pltpu.make_async_copy(share_rows(src, d), dst, e_recv.at[f, row]).start()

        @pl.when(swaps)
        def _():
            action(remote(share_rows(src, d), dst, e_send.at[f, 0], e_recv.at[f, row], (d, c)))

        def one(s):
            to = lax.rem(d + s + 1, n_dp)
            action(remote(share_rows(src, to), dst, e_send.at[f, s + 1], e_recv.at[f, row], (to, c)))

        each(n_dp - 1, one)

    def collect(f):
        def one(i):
            src, dst = eb.at[f, pl.ds(0, 32)], e_out.at[i, f]

            @pl.when(stays & (i == row))
            def _():
                pltpu.make_async_copy(src, dst, e_recv.at[f, i]).wait()

            @pl.when(jnp.logical_not(stays & (i == row)))
            def _():
                remote(src, dst, e_send.at[f, 0], e_recv.at[f, i], diag).wait_recv()

        each(n_dp, one)

    hid, gpre = work.at[0:LEN], work.at[LEN:2 * LEN]

    def expert_tile(f):
        cols = slice(f * TILE, (f + 1) * TILE)

        def first(i):
            r = slice(i * BLOCK, (i + 1) * BLOCK)
            return dot(n2[r, :], up[:, cols]), dot(cot[r, :], down[cols, :], NT)

        def second(i, made):
            r = slice(i * BLOCK, (i + 1) * BLOCK)
            pre, grad = made
            phi, slope = gelu_parts(pre)
            hid[r, cols] = (pre * phi).astype(BF16)
            gpre[r, cols] = (grad * slope).astype(BF16)

        made = first(0)
        for i in range(BLOCKS):
            following = first(i + 1) if i + 1 < BLOCKS else None
            second(i, made)
            made = following
        eb[f, :, 0:TILE] = dot(nt[...], gpre[:, cols]).astype(BF16)
        eb[f, :, TILE:2 * TILE] = dot(cot_t[...], hid[:, cols]).astype(BF16)
        scatter(f, begin)

    for f in range(TILES):
        wait_bring(UP + f)
        wait_bring(DOWN + f)
        expert_tile(f)

    def done_sending(e):
        each(BLOCKS, lambda i: exchange(e, i).wait_send())

    done_sending(0)

    def expert_back(i):
        r = block_rows(i)
        snd[0, r, :] = dot(gpre[r, :], up[...], NT).astype(BF16)
        exchange(2, i).start()

    each(BLOCKS, expert_back)

    def expert_out(i):
        r = block_rows(i)
        part = dot(hid[r, :], down[...])
        mine = lax.div(i, 2) == c
        rl = block_rows(lax.rem(i, 2))

        @pl.when(mine)
        def _():
            half_out[rl, :] = s2[r, :] + part

        @pl.when(jnp.logical_not(mine))
        def _():
            sndh[0, rl, :] = part.astype(BF16)
            half_exchange(0, lax.rem(i, 2)).start()

    each(BLOCKS, expert_out)

    def strip(n):
        return work.at[n * COLS:(n + 1) * COLS]

    dqt, dkb, dvb, ght = strip(0), strip(1), strip(2), strip(3)
    kt, qt = cot_t.at[0:COLS], cot_t.at[COLS:2 * COLS]
    dq, dk = down.at[:, 0:COLS], down.at[:, COLS:2 * COLS]
    gh, dv = n2.at[:, 0:COLS], n2.at[:, COLS:2 * COLS]
    gain_sum[...] = jnp.zeros_like(gain_sum)

    def branch_block(n, i, e, state, base, ht, inv, w_out):
        r = block_rows(i)
        exchange(e, i).wait_recv()
        grad = snd[e % 2, r, :].astype(F32) + rcv[e % 2, r, :].astype(F32)
        step, share_gain = norm_back(state[r, :], gains[n:n + 1, :], grad)
        total = base[r, :].astype(F32) + step
        gs[r, :] = total
        low = total.astype(BF16)
        gb[r, :] = low
        gain_sum[n:n + 1, :] += jnp.where(lax.div(i, 2) == c, share_gain, 0.0)
        gh[r, :] = dot(low, w_out[...], NT).astype(BF16)
        turned = dot(w_out[...], low, NT).astype(BF16).astype(F32)
        prod = turned * ht[:, r].astype(F32)
        for h in everything:
            rows = slice(h * 64, h * 64 + 64)
            inner[h:h + 1, r] = jnp.sum(prod[rows], axis=0, keepdims=True)
            ght[rows, r] = (turned[rows] * inv[h:h + 1, r]).astype(BF16)

    def turn_queries(q, k, inv):
        kt[...] = k[...].T
        turned = q[...].T
        for h in everything:
            rows = slice(h * 64, h * 64 + 64)
            qt[rows, :] = (turned[rows].astype(F32) * inv[h:h + 1, :]).astype(BF16)
        dkt[...] = jnp.zeros_like(dkt)
        dvt[...] = jnp.zeros_like(dvt)

    zs = n_dp // 4
    side = lax.rem(pair, 2)
    z = lax.div(d, 4)
    across = (d + 2 - 4 * side, t)
    pieces = ((a0, ax0, ay0, a0_out), (a1, ax1, ay1, a1_out), (a2, ax2, ay2, a2_out))

    def over_x(n):
        buf, place = pieces[n][:2]
        return remote(buf.at[:, 1 - side], place, p_send.at[0, n], p_recv.at[0, n], across)

    def over_y(n):
        buf, place = pieces[n][0], pieces[n][2]
        return remote(buf.at[:, side], place, p_send.at[1, n], p_recv.at[1, n], (d, c))

    def add_x(n):
        buf, place = pieces[n][:2]
        over_x(n).wait_recv()
        buf[:, side] = (buf[:, side].astype(F32) + place[...].astype(F32)).astype(BF16)

        @pl.when(swaps)
        def _():
            over_y(n).start()

    def owners(n, action):
        buf, out = pieces[n][0], pieces[n][3]

        def one(s):
            to = lax.rem(z * 2 + c + s + 1, 2 * zs)
            to_z, to_c = lax.div(to, 2), lax.rem(to, 2)
            src = buf.at[to_z, side, pl.ds(pl.multiple_of(to_c * 32, 32), 32)]
            action(remote(src, out.at[z], a_send.at[n, s], a_recv.at[n, z], (to_z * 4 + side * 2 + to_c, t)))

        each(2 * zs - 1, one)

    def own_share(n):
        src = pieces[n][0].at[z, side, pl.ds(pl.multiple_of(c * 32, 32), 32)]
        return pltpu.make_async_copy(src, pieces[n][3].at[z], a_recv.at[n, z])

    def add_y(n):
        @pl.when(stays)
        def _():
            buf, place = pieces[n][0], pieces[n][2]
            over_y(n).wait_recv()
            buf[:, side] = (buf[:, side].astype(F32) + place[...].astype(F32)).astype(BF16)
            own_share(n).start()
            owners(n, begin)

    def collect_piece(n):
        buf, out = pieces[n][0], pieces[n][3]

        def one(i):
            @pl.when(stays & (i == z))
            def _():
                own_share(n).wait()

            @pl.when(jnp.logical_not(stays & (i == z)))
            def _():
                remote(buf.at[0, 0, pl.ds(0, 32)], out.at[i], a_send.at[n, 0], a_recv.at[n, i], diag).wait_recv()

        each(zs, one)

        @pl.when(stays)
        def _():
            owners(n, finish_send)

        @pl.when(swaps)
        def _():
            over_y(n).wait_send()

        over_x(n).wait_send()

    def by_owner(grad):
        return grad.astype(BF16).T.reshape(zs, 2, WIDTH // (2 * zs), grad.shape[0])

    each(BLOCKS, lambda i: branch_block(2, i, 2, s2, cot, ht1, inv1, woc))
    turn_queries(q1, k1, inv1)

    def cross_back(h):
        units = [(hh, i * 4 + hh, i * 256, 0) for hh in (2 * h, 2 * h + 1) for i in range(BLOCKS)]
        attend_back(units, v1, kt, qt, gh, ght, kept2, inner, inv1, dqt, dkt, dvt, 256, LEN, 256)

    cross_back(0)
    cross_back(1)

    def leave(n, out):
        buf = leaving.at[n]
        return (lambda: remote(buf, out, o_send.at[n], o_recv.at[n], diag),
                lambda: pltpu.make_async_copy(buf, out, o_recv.at[n]))

    def start_leave(n, out):
        far, near = leave(n, out)

        @pl.when(swaps)
        def _():
            far().start()

        @pl.when(stays)
        def _():
            near().start()

    def wait_leave(n, out):
        far, near = leave(n, out)

        @pl.when(swaps)
        def _():
            far().wait()

        @pl.when(stays)
        def _():
            near().wait()

    def half_done(n, out):
        def one(low):
            half_exchange(n, low).wait_recv()
            r = block_rows(low)
            leaving[n, r, :] = (half_out[r, :] + rcvh[n, r, :].astype(F32)).astype(BF16)

        each(2, one)
        start_leave(n, out)

    half_done(0, lo_out)

    def settle():
        dkb[...] = (dkt[...] * math.log(2.0)).astype(BF16)
        dvb[...] = dvt[...].astype(BF16)
        dq[...] = dqt[...].T
        dk[...] = dkb[...].T
        dv[...] = dvb[...].T

    settle()
    done_sending(1)

    def cross_grads(i):
        r = block_rows(i)
        snd[1, r, :] = dot(dq[r, :], wq[...], NT).astype(BF16)
        exchange(3, i).start()

    each(BLOCKS, cross_grads)
    a0[:, :, :, 0:256] = by_owner(dot(ht1[...], gb[...]))
    a0[:, :, :, 256:512] = by_owner(dot(dqt[...], n1[...]))
    a0[:, :, :, 512:768] = by_owner(dot(dkb[...], mem[...]))
    a0[:, :, :, 768:1024] = by_owner(dot(dvb[...], mem[...]))
    over_x(0).start()

    def memory_grads(i):
        r = block_rows(i)
        part = dot(dk[r, :], wkv[0], NT) + dot(dv[r, :], wkv[1], NT)
        mine = lax.div(i, 2) == c
        rl = block_rows(lax.rem(i, 2))

        @pl.when(mine)
        def _():
            half_out[rl, :] = part

        @pl.when(jnp.logical_not(mine))
        def _():
            sndh[1, rl, :] = part.astype(BF16)
            half_exchange(1, lax.rem(i, 2)).start()

    each(BLOCKS, memory_grads)

    each(BLOCKS, lambda i: branch_block(1, i, 3, s1, gs, ht0, inv0, wos))
    half_done(1, gm_out)
    turn_queries(q0, k0, inv0)

    def self_back(pair_of_heads):
        heads = (2 * pair_of_heads, 2 * pair_of_heads + 1)
        attend_back([(h, h, 0, 0) for h in heads], v0, kt, qt, gh, ght, kept0, inner, inv0, dqt, dkt, dvt, 256, 256, 256)
        units = [(h, j * 4 + h, (j + 1) * 256, j * 256) for h in heads for j in range(BLOCKS - 1)]
        attend_back(units, v0, kt, qt, gh, ght, kept1, inner, inv0, dqt, dkt, dvt, 256, 512, 256)
        rows = slice(pair_of_heads * 128, pair_of_heads * 128 + 128)
        dkb[rows, :] = (dkt[rows, :] * math.log(2.0)).astype(BF16)
        dvb[rows, :] = dvt[rows, :].astype(BF16)
        buf = pieces[1 + pair_of_heads][0]
        for n, grad in enumerate((dqt, dkb, dvb)):
            buf[:, :, :, n * 128:n * 128 + 128] = by_owner(dot(grad[rows, :], n0[...]))

    a1[:, :, :, 384:640] = by_owner(dot(ht0[...], gb[...]))
    self_back(0)
    over_x(1).start()
    add_x(0)
    self_back(1)
    over_x(2).start()
    dq[...] = dqt[...].T
    dk[...] = dkb[...].T
    dv[...] = dvb[...].T

    def input_grads(i):
        r = block_rows(i)
        return dot(dq[r, :], wqkv[0], NT) + dot(dk[r, :], wqkv[1], NT) + dot(dv[r, :], wqkv[2], NT)

    def input_send(low):
        sndh[2, block_rows(low), :] = input_grads((1 - c) * 2 + low).astype(BF16)
        half_exchange(2, low).start()

    each(2, input_send)
    add_y(0)
    add_x(1)

    def input_keep(low):
        half_out[block_rows(low), :] = input_grads(c * 2 + low)

    each(2, input_keep)

    def input_done(low):
        half_exchange(2, low).wait_recv()
        rl = block_rows(low)
        r = block_rows(c * 2 + low)
        grad = half_out[rl, :] + rcvh[2, rl, :].astype(F32)
        step, share_gain = norm_back(x[r, :].astype(F32), gains[0:1, :], grad)
        gain_sum[0:1, :] += share_gain
        leaving[2, rl, :] = (gs[r, :] + step).astype(BF16)

    each(2, input_done)
    start_leave(2, gi_out)
    add_x(2)
    add_y(1)

    number = jnp.full((1, 128), expert[0, 0].astype(F32))
    for j in range(n_dp):
        turned = gain_sum[...] if j == 0 else pltpu.roll(gain_sum[...], (WIDTH - 32 * j) % WIDTH, 1)
        g_send[j] = turned[:, :128]
        g_send[j, 3:4, :] = number

    def gain_copy(s):
        to = lax.rem(lin + s, n_all)
        to_dp = lax.div(to, 2)
        return remote(g_send.at[to_dp], g_out.at[lin], g_ssem.at[s], g_rsem.at[lin], (to_dp, lax.rem(to, 2)))

    each(n_all - 1, lambda s: gain_copy(s + 1).start())
    keep_gain = pltpu.make_async_copy(g_send.at[d], g_out.at[lin], g_rsem.at[lin])
    keep_gain.start()

    add_y(2)

    wait_leave(0, lo_out)
    wait_leave(1, gm_out)
    wait_leave(2, gi_out)
    for f in range(TILES):
        collect(f)
        scatter(f, finish_send)
    for n in range(3):
        collect_piece(n)
    keep_gain.wait()

    def gain_wait(s):
        gain_copy(s + 1).wait_send()
        who = lax.rem(lin + s + 1, n_all)
        remote(g_send.at[0], g_out.at[who], g_ssem.at[0], g_rsem.at[who], diag).wait_recv()

    each(n_all - 1, gain_wait)

    @pl.when(swaps)
    def _():
        for n in range(n_brought):
            bring(n, theirs)[0]().wait_send()
        for n in range(5):
            first_piece(n).wait_send()
            each(n_pairs - 1, lambda s: hand_piece(n, s + 1).wait_send())

    for n, buf in enumerate((x, mem, cot)):
        share(n, buf).wait_send()

    @pl.when(stays)
    def _():
        share_starts().wait_send()

    done_sending(2)
    done_sending(3)
    for e in range(3):
        each(2, lambda i: half_exchange(e, i).wait_send())


VMEM_BYTES = 63 * 2**20
ANY_PLACE = pl.BlockSpec(memory_space=pl.ANY)
IN_HBM = pl.BlockSpec(memory_space=pltpu.HBM)
IN_SMEM = pl.BlockSpec(memory_space=pltpu.SMEM)
IN_VMEM = pl.BlockSpec(memory_space=pltpu.VMEM)


def paired_layer(n_dp, lens, expert, gains, *arrays):
    bf = lambda *shape: pltpu.VMEM(shape, BF16)
    fl = lambda *shape: pltpu.VMEM(shape, F32)
    dma = lambda *shape: pltpu.SemaphoreType.DMA(shape)
    tokens = bf(LEN, WIDTH)
    heads = bf(LEN, COLS)
    turned = bf(COLS, LEN)
    half = jax.ShapeDtypeStruct((HALF, WIDTH), BF16)
    zs = n_dp // 4
    sizes = (4 * COLS, 5 * COLS // 2, 3 * COLS // 2)
    split = [bf(zs, 2, WIDTH // (2 * zs), size) for size in sizes]
    parts = [bf(zs, WIDTH // (2 * zs), size) for size in sizes]
    return pl.pallas_call(
        partial(layer_kernel, n_dp),
        out_shape=(half, half, half, jax.ShapeDtypeStruct((n_dp, TILES, 32, 2 * TILE), BF16),
                   *[jax.ShapeDtypeStruct((zs, 32, size), BF16) for size in sizes],
                   jax.ShapeDtypeStruct((2 * n_dp, 8, 128), F32)),
        in_specs=[IN_SMEM] * 2 + [IN_VMEM] + [ANY_PLACE] * 10,
        out_specs=(ANY_PLACE,) * 8,
        scratch_shapes=[
            tokens, tokens, tokens, bf(3, WIDTH, COLS), bf(COLS, WIDTH), bf(WIDTH, COLS), bf(2, WIDTH, COLS),
            bf(COLS, WIDTH), bf(WIDTH, HIDDEN), bf(HIDDEN, WIDTH), pltpu.VMEM((8, LEN), jnp.int32),
            fl(LEN, WIDTH), fl(LEN, WIDTH), fl(LEN, WIDTH), tokens, tokens, tokens,
            heads, heads, heads, heads, heads, heads, turned, turned, turned, fl(8, LEN), fl(8, LEN), fl(8, LEN),
            bf(4, 256, 256), bf(12, 512, 256), bf(16, LEN, 256), tokens, fl(COLS, LEN), fl(COLS, LEN),
            bf(2 * LEN, HIDDEN), bf(WIDTH, LEN), bf(WIDTH, LEN), bf(TILES, WIDTH, 2 * TILE), *split, *parts, *parts,
            bf(2, LEN, WIDTH), bf(2, LEN, WIDTH), bf(3, HALF, WIDTH), bf(3, HALF, WIDTH), bf(3, HALF, WIDTH),
            fl(HALF, WIDTH), fl(8, WIDTH), fl(n_dp, 8, 128),
            dma(3 + 2 * TILES), dma(3 + 2 * TILES), dma(5, n_dp // 2), dma(5, n_dp // 2), dma(4), dma(4),
            dma(4, 4), dma(4, 4), dma(3, 2), dma(3, 2),
            dma(TILES, n_dp), dma(TILES, n_dp), dma(2, 3), dma(2, 3), dma(3, 2 * zs), dma(3, zs),
            dma(2 * n_dp), dma(2 * n_dp), dma(3), dma(3),
        ],
        compiler_params=pltpu.CompilerParams(
            collective_id=0, has_side_effects=True, vmem_limit_bytes=VMEM_BYTES),
        cost_estimate=pl.CostEstimate(flops=20 * 10**9, bytes_accessed=20 * 2**20, transcendentals=0),
    )(lens, expert, gains, *arrays)


def choose_kernel(expert, up_in, down_in, up_out, down_out, sems):
    e = expert[0, 0]
    parts = 4
    copies = []
    for p in range(parts):
        for n, (src, dst) in enumerate(((up_in, up_out), (down_in, down_out))):
            rows = dst.shape[0] // parts
            at = pl.ds(p * rows, rows)
            copies.append(pltpu.make_async_copy(src.at[e, at], dst.at[at], sems.at[n, p]))
    for copy in copies:
        copy.start()
    for copy in copies:
        copy.wait()


def choose_expert(expert, w_up, w_down):
    return pl.pallas_call(
        choose_kernel,
        out_shape=(jax.ShapeDtypeStruct(w_up.shape[1:], BF16), jax.ShapeDtypeStruct(w_down.shape[1:], BF16)),
        in_specs=[IN_SMEM, ANY_PLACE, ANY_PLACE],
        out_specs=(IN_VMEM, IN_VMEM),
        scratch_shapes=[pltpu.SemaphoreType.DMA((2, 4))],
        compiler_params=pltpu.CompilerParams(vmem_limit_bytes=VMEM_BYTES),
    )(expert, w_up, w_down)


def place_kernel(
    gains_any, e_any, a0_any, a1_any, a2_any, gi_any, gm_any, lo_any,
    lo_out, gi_out, gm_out, gain_out, qkv_out, os_out, q_out, kv_out, oc_out, up_out, down_out,
    ids, gains_in, e_in, a0_in, a1_in, a2_in, gi_in, gm_in, lo_in, gi_v, gm_v, ups, downs, in_sems, e_sems, up_sems, down_sems, out_sems,
):
    rows = e_in.shape[0]
    number = pltpu.make_async_copy(gains_any, ids, in_sems.at[0])
    number.start()
    blocks = [pltpu.make_async_copy(e_any.at[r], e_in.at[r], e_sems.at[r]) for r in range(rows)]
    for copy in blocks:
        copy.start()
    pairs = ((lo_any, lo_in), (gi_any, gi_in), (gm_any, gm_in), (gains_any, gains_in), (a0_any, a0_in),
             (a1_any, a1_in), (a2_any, a2_in))
    reads = [pltpu.make_async_copy(src, dst, in_sems.at[1 + n]) for n, (src, dst) in enumerate(pairs)]
    for copy in reads:
        copy.start()
    number.wait()
    writes = []

    def write(src, dst, sem):
        writes.append(pltpu.make_async_copy(src, dst, sem))
        writes[-1].start()

    for r in range(rows):
        blocks[r].wait()
        for f in range(TILES):
            ups[r, :, f * TILE:(f + 1) * TILE] = e_in[r, f, :, 0:TILE].astype(F32)
            downs[r, :, f * TILE:(f + 1) * TILE] = e_in[r, f, :, TILE:2 * TILE].astype(F32)
        e = ids[2 * r, 3, 0].astype(jnp.int32)
        write(ups.at[r], up_out.at[e], up_sems.at[r])
        write(downs.at[r], down_out.at[e], down_sems.at[r])
    reads[0].wait()
    write(lo_in, lo_out, out_sems.at[2])
    reads[1].wait()
    gi_v[...] = gi_in[...].astype(F32)
    write(gi_v, gi_out, out_sems.at[0])
    reads[2].wait()
    gm_v[...] = gm_in[...].astype(F32)
    write(gm_v, gm_out, out_sems.at[1])
    for copy in reads[3:]:
        copy.wait()
    gain_out[...] = jnp.sum(gains_in[...], axis=0)[:3, :32]
    first = jnp.sum(a0_in[...].astype(F32), axis=0)
    oc_out[...] = first[:, 0:COLS]
    q_out[...] = first[:, COLS:2 * COLS]
    kv_out[0] = first[:, 2 * COLS:3 * COLS]
    kv_out[1] = first[:, 3 * COLS:4 * COLS]
    second = jnp.sum(a1_in[...].astype(F32), axis=0)
    third = jnp.sum(a2_in[...].astype(F32), axis=0)
    for n in range(3):
        qkv_out[n, :, 0:128] = second[:, n * 128:n * 128 + 128]
        qkv_out[n, :, 128:256] = third[:, n * 128:n * 128 + 128]
    os_out[...] = second[:, 384:640]
    for copy in writes:
        copy.wait()


def place_grads(experts, *arrays):
    shape = lambda *dims: jax.ShapeDtypeStruct(dims, F32)
    like = lambda array: pltpu.VMEM(array.shape, array.dtype)
    dma = lambda *dims: pltpu.SemaphoreType.DMA(dims)
    rows = arrays[1].shape[0]
    staged = pltpu.VMEM((rows, 32, HIDDEN), F32)
    half = pltpu.VMEM((HALF, WIDTH), F32)
    return pl.pallas_call(
        place_kernel,
        out_shape=(jax.ShapeDtypeStruct((HALF, WIDTH), BF16), shape(HALF, WIDTH), shape(HALF, WIDTH), shape(3, 32), shape(3, 32, COLS), shape(32, COLS),
                   shape(32, COLS), shape(2, 32, COLS), shape(32, COLS),
                   shape(experts, 32, HIDDEN), shape(experts, 32, HIDDEN)),
        in_specs=[IN_HBM] * 8,
        out_specs=(IN_HBM,) * 3 + (IN_VMEM,) * 6 + (IN_HBM,) * 2,
        scratch_shapes=[pltpu.SMEM(arrays[0].shape, F32)] + [like(array) for array in arrays] + [
            half, half, staged, staged, dma(8), dma(rows), dma(rows), dma(rows), dma(3)],
        compiler_params=pltpu.CompilerParams(vmem_limit_bytes=VMEM_BYTES),
    )(*arrays)


def per_device_paired(
    layer_input, memory, seg_lengths, expert_ids, ln_gains, w_qkv, w_out_self, w_query_cross, w_kv_cross,
    w_out_cross, w_up, w_down, cotangent,
):
    n_dp = lax.axis_size("dp")
    up, down = choose_expert(expert_ids, w_up, w_down)
    layer_output, grad_input, grad_memory, e_rows, a0_rows, a1_rows, a2_rows, gain_rows = paired_layer(
        n_dp, seg_lengths, expert_ids, ln_gains,
        layer_input[0], memory[0], cotangent[0], w_qkv, w_out_self, w_query_cross, w_kv_cross, w_out_cross, up, down,
    )
    layer_output, grad_input, grad_memory, gain_share, qkv, out_self, query, key_value, out_cross, grad_up, grad_down = place_grads(
        w_up.shape[0], gain_rows, e_rows, a0_rows, a1_rows, a2_rows, grad_input, grad_memory, layer_output)
    return (
        layer_output[None], grad_input[None], grad_memory[None], gain_share, qkv, out_self.T, query, key_value,
        out_cross.T, grad_up, jnp.swapaxes(grad_down, 1, 2),
    )


def fits_pairs(mesh, layer_input, seg_lengths, w_up):
    return (
        mesh.shape["tp"] == 2
        and mesh.shape["dp"] == 16
        and layer_input.shape == (mesh.shape["dp"], LEN, WIDTH)
        and w_up.shape == (mesh.shape["dp"], WIDTH, 2 * HIDDEN)
    )


def solution(mesh):
    in_specs = (
        P("dp", "tp", None),
        P("dp", "tp", None),
        P("dp", None),
        P("dp", None),
        P(),
        P(None, None, "tp"),
        P("tp", None),
        P(None, "tp"),
        P(None, None, "tp"),
        P("tp", None),
        P(None, None, "tp"),
        P(None, "tp", None),
        P("dp", "tp", None),
    )
    out_specs = (
        P("dp", "tp", None),
        P("dp", "tp", None),
        P("dp", "tp", None),
        P(None, "dp"),
        P(None, "dp", "tp"),
        P("tp", "dp"),
        P("dp", "tp"),
        P(None, "dp", "tp"),
        P("tp", "dp"),
        P(None, "dp", "tp"),
        P(None, "tp", "dp"),
    )

    def run(*args):
        layer_input, seg_lengths, w_up = args[0], args[2], args[10]
        paired = fits_pairs(mesh, layer_input, seg_lengths, w_up)
        return jax.shard_map(
            per_device_paired if paired else per_device,
            mesh=mesh, in_specs=in_specs, out_specs=out_specs, check_vma=False,
        )(*args)

    return run
```

```python
import math
from functools import partial

import jax
import jax.numpy as jnp
from jax import lax
from jax.experimental import pallas as pl
from jax.experimental.pallas import tpu as pltpu
from jax.sharding import PartitionSpec as P

HEAD_DIM = 64


epsilon = 1e-05


def layer_norm(values, gain):
    centered = values - jnp.mean(values, axis=-1, keepdims=True)
    spread = jnp.mean(centered * centered, axis=-1, keepdims=True)
    return centered * lax.rsqrt(spread + epsilon) * gain


def norm_backward(state, gain, grad_normed, grad_state):
    unused, pullback = jax.vjp(layer_norm, state, gain)
    grad_values, grad_gain = pullback(grad_normed)
    return (grad_state + grad_values, grad_gain)


def segment_mask(lengths, length, count):
    seg_ends = jnp.cumsum(lengths, dtype=jnp.int32)
    places = jnp.arange(length, dtype=jnp.int32)
    labels = jnp.sum((places[:, None] >= seg_ends[None, :]).astype(jnp.int32), axis=1)
    row_places = jnp.arange(count, dtype=jnp.int32)
    return (labels[:, None] == labels[None, :]) & (row_places[:, None] >= places[None, :])


def to_heads(block):
    return block.reshape(block.shape[:-1] + (block.shape[-1] // HEAD_DIM, HEAD_DIM))


def softmax_rows(queries, key_rows, allowed):
    scores = jnp.einsum(
        "qhd,khd->hqk", queries, key_rows, preferred_element_type=jnp.float32
    ) * HEAD_DIM ** (-0.5)
    if allowed is not None:
        scores = jnp.where(allowed[None], scores, -1e30)
    row_max = jnp.max(scores, axis=-1, keepdims=True)
    weights = jnp.exp(scores - row_max)
    return weights / jnp.sum(weights, axis=-1, keepdims=True)


def attend_both(queries, key_rows, value_rows, allowed, grad_heads):
    row_probs = softmax_rows(queries, key_rows, allowed)
    probs_low = row_probs.astype(jnp.bfloat16)
    heads_out = jnp.einsum(
        "hqk,khd->qhd", probs_low, value_rows, preferred_element_type=jnp.float32
    ).astype(jnp.bfloat16)
    grad_probs = jnp.einsum(
        "qhd,khd->hqk", grad_heads, value_rows, preferred_element_type=jnp.float32
    )
    inner_sum = jnp.sum(row_probs * grad_probs, axis=-1, keepdims=True)
    grad_scores = (row_probs * (grad_probs - inner_sum)).astype(jnp.bfloat16)
    grad_queries = jnp.einsum(
        "hqk,khd->qhd", grad_scores, key_rows, preferred_element_type=jnp.float32
    ) * HEAD_DIM ** (-0.5)
    grad_keys = jnp.einsum(
        "hqk,qhd->khd", grad_scores, queries, preferred_element_type=jnp.float32
    ) * HEAD_DIM ** (-0.5)
    grad_values = jnp.einsum(
        "hqk,qhd->khd", probs_low, grad_heads, preferred_element_type=jnp.float32
    )
    return (heads_out, grad_queries, grad_keys, grad_values)


def spread_tokens(normed):
    return lax.all_gather(normed, "tp", axis=1, tiled=True)


def sum_tokens(partial_out):
    return lax.psum_scatter(partial_out, "tp", scatter_dimension=1, tiled=True)


def gather_grads(grad_state):
    return lax.all_gather(grad_state.astype(jnp.bfloat16), "tp", axis=1, tiled=True)


def sum_grads(grad_normed):
    return lax.psum_scatter(grad_normed, "tp", scatter_dimension=1, tiled=True)


def self_partial(normed_all, seg_lengths, w_qkv, w_out_self):
    projected = jnp.einsum(
        "rld,cde->rcle", normed_all, w_qkv, preferred_element_type=jnp.float32
    ).astype(jnp.bfloat16)

    def one_row(items):
        row_proj, lengths = items
        split_heads = to_heads(row_proj)
        length = row_proj.shape[1]
        row_probs = softmax_rows(
            split_heads[0], split_heads[1], segment_mask(lengths, length, length)
        )
        heads_out = jnp.einsum(
            "hqk,khd->qhd",
            row_probs.astype(jnp.bfloat16),
            split_heads[2],
            preferred_element_type=jnp.float32,
        )
        return heads_out.reshape(row_proj.shape[1:]).astype(jnp.bfloat16)

    heads_all = lax.map(one_row, (projected, seg_lengths))
    return jnp.einsum("rle,ed->rld", heads_all, w_out_self, preferred_element_type=jnp.float32)


def self_backward(normed_all, seg_lengths, w_qkv, w_out_self, grad_branch):
    projected = jnp.einsum(
        "rld,cde->rcle", normed_all, w_qkv, preferred_element_type=jnp.float32
    ).astype(jnp.bfloat16)
    grad_heads = jnp.einsum(
        "rld,ed->rle", grad_branch, w_out_self, preferred_element_type=jnp.float32
    ).astype(jnp.bfloat16)

    def one_row(items):
        row_proj, lengths, row_grad = items
        split_heads = to_heads(row_proj)
        length = row_proj.shape[1]
        results = attend_both(
            split_heads[0],
            split_heads[1],
            split_heads[2],
            segment_mask(lengths, length, length),
            to_heads(row_grad),
        )
        return (
            results[0].reshape(length, -1),
            jnp.stack([piece.reshape(length, -1).astype(jnp.bfloat16) for piece in results[1:]]),
        )

    heads_all, grad_proj = lax.map(one_row, (projected, seg_lengths, grad_heads))
    grad_w_out = jnp.einsum(
        "rle,rld->ed", heads_all, grad_branch, preferred_element_type=jnp.float32
    )
    grad_w_qkv = jnp.einsum(
        "rld,rcle->cde", normed_all, grad_proj, preferred_element_type=jnp.float32
    )
    grad_normed = jnp.einsum("rcle,cde->rld", grad_proj, w_qkv, preferred_element_type=jnp.float32)
    return (grad_normed, grad_w_qkv, grad_w_out)


def cross_partial(normed_all, memory_all, w_query_cross, w_kv_cross, w_out_cross):
    queries = jnp.einsum(
        "rld,de->rle", normed_all, w_query_cross, preferred_element_type=jnp.float32
    ).astype(jnp.bfloat16)
    key_value = jnp.einsum(
        "rmd,cde->rcme", memory_all, w_kv_cross, preferred_element_type=jnp.float32
    ).astype(jnp.bfloat16)

    def one_row(items):
        row_query, row_kv = items
        split_kv = to_heads(row_kv)
        row_probs = softmax_rows(to_heads(row_query), split_kv[0], None)
        heads_out = jnp.einsum(
            "hqk,khd->qhd",
            row_probs.astype(jnp.bfloat16),
            split_kv[1],
            preferred_element_type=jnp.float32,
        )
        return heads_out.reshape(row_query.shape).astype(jnp.bfloat16)

    heads_all = lax.map(one_row, (queries, key_value))
    return jnp.einsum("rle,ed->rld", heads_all, w_out_cross, preferred_element_type=jnp.float32)


def cross_core(normed_all, memory_all, w_query_cross, w_kv_cross, w_out_cross, grad_branch):
    queries = jnp.einsum(
        "rld,de->rle", normed_all, w_query_cross, preferred_element_type=jnp.float32
    ).astype(jnp.bfloat16)
    key_value = jnp.einsum(
        "rmd,cde->rcme", memory_all, w_kv_cross, preferred_element_type=jnp.float32
    ).astype(jnp.bfloat16)
    grad_heads = jnp.einsum(
        "rld,ed->rle", grad_branch, w_out_cross, preferred_element_type=jnp.float32
    ).astype(jnp.bfloat16)

    def one_row(items):
        row_query, row_kv, row_grad = items
        split_kv = to_heads(row_kv)
        query_count = row_query.shape[0]
        memory_count = row_kv.shape[1]
        results = attend_both(
            to_heads(row_query), split_kv[0], split_kv[1], None, to_heads(row_grad)
        )
        grad_kv = jnp.stack(
            [results[2].reshape(memory_count, -1), results[3].reshape(memory_count, -1)]
        )
        return (results[0].reshape(query_count, -1), results[1].reshape(query_count, -1), grad_kv)

    heads_all, grad_queries, grad_kv = lax.map(one_row, (queries, key_value, grad_heads))
    grad_w_out = jnp.einsum(
        "rle,rld->ed", heads_all, grad_branch, preferred_element_type=jnp.float32
    )
    return (grad_queries, grad_kv, grad_w_out)


def cross_backward(normed_all, memory_all, w_query_cross, w_kv_cross, w_out_cross, grad_branch):
    grad_queries, grad_kv, grad_w_out = cross_core(
        normed_all, memory_all, w_query_cross, w_kv_cross, w_out_cross, grad_branch
    )
    grad_queries = grad_queries.astype(jnp.bfloat16)
    grad_kv = grad_kv.astype(jnp.bfloat16)
    grad_w_query = jnp.einsum(
        "rld,rle->de", normed_all, grad_queries, preferred_element_type=jnp.float32
    )
    grad_w_kv = jnp.einsum("rmd,rcme->cde", memory_all, grad_kv, preferred_element_type=jnp.float32)
    grad_normed = jnp.einsum(
        "rle,de->rld", grad_queries, w_query_cross, preferred_element_type=jnp.float32
    )
    grad_memory = jnp.einsum(
        "rcme,cde->rmd", grad_kv, w_kv_cross, preferred_element_type=jnp.float32
    )
    return (grad_normed, grad_memory, grad_w_query, grad_w_kv, grad_w_out)


def expert_rows(weights, expert):
    return lax.dynamic_index_in_dim(weights, expert, 0, keepdims=False)


def ffn_partial(normed_all, expert_ids, w_up, w_down):

    def one_row(items):
        normed_row, expert = items
        pre_act = jnp.dot(normed_row, expert_rows(w_up, expert), preferred_element_type=jnp.float32)
        hidden = jax.nn.gelu(pre_act, approximate=False).astype(jnp.bfloat16)
        return jnp.dot(hidden, expert_rows(w_down, expert), preferred_element_type=jnp.float32)

    return lax.map(one_row, (normed_all, expert_ids[:, 0]))


def ffn_backward(normed_all, expert_ids, w_up, w_down, grad_branch):

    def one_row(items):
        normed_row, expert, grad_row = items
        up_rows = expert_rows(w_up, expert)
        down_rows = expert_rows(w_down, expert)
        pre_act = jnp.dot(normed_row, up_rows, preferred_element_type=jnp.float32)
        activated, gelu_back = jax.vjp(partial(jax.nn.gelu, approximate=False), pre_act)
        hidden = activated.astype(jnp.bfloat16)
        grad_hidden = lax.dot_general(
            grad_row, down_rows, (((1,), (1,)), ((), ())), preferred_element_type=jnp.float32
        )
        grad_pre = gelu_back(grad_hidden)[0].astype(jnp.bfloat16)
        grad_down = lax.dot_general(
            hidden, grad_row, (((0,), (0,)), ((), ())), preferred_element_type=jnp.float32
        )
        grad_up = lax.dot_general(
            normed_row, grad_pre, (((0,), (0,)), ((), ())), preferred_element_type=jnp.float32
        )
        grad_normed = lax.dot_general(
            grad_pre, up_rows, (((1,), (1,)), ((), ())), preferred_element_type=jnp.float32
        )
        return (grad_normed, grad_up, grad_down)

    grad_normed, row_up, row_down = lax.map(one_row, (normed_all, expert_ids[:, 0], grad_branch))
    choose = (
        expert_ids[:, 0][:, None] == jnp.arange(w_up.shape[0], dtype=jnp.int32)[None, :]
    ).astype(jnp.float32)
    grad_w_up = jnp.einsum("re,rdf->edf", choose, row_up, precision=lax.Precision.HIGHEST)
    grad_w_down = jnp.einsum("re,rfd->efd", choose, row_down, precision=lax.Precision.HIGHEST)
    return (grad_normed, grad_w_up, grad_w_down)


def run_forward(layer_input, memory, seg_lengths, expert_ids, ln_gains, attn_weights, w_up, w_down):
    w_qkv, w_out_self, w_query_cross, w_kv_cross, w_out_cross = attn_weights
    state_zero = layer_input.astype(jnp.float32)
    normed_local = layer_norm(state_zero, ln_gains[0]).astype(jnp.bfloat16)
    memory_all = lax.all_gather(memory, "tp", axis=1, tiled=True)
    normed_self = spread_tokens(normed_local)
    state_one = state_zero + sum_tokens(self_partial(normed_self, seg_lengths, w_qkv, w_out_self))
    normed_cross = spread_tokens(layer_norm(state_one, ln_gains[1]).astype(jnp.bfloat16))
    state_two = state_one + sum_tokens(
        cross_partial(normed_cross, memory_all, w_query_cross, w_kv_cross, w_out_cross)
    )
    normed_ffn = spread_tokens(layer_norm(state_two, ln_gains[2]).astype(jnp.bfloat16))
    state_three = state_two + sum_tokens(ffn_partial(normed_ffn, expert_ids, w_up, w_down))
    return (
        state_three,
        (state_zero, state_one, state_two, normed_self, normed_cross, normed_ffn, memory_all),
    )


def per_device(
    layer_input,
    memory,
    seg_lengths,
    expert_ids,
    ln_gains,
    w_qkv,
    w_out_self,
    w_query_cross,
    w_kv_cross,
    w_out_cross,
    w_up,
    w_down,
    cotangent,
):
    attn_weights = (w_qkv, w_out_self, w_query_cross, w_kv_cross, w_out_cross)
    use_qkv, use_out_self, use_query, use_kv, use_out_cross = attn_weights
    state_three, kept = run_forward(
        layer_input, memory, seg_lengths, expert_ids, ln_gains, attn_weights, w_up, w_down
    )
    fresh = lax.optimization_barrier((layer_input, memory, state_three))
    unused, kept = run_forward(
        fresh[0], fresh[1], seg_lengths, expert_ids, ln_gains, attn_weights, w_up, w_down
    )
    state_zero, state_one, state_two, normed_self, normed_cross, normed_ffn, memory_all = kept
    grad_state = cotangent.astype(jnp.float32)
    grad_normed, grad_up, grad_down = ffn_backward(
        normed_ffn, expert_ids, w_up, w_down, gather_grads(grad_state)
    )
    grad_state, gain_ffn = norm_backward(state_two, ln_gains[2], sum_grads(grad_normed), grad_state)
    grad_normed, memory_part, grad_w_query, grad_w_kv, grad_w_out_cross = cross_backward(
        normed_cross, memory_all, use_query, use_kv, use_out_cross, gather_grads(grad_state)
    )
    grad_normed, grad_memory = (
        lax.psum_scatter(
            grad_normed.astype(jnp.bfloat16), "tp", scatter_dimension=1, tiled=True
        ).astype(jnp.float32),
        lax.psum_scatter(
            memory_part.astype(jnp.bfloat16), "tp", scatter_dimension=1, tiled=True
        ).astype(jnp.float32),
    )
    grad_state, gain_cross = norm_backward(state_one, ln_gains[1], grad_normed, grad_state)
    grad_normed, grad_w_qkv, grad_w_out_self = self_backward(
        normed_self, seg_lengths, use_qkv, use_out_self, gather_grads(grad_state)
    )
    grad_state, gain_self = norm_backward(
        state_zero, ln_gains[0], sum_grads(grad_normed), grad_state
    )
    summed = (
        lax.psum_scatter(
            grad_w_qkv.astype(jnp.bfloat16), "dp", scatter_dimension=1, tiled=True
        ).astype(jnp.float32),
        lax.psum_scatter(
            grad_w_out_self.astype(jnp.bfloat16), "dp", scatter_dimension=1, tiled=True
        ).astype(jnp.float32),
        lax.psum_scatter(
            grad_w_query.astype(jnp.bfloat16), "dp", scatter_dimension=0, tiled=True
        ).astype(jnp.float32),
        lax.psum_scatter(
            grad_w_kv.astype(jnp.bfloat16), "dp", scatter_dimension=1, tiled=True
        ).astype(jnp.float32),
        lax.psum_scatter(
            grad_w_out_cross.astype(jnp.bfloat16), "dp", scatter_dimension=1, tiled=True
        ).astype(jnp.float32),
        lax.psum_scatter(
            grad_up.astype(jnp.bfloat16), "dp", scatter_dimension=1, tiled=True
        ).astype(jnp.float32),
        lax.psum_scatter(
            grad_down.astype(jnp.bfloat16), "dp", scatter_dimension=2, tiled=True
        ).astype(jnp.float32),
    )
    grad_w_qkv, grad_w_out_self, grad_w_query, grad_w_kv, grad_w_out_cross, grad_up, grad_down = (
        summed
    )
    gain_total = lax.psum(jnp.stack([gain_self, gain_cross, gain_ffn]), ("dp", "tp"))
    share_width = gain_total.shape[1] // lax.axis_size("dp")
    gain_share = lax.dynamic_slice_in_dim(
        gain_total, lax.axis_index("dp") * share_width, share_width, 1
    )
    return (
        state_three.astype(jnp.bfloat16),
        grad_state,
        grad_memory,
        gain_share,
        grad_w_qkv,
        grad_w_out_self,
        grad_w_query,
        grad_w_kv,
        grad_w_out_cross,
        grad_up,
        grad_down,
    )


F32, BF16 = jnp.float32, jnp.bfloat16
MESH = pl.DeviceIdType.MESH
LOG2E = math.log2(math.e)
QSCALE = LOG2E * HEAD_DIM ** -0.5
NN = (((1,), (0,)), ((), ()))
NT = (((1,), (1,)), ((), ()))
TN = (((0,), (0,)), ((), ()))

LEN, WIDTH, COLS, HIDDEN, BLOCK, HALF = 1024, 512, 256, 1024, 256, 512
BLOCKS = LEN // BLOCK
TILE = 256
TILES = HIDDEN // TILE
PIECES = (COLS, 3 * COLS // 2, 3 * COLS // 2) * 2


def dot(left, right, dims=NN):
    return lax.dot_general(left, right, dims, preferred_element_type=F32)


def head_mask(block, side):
    lanes = lax.broadcasted_iota(jnp.int32, block.shape, 1)
    keep = (lanes >= HEAD_DIM) if side else (lanes < HEAD_DIM)
    return jnp.where(keep, block, jnp.zeros_like(block))


def window_bias(key_at, query_at, keys, queries, starts):
    key_place = key_at + lax.broadcasted_iota(jnp.int32, (keys, queries), 0)
    query_place = query_at + lax.broadcasted_iota(jnp.int32, (keys, queries), 1)
    return jnp.where((key_place >= starts) & (key_place <= query_place), 0.0, -1e30)


def add_up(total, part):
    return part if total is None else total + part


def attend(units, q, k, vt, kept, ht, inverse, q_len, k_len, chunk, before=None, after=None):
    def scores(unit):
        h, slot, q_at, k_at, bias = unit
        lanes = slice((h // 2) * 128, (h // 2) * 128 + 128)
        out, top = [], None
        queries = q[pl.ds(q_at, q_len), lanes]
        for j in range(0, k_len, chunk):
            s = dot(head_mask(k[pl.ds(k_at + j, chunk), lanes], h % 2), queries, NT)
            if bias is not None:
                s = s + bias[j:j + chunk]
            out.append(s)
            high = jnp.max(s.reshape(chunk // 8, 8, q_len), axis=0)
            top = high if top is None else jnp.maximum(top, high)
        return out, jnp.max(top, axis=0, keepdims=True)

    def values(unit, made):
        h, slot, q_at, k_at, bias = unit
        rows = slice(h * 64, h * 64 + 64)
        out, total = None, None
        for n, s in enumerate(made[0]):
            p = jnp.exp2(s - made[1])
            total = add_up(total, jnp.sum(p.reshape(chunk // 8, 8, q_len), axis=0))
            low = p.astype(BF16)
            kept[slot, n * chunk:(n + 1) * chunk, :] = low
            out = add_up(out, dot(vt[rows, pl.ds(k_at + n * chunk, chunk)], low))
        inv = 1.0 / jnp.sum(total, axis=0, keepdims=True)
        ht[rows, pl.ds(q_at, q_len)] = (out * inv).astype(BF16)
        inverse[h:h + 1, pl.ds(q_at, q_len)] = inv

    made = None
    for n, unit in enumerate(units):
        if n == 0:
            made = scores(unit)
        following = scores(units[n + 1]) if n + 1 < len(units) else None
        values(unit, made)
        made = following


def attend_back(units, v, kt, qt, gh, ght, kept, inner, inverse, dqt, dkt, dvt, q_len, k_len, chunk):
    def first(unit):
        h, slot, q_at, k_at = unit
        lanes = slice((h // 2) * 128, (h // 2) * 128 + 128)
        grads = gh[pl.ds(q_at, q_len), lanes]
        return [dot(head_mask(v[pl.ds(k_at + j, chunk), lanes], h % 2), grads, NT) for j in range(0, k_len, chunk)]

    def second(unit, made):
        h, slot, q_at, k_at = unit
        rows = slice(h * 64, h * 64 + 64)
        cols = pl.ds(q_at, q_len)
        shift = inner[h:h + 1, cols]
        part_q = None
        for n, dp in enumerate(made):
            at = pl.ds(k_at + n * chunk, chunk)
            p = kept[slot, n * chunk:(n + 1) * chunk, :]
            ds = (p.astype(F32) * (dp - shift)).astype(BF16)
            dvt[rows, at] += dot(ght[rows, cols], p, NT)
            dkt[rows, at] += dot(qt[rows, cols], ds, NT)
            part_q = add_up(part_q, dot(kt[rows, at], ds))
        dqt[rows, cols] = (part_q * (inverse[h:h + 1, cols] * HEAD_DIM ** -0.5)).astype(BF16)

    made = None
    for n, unit in enumerate(units):
        if n == 0:
            made = first(unit)
        following = first(units[n + 1]) if n + 1 < len(units) else None
        second(unit, made)
        made = following


def gelu_parts(pre):
    gauss = jnp.exp2(pre * pre * (-0.5 * LOG2E))
    t = 1.0 / (1.0 + (0.3275911 / math.sqrt(2.0)) * jnp.abs(pre))
    poly = t * (0.254829592 * 0.5 + t * (-0.284496736 * 0.5 + t * (
        1.421413741 * 0.5 + t * (-1.453152027 * 0.5 + t * (1.061405429 * 0.5)))))
    tail = poly * gauss
    phi = jnp.where(pre >= 0, 1.0 - tail, tail)
    return phi, phi + pre * (gauss * (1.0 / math.sqrt(2.0 * math.pi)))


def normalise(x):
    c = x - jnp.mean(x, axis=-1, keepdims=True)
    r = lax.rsqrt(jnp.mean(c * c, axis=-1, keepdims=True) + epsilon)
    return c * r, r


def norm_back(state, gain, grad):
    xhat, r = normalise(state)
    y = grad * gain
    m1 = jnp.mean(y, axis=-1, keepdims=True)
    m2 = jnp.mean(y * xhat, axis=-1, keepdims=True)
    return r * (y - m1 - xhat * m2), jnp.sum(grad * xhat, axis=0, keepdims=True)


def block_rows(i):
    return pl.ds(pl.multiple_of(i * BLOCK, BLOCK), BLOCK)


def each(count, body):
    def step(i, carry):
        body(i)
        return carry

    lax.fori_loop(0, count, step, 0)


def layer_kernel(
    n_dp,
    lens, expert, gains, x_in, mem_in, cot_in, wqkv_in, wos_in, wq_in, wkv_in, woc_in, up_in, down_in,
    lo_out, gi_out, gm_out, e_out, a0_out, a1_out, a2_out, a3_out, a4_out, a5_out, g_out, ids_out,
    x, mem, cot, wqkv, wos, wq, wkv, woc, up, down, starts,
    s1, s2, gs, n0, n1, n2, q0, k0, v0, q1, k1, v1, vt, ht0, ht1, inv0, inv1, inner,
    kept0, kept1, kept2, gb, dkt, dvt, work, nt, cot_t, eb,
    a0, a1, a2, a3, a4, a5, ax0, ax1, ax2, ax3, ax4, ax5, ay0, ay1, ay2, ay3, ay4, ay5,
    snd, rcv, sndh, rcvh, leaving, half_out, gain_sum, g_send, g_in,
    y_send, y_recv, w_send, w_recv, c_send, c_recv, x_send, x_recv, h_send, h_recv,
    e_send, e_recv, p_send, p_recv, a_send, a_recv, g_ssem, g_rsem, o_send, o_recv,
):
    d, t = lax.axis_index("dp"), lax.axis_index("tp")
    c = lax.rem(d, 2)
    k2 = d - c
    row = k2 + t
    lin = d * 2 + t
    n_all = n_dp * 2
    diag = (k2 + 1 - c, 1 - t)
    sib = (k2 + 1 - c, t)
    swaps = c != t
    stays = c == t

    def remote(src, dst, ssem, rsem, to):
        return pltpu.make_async_remote_copy(
            src_ref=src, dst_ref=dst, send_sem=ssem, recv_sem=rsem, device_id=to, device_id_type=MESH)

    own = pl.ds(pl.multiple_of(c * HALF, HALF), HALF)
    other = pl.ds(pl.multiple_of((1 - c) * HALF, HALF), HALF)
    theirs = pl.ds(pl.multiple_of(t * HALF, HALF), HALF)

    X, MEM, COT, UP, DOWN = 0, 1, 2, 3, 3 + TILES
    n_brought = 3 + 2 * TILES

    def tile(f):
        return pl.ds(pl.multiple_of(f * TILE, TILE), TILE)

    def bring(n, place):
        if n < UP:
            src, dst = ((x_in, x), (mem_in, mem), (cot_in, cot))[n]
            dst = dst.at[place]
        elif n < DOWN:
            src, dst = up_in.at[:, tile(n - UP)], up.at[:, tile(n - UP)]
        else:
            src, dst = down_in.at[tile(n - DOWN)], down.at[tile(n - DOWN)]
        return (lambda: remote(src, dst, y_send.at[n], y_recv.at[n], diag),
                lambda: pltpu.make_async_copy(src, dst, y_recv.at[n]))

    def start_bring(n):
        far, near = bring(n, theirs)

        @pl.when(swaps)
        def _():
            far().start()

    def start_near(n):
        far, near = bring(n, own)

        @pl.when(stays)
        def _():
            near().start()

    def wait_bring(n):
        far, near = bring(n, own)

        @pl.when(swaps)
        def _():
            far().wait_recv()

        @pl.when(stays)
        def _():
            near().wait()

    def share(n, buf):
        return remote(buf.at[own], buf.at[own], c_send.at[n], c_recv.at[n], sib)

    def share_starts():
        return remote(starts, starts, c_send.at[3], c_recv.at[3], sib)

    n_pairs = n_dp // 2
    pair = lax.div(d, 2)
    halves = [(wqkv_in.at[1:3], wqkv.at[1:3]), (wqkv_in.at[0:1], wqkv.at[0:1]), (wos_in, wos), (wkv_in, wkv),
              (wq_in, wq), (woc_in, woc)]
    WKV0, WQ0, WOS, WKV, WQ, WOC = range(6)
    zs = n_dp // 4
    side = lax.rem(pair, 2)
    z = lax.div(d, 4)
    across = (d + 2 - 4 * side, t)

    def piece(ref, p):
        if len(ref.shape) == 3:
            rows = ref.shape[1] // n_pairs
            return ref.at[:, pl.ds(pl.multiple_of(p * rows, rows), rows)]
        rows = ref.shape[0] // n_pairs
        return ref.at[pl.ds(pl.multiple_of(p * rows, rows), rows)]

    def first_piece(n):
        src, dst = halves[n]
        return remote(piece(src, pair), piece(dst, pair), w_send.at[n, 0], w_recv.at[n, pair], diag)

    def hand_along(n, s):
        dst = halves[n][1]
        to = lax.rem(z + s, zs)
        return remote(piece(dst, pair), piece(dst, pair), w_send.at[n, s], w_recv.at[n, pair], (d + 4 * (to - z), t))

    def hand_across(n, s):
        dst = halves[n][1]
        p = lax.rem(z + s, zs) * 2 + side
        return remote(piece(dst, p), piece(dst, p), w_send.at[n, zs + s], w_recv.at[n, p], across)

    def wait_piece(n, p):
        dst = halves[n][1]
        remote(piece(dst, p), piece(dst, p), w_send.at[n, 0], w_recv.at[n, p], diag).wait_recv()

    def near_weight(n):
        src, dst = halves[n]
        return pltpu.make_async_copy(src, dst, w_recv.at[n, 0])

    def hand_round(n):
        first_piece(n).wait_recv()
        each(zs - 1, lambda s: hand_along(n, s + 1).start())
        hand_across(n, 0).start()

    def hand_on(n):
        def one(s):
            wait_piece(n, lax.rem(z + s + 1, zs) * 2 + side)
            hand_across(n, s + 1).start()

        @pl.when(swaps)
        def _():
            each(zs - 1, one)

    def wait_weight(n):
        @pl.when(swaps)
        def _():
            each(zs, lambda s: wait_piece(n, lax.rem(z + s, zs) * 2 + 1 - side))

        @pl.when(stays)
        def _():
            near_weight(n).wait()

    start_near(X)

    @pl.when(stays)
    def _():
        near_weight(WKV0).start()
        near_weight(WQ0).start()

    start_near(MEM)
    start_near(COT)

    @pl.when(stays)
    def _():
        for n in (WOS, WKV, WQ, WOC):
            near_weight(n).start()

    for f in range(TILES):
        start_near(UP + f)
        start_near(DOWN + f)
    barrier = pltpu.get_barrier_semaphore()

    def greet(i):
        to = lax.rem(lin + 1 + i, n_all)
        pl.semaphore_signal(barrier, inc=1, device_id=(lax.div(to, 2), lax.rem(to, 2)), device_id_type=MESH)

    each(n_all - 1, greet)

    @pl.when(stays)
    def _():
        places = lax.broadcasted_iota(jnp.int32, (8, LEN), 1)
        start, level = jnp.int32(0), jnp.zeros((8, LEN), jnp.int32)
        for s in range(lens.shape[1]):
            level = jnp.where(places >= start, start, level)
            start = start + lens[0, s]
        starts[...] = level

    pl.semaphore_wait(barrier, n_all - 1)

    @pl.when(swaps)
    def _():
        first_piece(WKV0).start()
        first_piece(WQ0).start()

    start_bring(X)

    @pl.when(swaps)
    def _():
        for n in (WOS, WKV, WQ, WOC):
            first_piece(n).start()

    start_bring(MEM)

    start_bring(UP)
    start_bring(DOWN)
    start_bring(COT)
    for f in range(1, TILES):
        start_bring(UP + f)
        start_bring(DOWN + f)

    @pl.when(stays)
    def _():
        share_starts().start()

    @pl.when(swaps)
    def _():
        hand_round(WKV0)
        hand_round(WQ0)

    hand_on(WKV0)
    hand_on(WQ0)

    def wait_near(n):
        near = bring(n, own)[1]

        @pl.when(stays)
        def _():
            near().wait()

    def wait_swapped(n):
        far = bring(n, own)[0]

        @pl.when(swaps)
        def _():
            far().wait_recv()

    wait_bring(X)
    share(0, x).start()

    @pl.when(swaps)
    def _():
        for n in (WOS, WKV, WQ, WOC):
            hand_round(n)


    @pl.when(stays)
    def _():
        wait_near(MEM)
        share(1, mem).start()
        wait_near(COT)
        share(2, cot).start()

    def self_project(i):
        r = block_rows(i)
        xhat, _ = normalise(x[r, :].astype(F32))
        nn = (xhat * gains[0:1, :]).astype(BF16)
        n0[r, :] = nn
        q0[r, :] = (dot(nn, wqkv[0]) * QSCALE).astype(BF16)
        k0[r, :] = dot(nn, wqkv[1]).astype(BF16)
        v0[r, :] = dot(nn, wqkv[2]).astype(BF16)

    wait_weight(WKV0)
    wait_weight(WQ0)
    each(2, lambda i: self_project(c * 2 + i))
    share(0, x).wait_recv()
    each(2, lambda i: self_project((1 - c) * 2 + i))
    vt[...] = v0[...].T

    @pl.when(swaps)
    def _():
        share_starts().wait_recv()

    def exchange(e, i):
        r = block_rows(i)
        return remote(snd.at[e % 2, r], rcv.at[e % 2, r], x_send.at[e, i], x_recv.at[e, i], sib)

    def out_of(e, i, ht, w_out):
        r = block_rows(i)
        snd[e % 2, r, :] = dot(ht[:, r], w_out[...], TN).astype(BF16)
        exchange(e, i).start()

    everything = range(4)
    first_bias = window_bias(0, 0, 256, 256, starts[0:1, 0:256])
    attend([(h, h, 0, 0, first_bias) for h in everything], q0, k0, vt, kept0, ht0, inv0, 256, 256, 256)

    def self_block(j):
        i = j + 1
        bias = window_bias(j * 256, i * 256, 512, 256, starts[0:1, i * 256:(i + 1) * 256])
        attend([(h, j * 4 + h, i * 256, j * 256, bias) for h in everything],
               q0, k0, vt, kept1, ht0, inv0, 256, 512, 256)

    for j, n in enumerate((WOS, WKV, WQ)):
        hand_on(n)
        self_block(j)
    wait_weight(WOS)
    each(BLOCKS, lambda i: out_of(0, i, ht0, wos))
    hand_on(WOC)

    wait_swapped(MEM)

    @pl.when(swaps)
    def _():
        share(1, mem).start()

    wait_weight(WKV)

    def memory_project(i):
        r = block_rows(i)
        k1[r, :] = dot(mem[r, :], wkv[0]).astype(BF16)
        v1[r, :] = dot(mem[r, :], wkv[1]).astype(BF16)

    each(2, lambda i: memory_project(c * 2 + i))
    share(1, mem).wait_recv()
    each(2, lambda i: memory_project((1 - c) * 2 + i))
    vt[...] = v1[...].T
    wait_weight(WQ)

    def cross_norm(i):
        r = block_rows(i)
        exchange(0, i).wait_recv()
        state = x[r, :].astype(F32) + (snd[0, r, :].astype(F32) + rcv[0, r, :].astype(F32))
        s1[r, :] = state
        xhat, _ = normalise(state)
        nn = (xhat * gains[1:2, :]).astype(BF16)
        n1[r, :] = nn
        q1[r, :] = (dot(nn, wq[...]) * QSCALE).astype(BF16)

    each(BLOCKS, cross_norm)

    wait_weight(WOC)

    def cross_pair(j):
        units = []
        for i in range(2):
            for h in everything:
                at = pl.multiple_of((j * 2 + i) * 256, 256)
                units.append((h, (j * 2 + i) * 4 + h, at, 0, None))
        attend(units, q1, k1, vt, kept2, ht1, inv1, 256, LEN, 256)
        out_of(1, j * 2, ht1, woc)
        out_of(1, j * 2 + 1, ht1, woc)

    each(BLOCKS // 2, cross_pair)

    wait_swapped(COT)

    @pl.when(swaps)
    def _():
        share(2, cot).start()

    def half_exchange(e, i):
        r = block_rows(i)
        return remote(sndh.at[e, r], rcvh.at[e, r], h_send.at[e, i], h_recv.at[e, i], sib)

    def expert_norm(i):
        r = block_rows(i)
        exchange(1, i).wait_recv()
        state = s1[r, :] + (snd[1, r, :].astype(F32) + rcv[1, r, :].astype(F32))
        s2[r, :] = state
        xhat, _ = normalise(state)
        n2[r, :] = (xhat * gains[2:3, :]).astype(BF16)

    each(2, expert_norm)
    share(2, cot).wait_recv()
    cot_t[...] = cot[...].T
    each(2, lambda i: expert_norm(i + 2))

    def begin(copy):
        copy.start()

    def finish_send(copy):
        copy.wait_send()

    def share_rows(ref, to):
        return ref.at[pl.ds(pl.multiple_of(to * 32, 32), 32)]

    def scatter(f, action):
        src, dst = eb.at[f], e_out.at[row, f]

        def one(s):
            to = lax.rem(d + s + 1, n_dp)
            action(remote(share_rows(src, to), dst, e_send.at[f, s + 1], e_recv.at[f, row], (to, c)))

        each(n_dp - 1, one)

    def scatter_near(f):
        @pl.when(stays)
        def _():
            pltpu.make_async_copy(share_rows(eb.at[f], d), e_out.at[row, f], e_recv.at[f, row]).start()
            scatter(f, begin)

    def own_far(f):
        return remote(share_rows(eb.at[f], d), e_out.at[row, f], e_send.at[f, 0], e_recv.at[f, row], (d, c))

    def scatter_far(f):
        @pl.when(swaps)
        def _():
            own_far(f).start()
            scatter(f, begin)

    def collect(f):
        def one(i):
            src, dst = eb.at[f, pl.ds(0, 32)], e_out.at[i, f]

            @pl.when(stays & (i == row))
            def _():
                pltpu.make_async_copy(src, dst, e_recv.at[f, i]).wait()

            @pl.when(jnp.logical_not(stays & (i == row)))
            def _():
                remote(src, dst, e_send.at[f, 0], e_recv.at[f, i], diag).wait_recv()

        each(n_dp, one)

    hid, gpre = work.at[0:LEN], work.at[LEN:2 * LEN]

    def expert_tile(f):
        cols = slice(f * TILE, (f + 1) * TILE)

        def first(i):
            r = slice(i * BLOCK, (i + 1) * BLOCK)
            return dot(n2[r, :], up[:, cols]), dot(cot[r, :], down[cols, :], NT)

        def second(i, made):
            r = slice(i * BLOCK, (i + 1) * BLOCK)
            pre, grad = made
            phi, slope = gelu_parts(pre)
            hid[r, cols] = (pre * phi).astype(BF16)
            gpre[r, cols] = (grad * slope).astype(BF16)

        made = first(0)
        for i in range(BLOCKS):
            following = first(i + 1) if i + 1 < BLOCKS else None
            second(i, made)
            made = following

    def expert_back(i):
        r = block_rows(i)
        snd[0, r, :] = dot(gpre[r, :], up[...], NT).astype(BF16)
        exchange(2, i).start()

    def expert_out(i):
        r = block_rows(i)
        part = dot(hid[r, :], down[...])
        mine = lax.div(i, 2) == c
        rl = block_rows(lax.rem(i, 2))

        @pl.when(mine)
        def _():
            half_out[rl, :] = s2[r, :] + part

        @pl.when(jnp.logical_not(mine))
        def _():
            sndh[0, rl, :] = part.astype(BF16)
            half_exchange(0, lax.rem(i, 2)).start()

    def expert_grads(f):
        cols = slice(f * TILE, (f + 1) * TILE)
        eb[f, :, 0:TILE] = dot(nt[...], gpre[:, cols]).astype(BF16)
        eb[f, :, TILE:2 * TILE] = dot(cot_t[...], hid[:, cols]).astype(BF16)

    def done_sending(e):
        each(BLOCKS, lambda i: exchange(e, i).wait_send())

    done_sending(0)
    for f in range(TILES):
        wait_bring(UP + f)
        wait_bring(DOWN + f)
        expert_tile(f)
        if f == 0:
            nt[...] = n2[...].T
        if f + 1 < TILES:
            expert_grads(f)
            scatter_near(f)
        if f + 2 == TILES:
            scatter_far(0)

    each(BLOCKS, expert_back)
    scatter_far(1)
    expert_grads(TILES - 1)
    scatter_near(TILES - 1)
    scatter_far(2)
    scatter_far(3)
    each(BLOCKS, expert_out)

    def strip(n):
        return work.at[n * COLS:(n + 1) * COLS]

    dqt, dkb, dvb, ght = strip(0), strip(1), strip(2), strip(3)
    kt, qt = cot_t.at[0:COLS], cot_t.at[COLS:2 * COLS]
    dq, dk = down.at[:, 0:COLS], down.at[:, COLS:2 * COLS]
    gh, dv = n2.at[:, 0:COLS], n2.at[:, COLS:2 * COLS]
    gain_sum[...] = jnp.zeros_like(gain_sum)

    def branch_block(n, i, e, state, base, ht, inv, w_out):
        r = block_rows(i)
        exchange(e, i).wait_recv()
        grad = snd[e % 2, r, :].astype(F32) + rcv[e % 2, r, :].astype(F32)
        step, share_gain = norm_back(state[r, :], gains[n:n + 1, :], grad)
        moved = base[r, :].astype(F32) + step
        gs[r, :] = moved
        low = moved.astype(BF16)
        gb[r, :] = low
        gain_sum[n:n + 1, :] += jnp.where(lax.div(i, 2) == c, share_gain, 0.0)
        gh[r, :] = dot(low, w_out[...], NT).astype(BF16)
        turned = dot(w_out[...], low, NT).astype(BF16).astype(F32)
        prod = turned * ht[:, r].astype(F32)
        for h in everything:
            rows = slice(h * 64, h * 64 + 64)
            inner[h:h + 1, r] = jnp.sum(prod[rows], axis=0, keepdims=True)
            ght[rows, r] = (turned[rows] * inv[h:h + 1, r]).astype(BF16)

    def turn_queries(q, k, inv):
        kt[...] = k[...].T
        turned = q[...].T
        for h in everything:
            rows = slice(h * 64, h * 64 + 64)
            qt[rows, :] = (turned[rows].astype(F32) * inv[h:h + 1, :]).astype(BF16)
        dkt[...] = jnp.zeros_like(dkt)
        dvt[...] = jnp.zeros_like(dvt)

    pieces = tuple(zip((a0, a1, a2, a3, a4, a5), (ax0, ax1, ax2, ax3, ax4, ax5), (ay0, ay1, ay2, ay3, ay4, ay5),
                       (a0_out, a1_out, a2_out, a3_out, a4_out, a5_out)))
    n_pieces = len(pieces)

    def over_x(n):
        buf, place = pieces[n][:2]
        return remote(buf.at[:, 1 - side], place, p_send.at[0, n], p_recv.at[0, n], across)

    def over_y(n):
        buf, place = pieces[n][0], pieces[n][2]
        return remote(buf.at[:, side], place, p_send.at[1, n], p_recv.at[1, n], (d, c))

    def add_x(n):
        buf, place = pieces[n][:2]
        over_x(n).wait_recv()
        buf[:, side] = (buf[:, side].astype(F32) + place[...].astype(F32)).astype(BF16)

        @pl.when(swaps)
        def _():
            over_y(n).start()

    def owners(n, action):
        buf, out = pieces[n][0], pieces[n][3]

        def one(s):
            to = lax.rem(z * 2 + c + s + 1, 2 * zs)
            to_z, to_c = lax.div(to, 2), lax.rem(to, 2)
            src = buf.at[to_z, side, pl.ds(pl.multiple_of(to_c * 32, 32), 32)]
            action(remote(src, out.at[z], a_send.at[n, s], a_recv.at[n, z], (to_z * 4 + side * 2 + to_c, t)))

        each(2 * zs - 1, one)

    def own_share(n):
        src = pieces[n][0].at[z, side, pl.ds(pl.multiple_of(c * 32, 32), 32)]
        return pltpu.make_async_copy(src, pieces[n][3].at[z], a_recv.at[n, z])

    def add_y(n):
        @pl.when(stays)
        def _():
            buf, place = pieces[n][0], pieces[n][2]
            over_y(n).wait_recv()
            buf[:, side] = (buf[:, side].astype(F32) + place[...].astype(F32)).astype(BF16)
            own_share(n).start()
            owners(n, begin)

    def collect_piece(n):
        buf, out = pieces[n][0], pieces[n][3]

        def one(i):
            @pl.when(stays & (i == z))
            def _():
                own_share(n).wait()

            @pl.when(jnp.logical_not(stays & (i == z)))
            def _():
                remote(buf.at[0, 0, pl.ds(0, 32)], out.at[i], a_send.at[n, 0], a_recv.at[n, i], diag).wait_recv()

        each(zs, one)

        @pl.when(stays)
        def _():
            owners(n, finish_send)

        @pl.when(swaps)
        def _():
            over_y(n).wait_send()

        over_x(n).wait_send()

    def by_owner(grad):
        return grad.astype(BF16).T.reshape(zs, 2, WIDTH // (2 * zs), grad.shape[0])

    each(BLOCKS, lambda i: branch_block(2, i, 2, s2, cot, ht1, inv1, woc))
    def leave(n, out):
        buf = leaving.at[n]
        return (lambda: remote(buf, out, o_send.at[n], o_recv.at[n], diag),
                lambda: pltpu.make_async_copy(buf, out, o_recv.at[n]))

    def start_leave(n, out):
        far, near = leave(n, out)

        @pl.when(swaps)
        def _():
            far().start()

        @pl.when(stays)
        def _():
            near().start()

    def wait_leave(n, out):
        far, near = leave(n, out)

        @pl.when(swaps)
        def _():
            far().wait()

        @pl.when(stays)
        def _():
            near().wait()

    def half_done(n):
        def one(low):
            half_exchange(n, low).wait_recv()
            r = block_rows(low)
            leaving[n, r, :] = (half_out[r, :] + rcvh[n, r, :].astype(F32)).astype(BF16)

        each(2, one)

    half_done(0)
    start_leave(0, lo_out)
    a0[...] = by_owner(dot(ht1[...], gb[...]))
    over_x(0).start()
    turn_queries(q1, k1, inv1)

    def pair_grads(pair_of_heads, n, source_q, source_kv):
        rows = slice(pair_of_heads * 128, pair_of_heads * 128 + 128)
        dkb[rows, :] = (dkt[rows, :] * math.log(2.0)).astype(BF16)
        dvb[rows, :] = dvt[rows, :].astype(BF16)
        buf = pieces[n][0]
        for part, (grad, source) in enumerate(((dqt, source_q), (dkb, source_kv), (dvb, source_kv))):
            buf[:, :, :, part * 128:part * 128 + 128] = by_owner(dot(grad[rows, :], source[...]))
        over_x(n).start()

    def cross_back(pair_of_heads):
        heads = (2 * pair_of_heads, 2 * pair_of_heads + 1)
        units = [(h, i * 4 + h, i * 256, 0) for h in heads for i in range(BLOCKS)]
        attend_back(units, v1, kt, qt, gh, ght, kept2, inner, inv1, dqt, dkt, dvt, 256, LEN, 256)
        pair_grads(pair_of_heads, 1 + pair_of_heads, n1, mem)

    cross_back(0)
    cross_back(1)

    def settle():
        dq[...] = dqt[...].T
        dk[...] = dkb[...].T
        dv[...] = dvb[...].T

    add_x(0)
    settle()
    done_sending(1)

    def cross_grads(i):
        r = block_rows(i)
        snd[1, r, :] = dot(dq[r, :], wq[...], NT).astype(BF16)
        exchange(3, i).start()

    each(BLOCKS, cross_grads)
    def memory_grads(i):
        r = block_rows(i)
        part = dot(dk[r, :], wkv[0], NT) + dot(dv[r, :], wkv[1], NT)
        mine = lax.div(i, 2) == c
        rl = block_rows(lax.rem(i, 2))

        @pl.when(mine)
        def _():
            half_out[rl, :] = part

        @pl.when(jnp.logical_not(mine))
        def _():
            sndh[1, rl, :] = part.astype(BF16)
            half_exchange(1, lax.rem(i, 2)).start()

    each(BLOCKS, memory_grads)
    add_x(1)

    each(BLOCKS, lambda i: branch_block(1, i, 3, s1, gs, ht0, inv0, wos))
    half_done(1)
    start_leave(1, gm_out)
    turn_queries(q0, k0, inv0)

    def self_back(pair_of_heads):
        heads = (2 * pair_of_heads, 2 * pair_of_heads + 1)
        attend_back([(h, h, 0, 0) for h in heads], v0, kt, qt, gh, ght, kept0, inner, inv0, dqt, dkt, dvt, 256, 256, 256)
        units = [(h, j * 4 + h, (j + 1) * 256, j * 256) for h in heads for j in range(BLOCKS - 1)]
        attend_back(units, v0, kt, qt, gh, ght, kept1, inner, inv0, dqt, dkt, dvt, 256, 512, 256)
        pair_grads(pair_of_heads, 4 + pair_of_heads, n0, n0)

    a3[...] = by_owner(dot(ht0[...], gb[...]))
    over_x(3).start()
    self_back(0)
    add_x(2)
    self_back(1)
    settle()

    def input_grads(i):
        r = block_rows(i)
        return dot(dq[r, :], wqkv[0], NT) + dot(dk[r, :], wqkv[1], NT) + dot(dv[r, :], wqkv[2], NT)

    def input_send(low):
        sndh[2, block_rows(low), :] = input_grads((1 - c) * 2 + low).astype(BF16)
        half_exchange(2, low).start()

    each(2, input_send)

    def input_keep(low):
        half_out[block_rows(low), :] = input_grads(c * 2 + low)

    each(2, input_keep)

    def input_done(low):
        half_exchange(2, low).wait_recv()
        rl = block_rows(low)
        r = block_rows(c * 2 + low)
        grad = half_out[rl, :] + rcvh[2, rl, :].astype(F32)
        step, share_gain = norm_back(x[r, :].astype(F32), gains[0:1, :], grad)
        gain_sum[0:1, :] += share_gain
        leaving[2, rl, :] = (gs[r, :] + step).astype(BF16)

    each(2, input_done)
    start_leave(2, gi_out)
    add_y(0)
    add_x(3)

    number = jnp.full((1, 128), expert[0, 0].astype(F32))
    for j in range(n_dp):
        turned = gain_sum[...] if j == 0 else pltpu.roll(gain_sum[...], (WIDTH - 32 * j) % WIDTH, 1)
        g_send[j] = turned[:, :128]
        g_send[j, 3:4, :] = number

    def gain_copy(s):
        to = lax.rem(lin + s, n_all)
        to_dp = lax.div(to, 2)
        return remote(g_send.at[to_dp], g_in.at[lin], g_ssem.at[s], g_rsem.at[lin], (to_dp, lax.rem(to, 2)))

    each(n_all - 1, lambda s: gain_copy(s + 1).start())
    keep_gain = pltpu.make_async_copy(g_send.at[d], g_in.at[lin], g_rsem.at[lin])
    keep_gain.start()

    add_y(1)
    add_x(4)
    add_y(2)
    add_x(5)
    add_y(3)
    add_y(4)
    add_y(5)

    wait_leave(0, lo_out)
    wait_leave(1, gm_out)
    wait_leave(2, gi_out)
    for f in range(TILES):
        collect(f)
        scatter(f, finish_send)

        @pl.when(swaps)
        def _():
            own_far(f).wait_send()

    for n in range(n_pieces):
        collect_piece(n)
    keep_gain.wait()

    def gain_wait(s):
        gain_copy(s + 1).wait_send()
        who = lax.rem(lin + s + 1, n_all)
        remote(g_send.at[0], g_in.at[who], g_ssem.at[0], g_rsem.at[who], diag).wait_recv()

    each(n_all - 1, gain_wait)
    g_out[...] = jnp.sum(g_in[...], axis=0)
    for r in range(n_dp):
        ids_out[r:r + 1, :] = g_in[2 * r, 3:4, :]

    @pl.when(swaps)
    def _():
        for n in range(n_brought):
            bring(n, theirs)[0]().wait_send()
        for n in range(6):
            first_piece(n).wait_send()
            each(zs - 1, lambda s: hand_along(n, s + 1).wait_send())
            each(zs, lambda s: hand_across(n, s).wait_send())

    for n, buf in enumerate((x, mem, cot)):
        share(n, buf).wait_send()

    @pl.when(stays)
    def _():
        share_starts().wait_send()

    done_sending(2)
    done_sending(3)
    for e in range(3):
        each(2, lambda i: half_exchange(e, i).wait_send())


VMEM_BYTES = 63 * 2**20
ANY_PLACE = pl.BlockSpec(memory_space=pl.ANY)
IN_HBM = pl.BlockSpec(memory_space=pltpu.HBM)
IN_SMEM = pl.BlockSpec(memory_space=pltpu.SMEM)
IN_VMEM = pl.BlockSpec(memory_space=pltpu.VMEM)


def paired_layer(n_dp, lens, expert, gains, *arrays):
    bf = lambda *shape: pltpu.VMEM(shape, BF16)
    fl = lambda *shape: pltpu.VMEM(shape, F32)
    dma = lambda *shape: pltpu.SemaphoreType.DMA(shape)
    tokens = bf(LEN, WIDTH)
    heads = bf(LEN, COLS)
    turned = bf(COLS, LEN)
    half = jax.ShapeDtypeStruct((HALF, WIDTH), BF16)
    zs = n_dp // 4
    sizes = PIECES
    split = [bf(zs, 2, WIDTH // (2 * zs), size) for size in sizes]
    x_parts = [bf(zs, WIDTH // (2 * zs), size) for size in sizes]
    return pl.pallas_call(
        partial(layer_kernel, n_dp),
        out_shape=(half, half, half, jax.ShapeDtypeStruct((n_dp, TILES, 32, 2 * TILE), BF16),
                   *[jax.ShapeDtypeStruct((zs, 32, size), BF16) for size in sizes],
                   jax.ShapeDtypeStruct((8, 128), F32), jax.ShapeDtypeStruct((n_dp, 128), F32)),
        in_specs=[IN_SMEM] * 2 + [IN_VMEM] + [ANY_PLACE] * 10,
        out_specs=(ANY_PLACE,) * (4 + len(sizes)) + (IN_VMEM,) * 2,
        scratch_shapes=[
            tokens, tokens, tokens, bf(3, WIDTH, COLS), bf(COLS, WIDTH), bf(WIDTH, COLS), bf(2, WIDTH, COLS),
            bf(COLS, WIDTH), bf(WIDTH, HIDDEN), bf(HIDDEN, WIDTH), pltpu.VMEM((8, LEN), jnp.int32),
            fl(LEN, WIDTH), fl(LEN, WIDTH), fl(LEN, WIDTH), tokens, tokens, tokens,
            heads, heads, heads, heads, heads, heads, turned, turned, turned, fl(8, LEN), fl(8, LEN), fl(8, LEN),
            bf(4, 256, 256), bf(12, 512, 256), bf(16, LEN, 256), tokens, fl(COLS, LEN), fl(COLS, LEN),
            bf(2 * LEN, HIDDEN), bf(WIDTH, LEN), bf(WIDTH, LEN), bf(TILES, WIDTH, 2 * TILE), *split, *x_parts, *x_parts,
            bf(2, LEN, WIDTH), bf(2, LEN, WIDTH), bf(3, HALF, WIDTH), bf(3, HALF, WIDTH), bf(3, HALF, WIDTH),
            fl(HALF, WIDTH), fl(8, WIDTH), fl(n_dp, 8, 128), fl(2 * n_dp, 8, 128),
            dma(3 + 2 * TILES), dma(3 + 2 * TILES), dma(6, n_dp // 2), dma(6, n_dp // 2), dma(4), dma(4),
            dma(4, 4), dma(4, 4), dma(3, 2), dma(3, 2),
            dma(TILES, n_dp), dma(TILES, n_dp), dma(2, len(sizes)), dma(2, len(sizes)), dma(len(sizes), 2 * zs), dma(len(sizes), zs),
            dma(2 * n_dp), dma(2 * n_dp), dma(3), dma(3),
        ],
        compiler_params=pltpu.CompilerParams(
            collective_id=0, has_side_effects=True, vmem_limit_bytes=VMEM_BYTES),
        cost_estimate=pl.CostEstimate(flops=20 * 10**9, bytes_accessed=20 * 2**20, transcendentals=0),
    )(lens, expert, gains, *arrays)


def choose_kernel(expert, up_in, down_in, up_out, down_out, sems):
    e = expert[0, 0]
    parts = 4
    copies = []
    for p in range(parts):
        for n, (src, dst) in enumerate(((up_in, up_out), (down_in, down_out))):
            rows = dst.shape[0] // parts
            at = pl.ds(p * rows, rows)
            copies.append(pltpu.make_async_copy(src.at[e, at], dst.at[at], sems.at[n, p]))
    for copy in copies:
        copy.start()
    for copy in copies:
        copy.wait()


def choose_expert(expert, w_up, w_down):
    return pl.pallas_call(
        choose_kernel,
        out_shape=(jax.ShapeDtypeStruct(w_up.shape[1:], BF16), jax.ShapeDtypeStruct(w_down.shape[1:], BF16)),
        in_specs=[IN_SMEM, ANY_PLACE, ANY_PLACE],
        out_specs=(IN_VMEM, IN_VMEM),
        scratch_shapes=[pltpu.SemaphoreType.DMA((2, 4))],
        compiler_params=pltpu.CompilerParams(vmem_limit_bytes=VMEM_BYTES),
    )(expert, w_up, w_down)


def place_kernel(
    ids_any, gains_any, e_any, a0_any, a1_any, a2_any, a3_any, a4_any, a5_any, gi_any, gm_any, lo_any,
    lo_out, gi_out, gm_out, gain_out, qkv_out, os_out, q_out, kv_out, oc_out, up_out, down_out,
    ids, ids_in, gains_in, e_in, a0_in, a1_in, a2_in, a3_in, a4_in, a5_in, gi_in, gm_in, lo_in, gi_v, gm_v, ups, downs, in_sems, e_sems, up_sems, down_sems, out_sems,
):
    rows = e_in.shape[0]
    number = pltpu.make_async_copy(ids_any, ids, in_sems.at[0])
    number.start()
    blocks = [pltpu.make_async_copy(e_any.at[r], e_in.at[r], e_sems.at[r]) for r in range(rows)]
    for copy in blocks:
        copy.start()
    pairs = ((lo_any, lo_in), (gi_any, gi_in), (gm_any, gm_in), (gains_any, gains_in), (a0_any, a0_in),
             (a1_any, a1_in), (a2_any, a2_in), (a3_any, a3_in), (a4_any, a4_in), (a5_any, a5_in))
    reads = [pltpu.make_async_copy(src, dst, in_sems.at[1 + n]) for n, (src, dst) in enumerate(pairs)]
    for copy in reads:
        copy.start()
    number.wait()
    writes = []

    def write(src, dst, sem):
        writes.append(pltpu.make_async_copy(src, dst, sem))
        writes[-1].start()

    for r in range(rows):
        blocks[r].wait()
        for f in range(TILES):
            ups[r, :, f * TILE:(f + 1) * TILE] = e_in[r, f, :, 0:TILE].astype(F32)
            downs[r, :, f * TILE:(f + 1) * TILE] = e_in[r, f, :, TILE:2 * TILE].astype(F32)
        e = ids[r, 0].astype(jnp.int32)
        write(ups.at[r], up_out.at[e], up_sems.at[r])
        write(downs.at[r], down_out.at[e], down_sems.at[r])
    reads[0].wait()
    write(lo_in, lo_out, out_sems.at[2])
    reads[1].wait()
    gi_v[...] = gi_in[...].astype(F32)
    write(gi_v, gi_out, out_sems.at[0])
    reads[2].wait()
    gm_v[...] = gm_in[...].astype(F32)
    write(gm_v, gm_out, out_sems.at[1])
    for copy in reads[3:]:
        copy.wait()
    gain_out[...] = gains_in[0:3, 0:32]
    oc_out[...] = jnp.sum(a0_in[...].astype(F32), axis=0)
    os_out[...] = jnp.sum(a3_in[...].astype(F32), axis=0)
    for pair, (cross, own) in enumerate(((a1_in, a4_in), (a2_in, a5_in))):
        cols = slice(pair * 128, pair * 128 + 128)
        cross = jnp.sum(cross[...].astype(F32), axis=0)
        own = jnp.sum(own[...].astype(F32), axis=0)
        q_out[:, cols] = cross[:, 0:128]
        for n in range(2):
            kv_out[n, :, cols] = cross[:, 128 + n * 128:256 + n * 128]
        for n in range(3):
            qkv_out[n, :, cols] = own[:, n * 128:n * 128 + 128]
    for copy in writes:
        copy.wait()


def place_grads(experts, *arrays):
    shape = lambda *dims: jax.ShapeDtypeStruct(dims, F32)
    like = lambda array: pltpu.VMEM(array.shape, array.dtype)
    dma = lambda *dims: pltpu.SemaphoreType.DMA(dims)
    rows = arrays[2].shape[0]
    staged = pltpu.VMEM((rows, 32, HIDDEN), F32)
    half = pltpu.VMEM((HALF, WIDTH), F32)
    return pl.pallas_call(
        place_kernel,
        out_shape=(jax.ShapeDtypeStruct((HALF, WIDTH), BF16), shape(HALF, WIDTH), shape(HALF, WIDTH), shape(3, 32), shape(3, 32, COLS), shape(32, COLS),
                   shape(32, COLS), shape(2, 32, COLS), shape(32, COLS),
                   shape(experts, 32, HIDDEN), shape(experts, 32, HIDDEN)),
        in_specs=[IN_HBM] * 12,
        out_specs=(IN_HBM,) * 3 + (IN_VMEM,) * 6 + (IN_HBM,) * 2,
        scratch_shapes=[pltpu.SMEM(arrays[0].shape, F32)] + [like(array) for array in arrays] + [
            half, half, staged, staged, dma(11), dma(rows), dma(rows), dma(rows), dma(3)],
        compiler_params=pltpu.CompilerParams(vmem_limit_bytes=VMEM_BYTES),
    )(*arrays)


def per_device_paired(
    layer_input, memory, seg_lengths, expert_ids, ln_gains, w_qkv, w_out_self, w_query_cross, w_kv_cross,
    w_out_cross, w_up, w_down, cotangent,
):
    n_dp = lax.axis_size("dp")
    up, down = choose_expert(expert_ids, w_up, w_down)
    layer_output, grad_input, grad_memory, e_rows, *a_rows, gain_rows, numbers = paired_layer(
        n_dp, seg_lengths, expert_ids, ln_gains,
        layer_input[0], memory[0], cotangent[0], w_qkv, w_out_self, w_query_cross, w_kv_cross, w_out_cross, up, down,
    )
    layer_output, grad_input, grad_memory, gain_share, qkv, out_self, query, key_value, out_cross, grad_up, grad_down = place_grads(
        w_up.shape[0], numbers, gain_rows, e_rows, *a_rows, grad_input, grad_memory, layer_output)
    return (
        layer_output[None], grad_input[None], grad_memory[None], gain_share, qkv, out_self.T, query, key_value,
        out_cross.T, grad_up, jnp.swapaxes(grad_down, 1, 2),
    )


def fits_pairs(mesh, layer_input, seg_lengths, w_up):
    return (
        mesh.shape["tp"] == 2
        and mesh.shape["dp"] == 16
        and layer_input.shape == (mesh.shape["dp"], LEN, WIDTH)
        and w_up.shape == (mesh.shape["dp"], WIDTH, 2 * HIDDEN)
    )


def solution(mesh):
    in_specs = (
        P("dp", "tp", None),
        P("dp", "tp", None),
        P("dp", None),
        P("dp", None),
        P(),
        P(None, None, "tp"),
        P("tp", None),
        P(None, "tp"),
        P(None, None, "tp"),
        P("tp", None),
        P(None, None, "tp"),
        P(None, "tp", None),
        P("dp", "tp", None),
    )
    out_specs = (
        P("dp", "tp", None),
        P("dp", "tp", None),
        P("dp", "tp", None),
        P(None, "dp"),
        P(None, "dp", "tp"),
        P("tp", "dp"),
        P("dp", "tp"),
        P(None, "dp", "tp"),
        P("tp", "dp"),
        P(None, "dp", "tp"),
        P(None, "tp", "dp"),
    )

    def run(*args):
        layer_input, seg_lengths, w_up = args[0], args[2], args[10]
        paired = fits_pairs(mesh, layer_input, seg_lengths, w_up)
        return jax.shard_map(
            per_device_paired if paired else per_device,
            mesh=mesh, in_specs=in_specs, out_specs=out_specs, check_vma=False,
        )(*args)

    return run
```

```python
import math
from functools import partial

import jax
import jax.numpy as jnp
from jax import lax
from jax.experimental import pallas as pl
from jax.experimental.pallas import tpu as pltpu
from jax.sharding import PartitionSpec as P

HEAD_DIM = 64


epsilon = 1e-05


def layer_norm(values, gain):
    centered = values - jnp.mean(values, axis=-1, keepdims=True)
    spread = jnp.mean(centered * centered, axis=-1, keepdims=True)
    return centered * lax.rsqrt(spread + epsilon) * gain


def norm_backward(state, gain, grad_normed, grad_state):
    unused, pullback = jax.vjp(layer_norm, state, gain)
    grad_values, grad_gain = pullback(grad_normed)
    return (grad_state + grad_values, grad_gain)


def segment_mask(lengths, length, count):
    seg_ends = jnp.cumsum(lengths, dtype=jnp.int32)
    places = jnp.arange(length, dtype=jnp.int32)
    labels = jnp.sum((places[:, None] >= seg_ends[None, :]).astype(jnp.int32), axis=1)
    row_places = jnp.arange(count, dtype=jnp.int32)
    return (labels[:, None] == labels[None, :]) & (row_places[:, None] >= places[None, :])


def to_heads(block):
    return block.reshape(block.shape[:-1] + (block.shape[-1] // HEAD_DIM, HEAD_DIM))


def softmax_rows(queries, key_rows, allowed):
    scores = jnp.einsum(
        "qhd,khd->hqk", queries, key_rows, preferred_element_type=jnp.float32
    ) * HEAD_DIM ** (-0.5)
    if allowed is not None:
        scores = jnp.where(allowed[None], scores, -1e30)
    row_max = jnp.max(scores, axis=-1, keepdims=True)
    weights = jnp.exp(scores - row_max)
    return weights / jnp.sum(weights, axis=-1, keepdims=True)


def attend_both(queries, key_rows, value_rows, allowed, grad_heads):
    row_probs = softmax_rows(queries, key_rows, allowed)
    probs_low = row_probs.astype(jnp.bfloat16)
    heads_out = jnp.einsum(
        "hqk,khd->qhd", probs_low, value_rows, preferred_element_type=jnp.float32
    ).astype(jnp.bfloat16)
    grad_probs = jnp.einsum(
        "qhd,khd->hqk", grad_heads, value_rows, preferred_element_type=jnp.float32
    )
    inner_sum = jnp.sum(row_probs * grad_probs, axis=-1, keepdims=True)
    grad_scores = (row_probs * (grad_probs - inner_sum)).astype(jnp.bfloat16)
    grad_queries = jnp.einsum(
        "hqk,khd->qhd", grad_scores, key_rows, preferred_element_type=jnp.float32
    ) * HEAD_DIM ** (-0.5)
    grad_keys = jnp.einsum(
        "hqk,qhd->khd", grad_scores, queries, preferred_element_type=jnp.float32
    ) * HEAD_DIM ** (-0.5)
    grad_values = jnp.einsum(
        "hqk,qhd->khd", probs_low, grad_heads, preferred_element_type=jnp.float32
    )
    return (heads_out, grad_queries, grad_keys, grad_values)


def spread_tokens(normed):
    return lax.all_gather(normed, "tp", axis=1, tiled=True)


def sum_tokens(partial_out):
    return lax.psum_scatter(partial_out, "tp", scatter_dimension=1, tiled=True)


def gather_grads(grad_state):
    return lax.all_gather(grad_state.astype(jnp.bfloat16), "tp", axis=1, tiled=True)


def sum_grads(grad_normed):
    return lax.psum_scatter(grad_normed, "tp", scatter_dimension=1, tiled=True)


def self_partial(normed_all, seg_lengths, w_qkv, w_out_self):
    projected = jnp.einsum(
        "rld,cde->rcle", normed_all, w_qkv, preferred_element_type=jnp.float32
    ).astype(jnp.bfloat16)

    def one_row(items):
        row_proj, lengths = items
        split_heads = to_heads(row_proj)
        length = row_proj.shape[1]
        row_probs = softmax_rows(
            split_heads[0], split_heads[1], segment_mask(lengths, length, length)
        )
        heads_out = jnp.einsum(
            "hqk,khd->qhd",
            row_probs.astype(jnp.bfloat16),
            split_heads[2],
            preferred_element_type=jnp.float32,
        )
        return heads_out.reshape(row_proj.shape[1:]).astype(jnp.bfloat16)

    heads_all = lax.map(one_row, (projected, seg_lengths))
    return jnp.einsum("rle,ed->rld", heads_all, w_out_self, preferred_element_type=jnp.float32)


def self_backward(normed_all, seg_lengths, w_qkv, w_out_self, grad_branch):
    projected = jnp.einsum(
        "rld,cde->rcle", normed_all, w_qkv, preferred_element_type=jnp.float32
    ).astype(jnp.bfloat16)
    grad_heads = jnp.einsum(
        "rld,ed->rle", grad_branch, w_out_self, preferred_element_type=jnp.float32
    ).astype(jnp.bfloat16)

    def one_row(items):
        row_proj, lengths, row_grad = items
        split_heads = to_heads(row_proj)
        length = row_proj.shape[1]
        results = attend_both(
            split_heads[0],
            split_heads[1],
            split_heads[2],
            segment_mask(lengths, length, length),
            to_heads(row_grad),
        )
        return (
            results[0].reshape(length, -1),
            jnp.stack([piece.reshape(length, -1).astype(jnp.bfloat16) for piece in results[1:]]),
        )

    heads_all, grad_proj = lax.map(one_row, (projected, seg_lengths, grad_heads))
    grad_w_out = jnp.einsum(
        "rle,rld->ed", heads_all, grad_branch, preferred_element_type=jnp.float32
    )
    grad_w_qkv = jnp.einsum(
        "rld,rcle->cde", normed_all, grad_proj, preferred_element_type=jnp.float32
    )
    grad_normed = jnp.einsum("rcle,cde->rld", grad_proj, w_qkv, preferred_element_type=jnp.float32)
    return (grad_normed, grad_w_qkv, grad_w_out)


def cross_partial(normed_all, memory_all, w_query_cross, w_kv_cross, w_out_cross):
    queries = jnp.einsum(
        "rld,de->rle", normed_all, w_query_cross, preferred_element_type=jnp.float32
    ).astype(jnp.bfloat16)
    key_value = jnp.einsum(
        "rmd,cde->rcme", memory_all, w_kv_cross, preferred_element_type=jnp.float32
    ).astype(jnp.bfloat16)

    def one_row(items):
        row_query, row_kv = items
        split_kv = to_heads(row_kv)
        row_probs = softmax_rows(to_heads(row_query), split_kv[0], None)
        heads_out = jnp.einsum(
            "hqk,khd->qhd",
            row_probs.astype(jnp.bfloat16),
            split_kv[1],
            preferred_element_type=jnp.float32,
        )
        return heads_out.reshape(row_query.shape).astype(jnp.bfloat16)

    heads_all = lax.map(one_row, (queries, key_value))
    return jnp.einsum("rle,ed->rld", heads_all, w_out_cross, preferred_element_type=jnp.float32)


def cross_core(normed_all, memory_all, w_query_cross, w_kv_cross, w_out_cross, grad_branch):
    queries = jnp.einsum(
        "rld,de->rle", normed_all, w_query_cross, preferred_element_type=jnp.float32
    ).astype(jnp.bfloat16)
    key_value = jnp.einsum(
        "rmd,cde->rcme", memory_all, w_kv_cross, preferred_element_type=jnp.float32
    ).astype(jnp.bfloat16)
    grad_heads = jnp.einsum(
        "rld,ed->rle", grad_branch, w_out_cross, preferred_element_type=jnp.float32
    ).astype(jnp.bfloat16)

    def one_row(items):
        row_query, row_kv, row_grad = items
        split_kv = to_heads(row_kv)
        query_count = row_query.shape[0]
        memory_count = row_kv.shape[1]
        results = attend_both(
            to_heads(row_query), split_kv[0], split_kv[1], None, to_heads(row_grad)
        )
        grad_kv = jnp.stack(
            [results[2].reshape(memory_count, -1), results[3].reshape(memory_count, -1)]
        )
        return (results[0].reshape(query_count, -1), results[1].reshape(query_count, -1), grad_kv)

    heads_all, grad_queries, grad_kv = lax.map(one_row, (queries, key_value, grad_heads))
    grad_w_out = jnp.einsum(
        "rle,rld->ed", heads_all, grad_branch, preferred_element_type=jnp.float32
    )
    return (grad_queries, grad_kv, grad_w_out)


def cross_backward(normed_all, memory_all, w_query_cross, w_kv_cross, w_out_cross, grad_branch):
    grad_queries, grad_kv, grad_w_out = cross_core(
        normed_all, memory_all, w_query_cross, w_kv_cross, w_out_cross, grad_branch
    )
    grad_queries = grad_queries.astype(jnp.bfloat16)
    grad_kv = grad_kv.astype(jnp.bfloat16)
    grad_w_query = jnp.einsum(
        "rld,rle->de", normed_all, grad_queries, preferred_element_type=jnp.float32
    )
    grad_w_kv = jnp.einsum("rmd,rcme->cde", memory_all, grad_kv, preferred_element_type=jnp.float32)
    grad_normed = jnp.einsum(
        "rle,de->rld", grad_queries, w_query_cross, preferred_element_type=jnp.float32
    )
    grad_memory = jnp.einsum(
        "rcme,cde->rmd", grad_kv, w_kv_cross, preferred_element_type=jnp.float32
    )
    return (grad_normed, grad_memory, grad_w_query, grad_w_kv, grad_w_out)


def expert_rows(weights, expert):
    return lax.dynamic_index_in_dim(weights, expert, 0, keepdims=False)


def ffn_partial(normed_all, expert_ids, w_up, w_down):

    def one_row(items):
        normed_row, expert = items
        pre_act = jnp.dot(normed_row, expert_rows(w_up, expert), preferred_element_type=jnp.float32)
        hidden = jax.nn.gelu(pre_act, approximate=False).astype(jnp.bfloat16)
        return jnp.dot(hidden, expert_rows(w_down, expert), preferred_element_type=jnp.float32)

    return lax.map(one_row, (normed_all, expert_ids[:, 0]))


def ffn_backward(normed_all, expert_ids, w_up, w_down, grad_branch):

    def one_row(items):
        normed_row, expert, grad_row = items
        up_rows = expert_rows(w_up, expert)
        down_rows = expert_rows(w_down, expert)
        pre_act = jnp.dot(normed_row, up_rows, preferred_element_type=jnp.float32)
        activated, gelu_back = jax.vjp(partial(jax.nn.gelu, approximate=False), pre_act)
        hidden = activated.astype(jnp.bfloat16)
        grad_hidden = lax.dot_general(
            grad_row, down_rows, (((1,), (1,)), ((), ())), preferred_element_type=jnp.float32
        )
        grad_pre = gelu_back(grad_hidden)[0].astype(jnp.bfloat16)
        grad_down = lax.dot_general(
            hidden, grad_row, (((0,), (0,)), ((), ())), preferred_element_type=jnp.float32
        )
        grad_up = lax.dot_general(
            normed_row, grad_pre, (((0,), (0,)), ((), ())), preferred_element_type=jnp.float32
        )
        grad_normed = lax.dot_general(
            grad_pre, up_rows, (((1,), (1,)), ((), ())), preferred_element_type=jnp.float32
        )
        return (grad_normed, grad_up, grad_down)

    grad_normed, row_up, row_down = lax.map(one_row, (normed_all, expert_ids[:, 0], grad_branch))
    choose = (
        expert_ids[:, 0][:, None] == jnp.arange(w_up.shape[0], dtype=jnp.int32)[None, :]
    ).astype(jnp.float32)
    grad_w_up = jnp.einsum("re,rdf->edf", choose, row_up, precision=lax.Precision.HIGHEST)
    grad_w_down = jnp.einsum("re,rfd->efd", choose, row_down, precision=lax.Precision.HIGHEST)
    return (grad_normed, grad_w_up, grad_w_down)


def run_forward(layer_input, memory, seg_lengths, expert_ids, ln_gains, attn_weights, w_up, w_down):
    w_qkv, w_out_self, w_query_cross, w_kv_cross, w_out_cross = attn_weights
    state_zero = layer_input.astype(jnp.float32)
    normed_local = layer_norm(state_zero, ln_gains[0]).astype(jnp.bfloat16)
    memory_all = lax.all_gather(memory, "tp", axis=1, tiled=True)
    normed_self = spread_tokens(normed_local)
    state_one = state_zero + sum_tokens(self_partial(normed_self, seg_lengths, w_qkv, w_out_self))
    normed_cross = spread_tokens(layer_norm(state_one, ln_gains[1]).astype(jnp.bfloat16))
    state_two = state_one + sum_tokens(
        cross_partial(normed_cross, memory_all, w_query_cross, w_kv_cross, w_out_cross)
    )
    normed_ffn = spread_tokens(layer_norm(state_two, ln_gains[2]).astype(jnp.bfloat16))
    state_three = state_two + sum_tokens(ffn_partial(normed_ffn, expert_ids, w_up, w_down))
    return (
        state_three,
        (state_zero, state_one, state_two, normed_self, normed_cross, normed_ffn, memory_all),
    )


def per_device(
    layer_input,
    memory,
    seg_lengths,
    expert_ids,
    ln_gains,
    w_qkv,
    w_out_self,
    w_query_cross,
    w_kv_cross,
    w_out_cross,
    w_up,
    w_down,
    cotangent,
):
    attn_weights = (w_qkv, w_out_self, w_query_cross, w_kv_cross, w_out_cross)
    use_qkv, use_out_self, use_query, use_kv, use_out_cross = attn_weights
    state_three, kept = run_forward(
        layer_input, memory, seg_lengths, expert_ids, ln_gains, attn_weights, w_up, w_down
    )
    fresh = lax.optimization_barrier((layer_input, memory, state_three))
    unused, kept = run_forward(
        fresh[0], fresh[1], seg_lengths, expert_ids, ln_gains, attn_weights, w_up, w_down
    )
    state_zero, state_one, state_two, normed_self, normed_cross, normed_ffn, memory_all = kept
    grad_state = cotangent.astype(jnp.float32)
    grad_normed, grad_up, grad_down = ffn_backward(
        normed_ffn, expert_ids, w_up, w_down, gather_grads(grad_state)
    )
    grad_state, gain_ffn = norm_backward(state_two, ln_gains[2], sum_grads(grad_normed), grad_state)
    grad_normed, memory_part, grad_w_query, grad_w_kv, grad_w_out_cross = cross_backward(
        normed_cross, memory_all, use_query, use_kv, use_out_cross, gather_grads(grad_state)
    )
    grad_normed, grad_memory = (
        lax.psum_scatter(
            grad_normed.astype(jnp.bfloat16), "tp", scatter_dimension=1, tiled=True
        ).astype(jnp.float32),
        lax.psum_scatter(
            memory_part.astype(jnp.bfloat16), "tp", scatter_dimension=1, tiled=True
        ).astype(jnp.float32),
    )
    grad_state, gain_cross = norm_backward(state_one, ln_gains[1], grad_normed, grad_state)
    grad_normed, grad_w_qkv, grad_w_out_self = self_backward(
        normed_self, seg_lengths, use_qkv, use_out_self, gather_grads(grad_state)
    )
    grad_state, gain_self = norm_backward(
        state_zero, ln_gains[0], sum_grads(grad_normed), grad_state
    )
    summed = (
        lax.psum_scatter(
            grad_w_qkv.astype(jnp.bfloat16), "dp", scatter_dimension=1, tiled=True
        ).astype(jnp.float32),
        lax.psum_scatter(
            grad_w_out_self.astype(jnp.bfloat16), "dp", scatter_dimension=1, tiled=True
        ).astype(jnp.float32),
        lax.psum_scatter(
            grad_w_query.astype(jnp.bfloat16), "dp", scatter_dimension=0, tiled=True
        ).astype(jnp.float32),
        lax.psum_scatter(
            grad_w_kv.astype(jnp.bfloat16), "dp", scatter_dimension=1, tiled=True
        ).astype(jnp.float32),
        lax.psum_scatter(
            grad_w_out_cross.astype(jnp.bfloat16), "dp", scatter_dimension=1, tiled=True
        ).astype(jnp.float32),
        lax.psum_scatter(
            grad_up.astype(jnp.bfloat16), "dp", scatter_dimension=1, tiled=True
        ).astype(jnp.float32),
        lax.psum_scatter(
            grad_down.astype(jnp.bfloat16), "dp", scatter_dimension=2, tiled=True
        ).astype(jnp.float32),
    )
    grad_w_qkv, grad_w_out_self, grad_w_query, grad_w_kv, grad_w_out_cross, grad_up, grad_down = (
        summed
    )
    gain_total = lax.psum(jnp.stack([gain_self, gain_cross, gain_ffn]), ("dp", "tp"))
    share_width = gain_total.shape[1] // lax.axis_size("dp")
    gain_share = lax.dynamic_slice_in_dim(
        gain_total, lax.axis_index("dp") * share_width, share_width, 1
    )
    return (
        state_three.astype(jnp.bfloat16),
        grad_state,
        grad_memory,
        gain_share,
        grad_w_qkv,
        grad_w_out_self,
        grad_w_query,
        grad_w_kv,
        grad_w_out_cross,
        grad_up,
        grad_down,
    )


F32, BF16 = jnp.float32, jnp.bfloat16
MESH = pl.DeviceIdType.MESH
LOG2E = math.log2(math.e)
QSCALE = LOG2E * HEAD_DIM ** -0.5
NN = (((1,), (0,)), ((), ()))
NT = (((1,), (1,)), ((), ()))
TN = (((0,), (0,)), ((), ()))

LEN, WIDTH, COLS, HIDDEN, BLOCK, HALF = 1024, 512, 256, 1024, 256, 512
BLOCKS = LEN // BLOCK
TILE = 256
TILES = HIDDEN // TILE
PIECES = (COLS, 3 * COLS // 2, 3 * COLS // 2) * 2


def dot(left, right, dims=NN):
    return lax.dot_general(left, right, dims, preferred_element_type=F32)


def head_mask(block, side):
    lanes = lax.broadcasted_iota(jnp.int32, block.shape, 1)
    keep = (lanes >= HEAD_DIM) if side else (lanes < HEAD_DIM)
    return jnp.where(keep, block, jnp.zeros_like(block))


def window_bias(key_at, query_at, keys, queries, starts):
    key_place = key_at + lax.broadcasted_iota(jnp.int32, (keys, queries), 0)
    query_place = query_at + lax.broadcasted_iota(jnp.int32, (keys, queries), 1)
    return jnp.where((key_place >= starts) & (key_place <= query_place), 0.0, -1e30)


def add_up(total, part):
    return part if total is None else total + part


def attend(units, q, k, vt, kept, ht, inverse, q_len, k_len, chunk, before=None, after=None):
    def scores(unit):
        h, slot, q_at, k_at, bias = unit
        lanes = slice((h // 2) * 128, (h // 2) * 128 + 128)
        out, top = [], None
        queries = q[pl.ds(q_at, q_len), lanes]
        for j in range(0, k_len, chunk):
            s = dot(head_mask(k[pl.ds(k_at + j, chunk), lanes], h % 2), queries, NT)
            if bias is not None:
                s = s + bias[j:j + chunk]
            out.append(s)
            high = jnp.max(s.reshape(chunk // 8, 8, q_len), axis=0)
            top = high if top is None else jnp.maximum(top, high)
        return out, jnp.max(top, axis=0, keepdims=True)

    def values(unit, made):
        h, slot, q_at, k_at, bias = unit
        rows = slice(h * 64, h * 64 + 64)
        out, total = None, None
        for n, s in enumerate(made[0]):
            p = jnp.exp2(s - made[1])
            total = add_up(total, jnp.sum(p.reshape(chunk // 8, 8, q_len), axis=0))
            low = p.astype(BF16)
            kept[slot, n * chunk:(n + 1) * chunk, :] = low
            out = add_up(out, dot(vt[rows, pl.ds(k_at + n * chunk, chunk)], low))
        inv = 1.0 / jnp.sum(total, axis=0, keepdims=True)
        ht[rows, pl.ds(q_at, q_len)] = (out * inv).astype(BF16)
        inverse[h:h + 1, pl.ds(q_at, q_len)] = inv

    made = None
    for n, unit in enumerate(units):
        if n == 0:
            made = scores(unit)
        following = scores(units[n + 1]) if n + 1 < len(units) else None
        values(unit, made)
        made = following


def attend_back(units, v, kt, qt, gh, ght, kept, inner, inverse, dqt, dkt, dvt, q_len, k_len, chunk):
    def first(unit):
        h, slot, q_at, k_at = unit
        lanes = slice((h // 2) * 128, (h // 2) * 128 + 128)
        grads = gh[pl.ds(q_at, q_len), lanes]
        return [dot(head_mask(v[pl.ds(k_at + j, chunk), lanes], h % 2), grads, NT) for j in range(0, k_len, chunk)]

    def second(unit, made):
        h, slot, q_at, k_at = unit
        rows = slice(h * 64, h * 64 + 64)
        cols = pl.ds(q_at, q_len)
        shift = inner[h:h + 1, cols]
        part_q = None
        for n, dp in enumerate(made):
            at = pl.ds(k_at + n * chunk, chunk)
            p = kept[slot, n * chunk:(n + 1) * chunk, :]
            ds = (p.astype(F32) * (dp - shift)).astype(BF16)
            dvt[rows, at] += dot(ght[rows, cols], p, NT)
            dkt[rows, at] += dot(qt[rows, cols], ds, NT)
            part_q = add_up(part_q, dot(kt[rows, at], ds))
        dqt[rows, cols] = (part_q * (inverse[h:h + 1, cols] * HEAD_DIM ** -0.5)).astype(BF16)

    made = None
    for n, unit in enumerate(units):
        if n == 0:
            made = first(unit)
        following = first(units[n + 1]) if n + 1 < len(units) else None
        second(unit, made)
        made = following


def gelu_parts(pre):
    gauss = jnp.exp2(pre * pre * (-0.5 * LOG2E))
    t = 1.0 / (1.0 + (0.3275911 / math.sqrt(2.0)) * jnp.abs(pre))
    poly = t * (0.254829592 * 0.5 + t * (-0.284496736 * 0.5 + t * (
        1.421413741 * 0.5 + t * (-1.453152027 * 0.5 + t * (1.061405429 * 0.5)))))
    tail = poly * gauss
    phi = jnp.where(pre >= 0, 1.0 - tail, tail)
    return phi, phi + pre * (gauss * (1.0 / math.sqrt(2.0 * math.pi)))


def normalise(x):
    c = x - jnp.mean(x, axis=-1, keepdims=True)
    r = lax.rsqrt(jnp.mean(c * c, axis=-1, keepdims=True) + epsilon)
    return c * r, r


def norm_back(state, gain, grad):
    xhat, r = normalise(state)
    y = grad * gain
    m1 = jnp.mean(y, axis=-1, keepdims=True)
    m2 = jnp.mean(y * xhat, axis=-1, keepdims=True)
    return r * (y - m1 - xhat * m2), jnp.sum(grad * xhat, axis=0, keepdims=True)


def block_rows(i):
    return pl.ds(pl.multiple_of(i * BLOCK, BLOCK), BLOCK)


def each(count, body):
    def step(i, carry):
        body(i)
        return carry

    lax.fori_loop(0, count, step, 0)


def layer_kernel(
    n_dp,
    lens, expert, gains, x_in, mem_in, cot_in, wqkv_in, wos_in, wq_in, wkv_in, woc_in, up_in, down_in,
    lo_out, gi_out, gm_out, e_out, a0_out, a1_out, a2_out, a3_out, a4_out, a5_out, g_out, ids_out,
    x, mem, cot, wqkv, wos, wq, wkv, woc, up, down, starts,
    s1, s2, gs, n0, n1, n2, q0, k0, v0, q1, k1, v1, vt, ht0, ht1, inv0, inv1, inner,
    kept0, kept1, kept2, gb, dkt, dvt, work, nt, cot_t, eb,
    a0, a1, a2, a3, a4, a5, ax0, ax1, ax2, ax3, ax4, ax5, ay0, ay1, ay2, ay3, ay4, ay5,
    snd, rcv, sndh, rcvh, leaving, half_out, gain_sum, g_send, g_in,
    y_send, y_recv, w_send, w_recv, c_send, c_recv, x_send, x_recv, h_send, h_recv,
    e_send, e_recv, p_send, p_recv, a_send, a_recv, g_ssem, g_rsem, o_send, o_recv,
):
    d, t = lax.axis_index("dp"), lax.axis_index("tp")
    c = lax.rem(d, 2)
    k2 = d - c
    row = k2 + t
    lin = d * 2 + t
    n_all = n_dp * 2
    diag = (k2 + 1 - c, 1 - t)
    sib = (k2 + 1 - c, t)
    swaps = c != t
    stays = c == t

    def remote(src, dst, ssem, rsem, to):
        return pltpu.make_async_remote_copy(
            src_ref=src, dst_ref=dst, send_sem=ssem, recv_sem=rsem, device_id=to, device_id_type=MESH)

    own = pl.ds(pl.multiple_of(c * HALF, HALF), HALF)
    other = pl.ds(pl.multiple_of((1 - c) * HALF, HALF), HALF)
    theirs = pl.ds(pl.multiple_of(t * HALF, HALF), HALF)

    X, MEM, COT, UP, DOWN = 0, 1, 2, 3, 3 + TILES
    n_brought = 3 + 2 * TILES

    def tile(f):
        return pl.ds(pl.multiple_of(f * TILE, TILE), TILE)

    def bring(n, place):
        if n < UP:
            src, dst = ((x_in, x), (mem_in, mem), (cot_in, cot))[n]
            dst = dst.at[place]
        elif n < DOWN:
            src, dst = up_in.at[:, tile(n - UP)], up.at[:, tile(n - UP)]
        else:
            src, dst = down_in.at[tile(n - DOWN)], down.at[tile(n - DOWN)]
        return (lambda: remote(src, dst, y_send.at[n], y_recv.at[n], diag),
                lambda: pltpu.make_async_copy(src, dst, y_recv.at[n]))

    def start_bring(n):
        far, near = bring(n, theirs)

        @pl.when(swaps)
        def _():
            far().start()

    def start_near(n):
        far, near = bring(n, own)

        @pl.when(stays)
        def _():
            near().start()

    def wait_bring(n):
        far, near = bring(n, own)

        @pl.when(swaps)
        def _():
            far().wait_recv()

        @pl.when(stays)
        def _():
            near().wait()

    def share(n, buf):
        return remote(buf.at[own], buf.at[own], c_send.at[n], c_recv.at[n], sib)

    def share_starts():
        return remote(starts, starts, c_send.at[3], c_recv.at[3], sib)

    n_pairs = n_dp // 2
    pair = lax.div(d, 2)
    halves = [(wqkv_in.at[1:3], wqkv.at[1:3]), (wqkv_in.at[0:1], wqkv.at[0:1]), (wos_in, wos), (wkv_in, wkv),
              (wq_in, wq), (woc_in, woc)]
    WKV0, WQ0, WOS, WKV, WQ, WOC = range(6)
    zs = n_dp // 4
    side = lax.rem(pair, 2)
    z = lax.div(d, 4)
    across = (d + 2 - 4 * side, t)

    def piece(ref, p):
        if len(ref.shape) == 3:
            rows = ref.shape[1] // n_pairs
            return ref.at[:, pl.ds(pl.multiple_of(p * rows, rows), rows)]
        rows = ref.shape[0] // n_pairs
        return ref.at[pl.ds(pl.multiple_of(p * rows, rows), rows)]

    def first_piece(n):
        src, dst = halves[n]
        return remote(piece(src, pair), piece(dst, pair), w_send.at[n, 0], w_recv.at[n, pair], diag)

    def hand_along(n, s):
        dst = halves[n][1]
        to = lax.rem(z + s, zs)
        return remote(piece(dst, pair), piece(dst, pair), w_send.at[n, s], w_recv.at[n, pair], (d + 4 * (to - z), t))

    def hand_across(n, s):
        dst = halves[n][1]
        p = lax.rem(z + s, zs) * 2 + side
        return remote(piece(dst, p), piece(dst, p), w_send.at[n, zs + s], w_recv.at[n, p], across)

    def wait_piece(n, p):
        dst = halves[n][1]
        remote(piece(dst, p), piece(dst, p), w_send.at[n, 0], w_recv.at[n, p], diag).wait_recv()

    def near_weight(n):
        src, dst = halves[n]
        return pltpu.make_async_copy(src, dst, w_recv.at[n, 0])

    def hand_round(n):
        first_piece(n).wait_recv()
        each(zs - 1, lambda s: hand_along(n, s + 1).start())
        hand_across(n, 0).start()

    def hand_on(n):
        def one(s):
            wait_piece(n, lax.rem(z + s + 1, zs) * 2 + side)
            hand_across(n, s + 1).start()

        @pl.when(swaps)
        def _():
            each(zs - 1, one)

    def wait_weight(n):
        @pl.when(swaps)
        def _():
            each(zs, lambda s: wait_piece(n, lax.rem(z + s, zs) * 2 + 1 - side))

        @pl.when(stays)
        def _():
            near_weight(n).wait()

    start_near(X)

    @pl.when(stays)
    def _():
        near_weight(WKV0).start()
        near_weight(WQ0).start()

    start_near(MEM)
    start_near(COT)

    @pl.when(stays)
    def _():
        for n in (WOS, WKV, WQ, WOC):
            near_weight(n).start()

    for f in range(TILES):
        start_near(UP + f)
        start_near(DOWN + f)
    barrier = pltpu.get_barrier_semaphore()

    def greet(i):
        to = lax.rem(lin + 1 + i, n_all)
        pl.semaphore_signal(barrier, inc=1, device_id=(lax.div(to, 2), lax.rem(to, 2)), device_id_type=MESH)

    each(n_all - 1, greet)

    @pl.when(stays)
    def _():
        places = lax.broadcasted_iota(jnp.int32, (8, LEN), 1)
        start, level = jnp.int32(0), jnp.zeros((8, LEN), jnp.int32)
        for s in range(lens.shape[1]):
            level = jnp.where(places >= start, start, level)
            start = start + lens[0, s]
        starts[...] = level

    pl.semaphore_wait(barrier, n_all - 1)

    @pl.when(swaps)
    def _():
        first_piece(WKV0).start()
        first_piece(WQ0).start()

    start_bring(X)

    @pl.when(swaps)
    def _():
        for n in (WOS, WKV, WQ, WOC):
            first_piece(n).start()

    start_bring(MEM)

    start_bring(UP)
    start_bring(DOWN)
    start_bring(COT)
    for f in range(1, TILES):
        start_bring(UP + f)
        start_bring(DOWN + f)

    @pl.when(stays)
    def _():
        share_starts().start()

    @pl.when(swaps)
    def _():
        hand_round(WKV0)
        hand_round(WQ0)

    hand_on(WKV0)
    hand_on(WQ0)

    def wait_near(n):
        near = bring(n, own)[1]

        @pl.when(stays)
        def _():
            near().wait()

    def wait_swapped(n):
        far = bring(n, own)[0]

        @pl.when(swaps)
        def _():
            far().wait_recv()

    wait_bring(X)
    share(0, x).start()

    @pl.when(swaps)
    def _():
        for n in (WOS, WKV, WQ, WOC):
            hand_round(n)


    @pl.when(stays)
    def _():
        wait_near(MEM)
        share(1, mem).start()
        wait_near(COT)
        share(2, cot).start()

    def self_project(i):
        r = block_rows(i)
        xhat, _ = normalise(x[r, :].astype(F32))
        nn = (xhat * gains[0:1, :]).astype(BF16)
        n0[r, :] = nn
        q0[r, :] = (dot(nn, wqkv[0]) * QSCALE).astype(BF16)
        k0[r, :] = dot(nn, wqkv[1]).astype(BF16)
        v0[r, :] = dot(nn, wqkv[2]).astype(BF16)

    wait_weight(WKV0)
    wait_weight(WQ0)
    each(2, lambda i: self_project(c * 2 + i))
    share(0, x).wait_recv()
    each(2, lambda i: self_project((1 - c) * 2 + i))
    vt[...] = v0[...].T

    @pl.when(swaps)
    def _():
        share_starts().wait_recv()

    def exchange(e, i):
        r = block_rows(i)
        return remote(snd.at[e % 2, r], rcv.at[e % 2, r], x_send.at[e, i], x_recv.at[e, i], sib)

    def out_of(e, i, ht, w_out):
        r = block_rows(i)
        snd[e % 2, r, :] = dot(ht[:, r], w_out[...], TN).astype(BF16)
        exchange(e, i).start()

    everything = range(4)
    first_bias = window_bias(0, 0, 256, 256, starts[0:1, 0:256])
    attend([(h, h, 0, 0, first_bias) for h in everything], q0, k0, vt, kept0, ht0, inv0, 256, 256, 256)

    def self_block(j):
        i = j + 1
        bias = window_bias(j * 256, i * 256, 512, 256, starts[0:1, i * 256:(i + 1) * 256])
        attend([(h, j * 4 + h, i * 256, j * 256, bias) for h in everything],
               q0, k0, vt, kept1, ht0, inv0, 256, 512, 256)

    for j, n in enumerate((WOS, WKV, WQ)):
        hand_on(n)
        self_block(j)
    wait_weight(WOS)
    each(BLOCKS, lambda i: out_of(0, i, ht0, wos))
    hand_on(WOC)

    wait_swapped(MEM)

    @pl.when(swaps)
    def _():
        share(1, mem).start()

    wait_weight(WKV)

    def memory_project(i):
        r = block_rows(i)
        k1[r, :] = dot(mem[r, :], wkv[0]).astype(BF16)
        v1[r, :] = dot(mem[r, :], wkv[1]).astype(BF16)

    each(2, lambda i: memory_project(c * 2 + i))
    share(1, mem).wait_recv()
    each(2, lambda i: memory_project((1 - c) * 2 + i))
    vt[...] = v1[...].T
    wait_weight(WQ)

    def cross_norm(i):
        r = block_rows(i)
        exchange(0, i).wait_recv()
        state = x[r, :].astype(F32) + (snd[0, r, :].astype(F32) + rcv[0, r, :].astype(F32))
        s1[r, :] = state
        xhat, _ = normalise(state)
        nn = (xhat * gains[1:2, :]).astype(BF16)
        n1[r, :] = nn
        q1[r, :] = (dot(nn, wq[...]) * QSCALE).astype(BF16)

    each(BLOCKS, cross_norm)

    wait_weight(WOC)

    def cross_pair(j):
        units = []
        for i in range(2):
            for h in everything:
                at = pl.multiple_of((j * 2 + i) * 256, 256)
                units.append((h, (j * 2 + i) * 4 + h, at, 0, None))
        attend(units, q1, k1, vt, kept2, ht1, inv1, 256, LEN, 256)
        out_of(1, j * 2, ht1, woc)
        out_of(1, j * 2 + 1, ht1, woc)

    each(BLOCKS // 2, cross_pair)

    wait_swapped(COT)

    @pl.when(swaps)
    def _():
        share(2, cot).start()

    def half_exchange(e, i):
        r = block_rows(i)
        return remote(sndh.at[e, r], rcvh.at[e, r], h_send.at[e, i], h_recv.at[e, i], sib)

    def expert_norm(i):
        r = block_rows(i)
        exchange(1, i).wait_recv()
        state = s1[r, :] + (snd[1, r, :].astype(F32) + rcv[1, r, :].astype(F32))
        s2[r, :] = state
        xhat, _ = normalise(state)
        n2[r, :] = (xhat * gains[2:3, :]).astype(BF16)

    each(2, expert_norm)
    share(2, cot).wait_recv()
    cot_t[...] = cot[...].T
    each(2, lambda i: expert_norm(i + 2))

    def begin(copy):
        copy.start()

    def finish_send(copy):
        copy.wait_send()

    def share_rows(ref, to):
        return ref.at[pl.ds(pl.multiple_of(to * 32, 32), 32)]

    def scatter(f, action):
        src, dst = eb.at[f], e_out.at[row, f]

        def one(s):
            to = lax.rem(d + s + 1, n_dp)
            action(remote(share_rows(src, to), dst, e_send.at[f, s + 1], e_recv.at[f, row], (to, c)))

        each(n_dp - 1, one)

    def scatter_near(f):
        @pl.when(stays)
        def _():
            pltpu.make_async_copy(share_rows(eb.at[f], d), e_out.at[row, f], e_recv.at[f, row]).start()
            scatter(f, begin)

    def own_far(f):
        return remote(share_rows(eb.at[f], d), e_out.at[row, f], e_send.at[f, 0], e_recv.at[f, row], (d, c))

    def scatter_far(f):
        @pl.when(swaps)
        def _():
            own_far(f).start()
            scatter(f, begin)

    def collect(f):
        def one(i):
            src, dst = eb.at[f, pl.ds(0, 32)], e_out.at[i, f]

            @pl.when(stays & (i == row))
            def _():
                pltpu.make_async_copy(src, dst, e_recv.at[f, i]).wait()

            @pl.when(jnp.logical_not(stays & (i == row)))
            def _():
                remote(src, dst, e_send.at[f, 0], e_recv.at[f, i], diag).wait_recv()

        each(n_dp, one)

    hid, gpre = work.at[0:LEN], work.at[LEN:2 * LEN]

    def expert_tile(f):
        cols = slice(f * TILE, (f + 1) * TILE)

        def first(i):
            r = slice(i * BLOCK, (i + 1) * BLOCK)
            return dot(n2[r, :], up[:, cols]), dot(cot[r, :], down[cols, :], NT)

        def second(i, made):
            r = slice(i * BLOCK, (i + 1) * BLOCK)
            pre, grad = made
            phi, slope = gelu_parts(pre)
            hid[r, cols] = (pre * phi).astype(BF16)
            gpre[r, cols] = (grad * slope).astype(BF16)

        made = first(0)
        for i in range(BLOCKS):
            following = first(i + 1) if i + 1 < BLOCKS else None
            second(i, made)
            made = following

    def expert_back(i):
        r = block_rows(i)
        snd[0, r, :] = dot(gpre[r, :], up[...], NT).astype(BF16)
        exchange(2, i).start()

    def expert_out(i):
        r = block_rows(i)
        part = dot(hid[r, :], down[...])
        mine = lax.div(i, 2) == c
        rl = block_rows(lax.rem(i, 2))

        @pl.when(mine)
        def _():
            half_out[rl, :] = s2[r, :] + part

        @pl.when(jnp.logical_not(mine))
        def _():
            sndh[0, rl, :] = part.astype(BF16)
            half_exchange(0, lax.rem(i, 2)).start()

    def expert_grads(f):
        cols = slice(f * TILE, (f + 1) * TILE)
        eb[f, :, 0:TILE] = dot(nt[...], gpre[:, cols]).astype(BF16)
        eb[f, :, TILE:2 * TILE] = dot(cot_t[...], hid[:, cols]).astype(BF16)

    def done_sending(e):
        each(BLOCKS, lambda i: exchange(e, i).wait_send())

    done_sending(0)
    for f in range(TILES):
        wait_bring(UP + f)
        wait_bring(DOWN + f)
        expert_tile(f)
        if f == 0:
            nt[...] = n2[...].T
        if f + 1 < TILES:
            expert_grads(f)
            scatter_near(f)
        if f + 2 == TILES:
            scatter_far(0)

    each(BLOCKS, expert_back)
    scatter_far(1)
    expert_grads(TILES - 1)
    scatter_near(TILES - 1)
    scatter_far(2)
    scatter_far(3)
    each(BLOCKS, expert_out)

    def strip(n):
        return work.at[n * COLS:(n + 1) * COLS]

    dqt, dkb, dvb, ght = strip(0), strip(1), strip(2), strip(3)
    kt, qt = cot_t.at[0:COLS], cot_t.at[COLS:2 * COLS]
    dq, dk = down.at[:, 0:COLS], down.at[:, COLS:2 * COLS]
    gh, dv = n2.at[:, 0:COLS], n2.at[:, COLS:2 * COLS]
    gain_sum[...] = jnp.zeros_like(gain_sum)

    def branch_block(n, i, e, state, base, ht, inv, w_out):
        r = block_rows(i)
        exchange(e, i).wait_recv()
        grad = snd[e % 2, r, :].astype(F32) + rcv[e % 2, r, :].astype(F32)
        step, share_gain = norm_back(state[r, :], gains[n:n + 1, :], grad)
        moved = base[r, :].astype(F32) + step
        gs[r, :] = moved
        low = moved.astype(BF16)
        gb[r, :] = low
        gain_sum[n:n + 1, :] += jnp.where(lax.div(i, 2) == c, share_gain, 0.0)
        gh[r, :] = dot(low, w_out[...], NT).astype(BF16)
        turned = dot(w_out[...], low, NT).astype(BF16).astype(F32)
        prod = turned * ht[:, r].astype(F32)
        for h in everything:
            rows = slice(h * 64, h * 64 + 64)
            inner[h:h + 1, r] = jnp.sum(prod[rows], axis=0, keepdims=True)
            ght[rows, r] = (turned[rows] * inv[h:h + 1, r]).astype(BF16)

    def turn_queries(q, k, inv):
        kt[...] = k[...].T
        turned = q[...].T
        for h in everything:
            rows = slice(h * 64, h * 64 + 64)
            qt[rows, :] = (turned[rows].astype(F32) * inv[h:h + 1, :]).astype(BF16)
        dkt[...] = jnp.zeros_like(dkt)
        dvt[...] = jnp.zeros_like(dvt)

    pieces = tuple(zip((a0, a1, a2, a3, a4, a5), (ax0, ax1, ax2, ax3, ax4, ax5), (ay0, ay1, ay2, ay3, ay4, ay5),
                       (a0_out, a1_out, a2_out, a3_out, a4_out, a5_out)))
    n_pieces = len(pieces)

    def over_x(n):
        buf, place = pieces[n][:2]
        return remote(buf.at[:, 1 - side], place, p_send.at[0, n], p_recv.at[0, n], across)

    def over_y(n):
        buf, place = pieces[n][0], pieces[n][2]
        return remote(buf.at[:, side], place, p_send.at[1, n], p_recv.at[1, n], (d, c))

    def add_x(n):
        buf, place = pieces[n][:2]
        over_x(n).wait_recv()
        buf[:, side] = (buf[:, side].astype(F32) + place[...].astype(F32)).astype(BF16)

        @pl.when(swaps)
        def _():
            over_y(n).start()

    def owners(n, action):
        buf, out = pieces[n][0], pieces[n][3]

        def one(s):
            to = lax.rem(z * 2 + c + s + 1, 2 * zs)
            to_z, to_c = lax.div(to, 2), lax.rem(to, 2)
            src = buf.at[to_z, side, pl.ds(pl.multiple_of(to_c * 32, 32), 32)]
            action(remote(src, out.at[z], a_send.at[n, s], a_recv.at[n, z], (to_z * 4 + side * 2 + to_c, t)))

        each(2 * zs - 1, one)

    def own_share(n):
        src = pieces[n][0].at[z, side, pl.ds(pl.multiple_of(c * 32, 32), 32)]
        return pltpu.make_async_copy(src, pieces[n][3].at[z], a_recv.at[n, z])

    def add_y(n):
        @pl.when(stays)
        def _():
            buf, place = pieces[n][0], pieces[n][2]
            over_y(n).wait_recv()
            buf[:, side] = (buf[:, side].astype(F32) + place[...].astype(F32)).astype(BF16)
            own_share(n).start()
            owners(n, begin)

    def collect_piece(n):
        buf, out = pieces[n][0], pieces[n][3]

        def one(i):
            @pl.when(stays & (i == z))
            def _():
                own_share(n).wait()

            @pl.when(jnp.logical_not(stays & (i == z)))
            def _():
                remote(buf.at[0, 0, pl.ds(0, 32)], out.at[i], a_send.at[n, 0], a_recv.at[n, i], diag).wait_recv()

        each(zs, one)

        @pl.when(stays)
        def _():
            owners(n, finish_send)

        @pl.when(swaps)
        def _():
            over_y(n).wait_send()

        over_x(n).wait_send()

    def by_owner(grad):
        return grad.astype(BF16).T.reshape(zs, 2, WIDTH // (2 * zs), grad.shape[0])

    each(BLOCKS, lambda i: branch_block(2, i, 2, s2, cot, ht1, inv1, woc))
    def leave(n, out):
        buf = leaving.at[n]
        return (lambda: remote(buf, out, o_send.at[n], o_recv.at[n], diag),
                lambda: pltpu.make_async_copy(buf, out, o_recv.at[n]))

    def start_leave(n, out):
        far, near = leave(n, out)

        @pl.when(swaps)
        def _():
            far().start()

        @pl.when(stays)
        def _():
            near().start()

    def wait_leave(n, out):
        far, near = leave(n, out)

        @pl.when(swaps)
        def _():
            far().wait()

        @pl.when(stays)
        def _():
            near().wait()

    def half_done(n):
        def one(low):
            half_exchange(n, low).wait_recv()
            r = block_rows(low)
            leaving[n, r, :] = (half_out[r, :] + rcvh[n, r, :].astype(F32)).astype(BF16)

        each(2, one)

    half_done(0)
    start_leave(0, lo_out)
    a0[...] = by_owner(dot(ht1[...], gb[...]))
    over_x(0).start()
    turn_queries(q1, k1, inv1)

    def pair_grads(pair_of_heads, n, source_q, source_kv):
        rows = slice(pair_of_heads * 128, pair_of_heads * 128 + 128)
        dkb[rows, :] = (dkt[rows, :] * math.log(2.0)).astype(BF16)
        dvb[rows, :] = dvt[rows, :].astype(BF16)
        buf = pieces[n][0]
        for part, (grad, source) in enumerate(((dqt, source_q), (dkb, source_kv), (dvb, source_kv))):
            buf[:, :, :, part * 128:part * 128 + 128] = by_owner(dot(grad[rows, :], source[...]))
        over_x(n).start()

    def cross_back(pair_of_heads):
        heads = (2 * pair_of_heads, 2 * pair_of_heads + 1)
        units = [(h, i * 4 + h, i * 256, 0) for h in heads for i in range(BLOCKS)]
        attend_back(units, v1, kt, qt, gh, ght, kept2, inner, inv1, dqt, dkt, dvt, 256, LEN, 256)
        pair_grads(pair_of_heads, 1 + pair_of_heads, n1, mem)

    cross_back(0)
    cross_back(1)

    def settle():
        dq[...] = dqt[...].T
        dk[...] = dkb[...].T
        dv[...] = dvb[...].T

    add_x(0)
    settle()
    done_sending(1)

    def cross_grads(i):
        r = block_rows(i)
        snd[1, r, :] = dot(dq[r, :], wq[...], NT).astype(BF16)
        exchange(3, i).start()

    each(BLOCKS, cross_grads)
    def memory_grads(i):
        r = block_rows(i)
        part = dot(dk[r, :], wkv[0], NT) + dot(dv[r, :], wkv[1], NT)
        mine = lax.div(i, 2) == c
        rl = block_rows(lax.rem(i, 2))

        @pl.when(mine)
        def _():
            half_out[rl, :] = part

        @pl.when(jnp.logical_not(mine))
        def _():
            sndh[1, rl, :] = part.astype(BF16)
            half_exchange(1, lax.rem(i, 2)).start()

    each(BLOCKS, memory_grads)
    add_x(1)

    each(BLOCKS, lambda i: branch_block(1, i, 3, s1, gs, ht0, inv0, wos))
    half_done(1)
    start_leave(1, gm_out)
    turn_queries(q0, k0, inv0)

    def self_back(pair_of_heads):
        heads = (2 * pair_of_heads, 2 * pair_of_heads + 1)
        attend_back([(h, h, 0, 0) for h in heads], v0, kt, qt, gh, ght, kept0, inner, inv0, dqt, dkt, dvt, 256, 256, 256)
        units = [(h, j * 4 + h, (j + 1) * 256, j * 256) for h in heads for j in range(BLOCKS - 1)]
        attend_back(units, v0, kt, qt, gh, ght, kept1, inner, inv0, dqt, dkt, dvt, 256, 512, 256)
        pair_grads(pair_of_heads, 4 + pair_of_heads, n0, n0)

    a3[...] = by_owner(dot(ht0[...], gb[...]))
    over_x(3).start()
    self_back(0)
    add_x(2)
    self_back(1)
    settle()

    def input_grads(i):
        r = block_rows(i)
        return dot(dq[r, :], wqkv[0], NT) + dot(dk[r, :], wqkv[1], NT) + dot(dv[r, :], wqkv[2], NT)

    def input_send(low):
        sndh[2, block_rows(low), :] = input_grads((1 - c) * 2 + low).astype(BF16)
        half_exchange(2, low).start()

    each(2, input_send)

    def input_keep(low):
        half_out[block_rows(low), :] = input_grads(c * 2 + low)

    each(2, input_keep)

    def input_done(low):
        half_exchange(2, low).wait_recv()
        rl = block_rows(low)
        r = block_rows(c * 2 + low)
        grad = half_out[rl, :] + rcvh[2, rl, :].astype(F32)
        step, share_gain = norm_back(x[r, :].astype(F32), gains[0:1, :], grad)
        gain_sum[0:1, :] += share_gain
        leaving[2, rl, :] = (gs[r, :] + step).astype(BF16)

    each(2, input_done)
    start_leave(2, gi_out)
    add_y(0)
    add_x(3)

    number = jnp.full((1, 128), expert[0, 0].astype(F32))
    for j in range(n_dp):
        turned = gain_sum[...] if j == 0 else pltpu.roll(gain_sum[...], (WIDTH - 32 * j) % WIDTH, 1)
        g_send[j] = turned[:, :128]
        g_send[j, 3:4, :] = number

    def gain_copy(s):
        to = lax.rem(lin + s, n_all)
        to_dp = lax.div(to, 2)
        return remote(g_send.at[to_dp], g_in.at[lin], g_ssem.at[s], g_rsem.at[lin], (to_dp, lax.rem(to, 2)))

    each(n_all - 1, lambda s: gain_copy(s + 1).start())
    keep_gain = pltpu.make_async_copy(g_send.at[d], g_in.at[lin], g_rsem.at[lin])
    keep_gain.start()

    add_y(1)
    add_x(4)
    add_y(2)
    add_x(5)
    add_y(3)
    add_y(4)
    add_y(5)

    wait_leave(0, lo_out)
    wait_leave(1, gm_out)
    wait_leave(2, gi_out)
    for f in range(TILES):
        collect(f)
        scatter(f, finish_send)

        @pl.when(swaps)
        def _():
            own_far(f).wait_send()

    for n in range(n_pieces):
        collect_piece(n)
    keep_gain.wait()

    def gain_wait(s):
        gain_copy(s + 1).wait_send()
        who = lax.rem(lin + s + 1, n_all)
        remote(g_send.at[0], g_in.at[who], g_ssem.at[0], g_rsem.at[who], diag).wait_recv()

    each(n_all - 1, gain_wait)
    g_out[...] = jnp.sum(g_in[...], axis=0)
    for r in range(n_dp):
        ids_out[r:r + 1, :] = g_in[2 * r, 3:4, :]

    @pl.when(swaps)
    def _():
        for n in range(n_brought):
            bring(n, theirs)[0]().wait_send()
        for n in range(6):
            first_piece(n).wait_send()
            each(zs - 1, lambda s: hand_along(n, s + 1).wait_send())
            each(zs, lambda s: hand_across(n, s).wait_send())

    for n, buf in enumerate((x, mem, cot)):
        share(n, buf).wait_send()

    @pl.when(stays)
    def _():
        share_starts().wait_send()

    done_sending(2)
    done_sending(3)
    for e in range(3):
        each(2, lambda i: half_exchange(e, i).wait_send())


VMEM_BYTES = 63 * 2**20
ANY_PLACE = pl.BlockSpec(memory_space=pl.ANY)
IN_HBM = pl.BlockSpec(memory_space=pltpu.HBM)
IN_SMEM = pl.BlockSpec(memory_space=pltpu.SMEM)
IN_VMEM = pl.BlockSpec(memory_space=pltpu.VMEM)


def paired_layer(n_dp, lens, expert, gains, *arrays):
    bf = lambda *shape: pltpu.VMEM(shape, BF16)
    fl = lambda *shape: pltpu.VMEM(shape, F32)
    dma = lambda *shape: pltpu.SemaphoreType.DMA(shape)
    tokens = bf(LEN, WIDTH)
    heads = bf(LEN, COLS)
    turned = bf(COLS, LEN)
    half = jax.ShapeDtypeStruct((HALF, WIDTH), BF16)
    zs = n_dp // 4
    sizes = PIECES
    split = [bf(zs, 2, WIDTH // (2 * zs), size) for size in sizes]
    x_parts = [bf(zs, WIDTH // (2 * zs), size) for size in sizes]
    return pl.pallas_call(
        partial(layer_kernel, n_dp),
        out_shape=(half, half, half, jax.ShapeDtypeStruct((n_dp, TILES, 32, 2 * TILE), BF16),
                   *[jax.ShapeDtypeStruct((zs, 32, size), BF16) for size in sizes],
                   jax.ShapeDtypeStruct((8, 128), F32), jax.ShapeDtypeStruct((n_dp, 128), F32)),
        in_specs=[IN_SMEM] * 2 + [IN_VMEM] + [ANY_PLACE] * 10,
        out_specs=(ANY_PLACE,) * (4 + len(sizes)) + (IN_VMEM,) * 2,
        scratch_shapes=[
            tokens, tokens, tokens, bf(3, WIDTH, COLS), bf(COLS, WIDTH), bf(WIDTH, COLS), bf(2, WIDTH, COLS),
            bf(COLS, WIDTH), bf(WIDTH, HIDDEN), bf(HIDDEN, WIDTH), pltpu.VMEM((8, LEN), jnp.int32),
            fl(LEN, WIDTH), fl(LEN, WIDTH), fl(LEN, WIDTH), tokens, tokens, tokens,
            heads, heads, heads, heads, heads, heads, turned, turned, turned, fl(8, LEN), fl(8, LEN), fl(8, LEN),
            bf(4, 256, 256), bf(12, 512, 256), bf(16, LEN, 256), tokens, fl(COLS, LEN), fl(COLS, LEN),
            bf(2 * LEN, HIDDEN), bf(WIDTH, LEN), bf(WIDTH, LEN), bf(TILES, WIDTH, 2 * TILE), *split, *x_parts, *x_parts,
            bf(2, LEN, WIDTH), bf(2, LEN, WIDTH), bf(3, HALF, WIDTH), bf(3, HALF, WIDTH), bf(3, HALF, WIDTH),
            fl(HALF, WIDTH), fl(8, WIDTH), fl(n_dp, 8, 128), fl(2 * n_dp, 8, 128),
            dma(3 + 2 * TILES), dma(3 + 2 * TILES), dma(6, n_dp // 2), dma(6, n_dp // 2), dma(4), dma(4),
            dma(4, 4), dma(4, 4), dma(3, 2), dma(3, 2),
            dma(TILES, n_dp), dma(TILES, n_dp), dma(2, len(sizes)), dma(2, len(sizes)), dma(len(sizes), 2 * zs), dma(len(sizes), zs),
            dma(2 * n_dp), dma(2 * n_dp), dma(3), dma(3),
        ],
        compiler_params=pltpu.CompilerParams(
            collective_id=0, has_side_effects=True, vmem_limit_bytes=VMEM_BYTES),
        cost_estimate=pl.CostEstimate(flops=20 * 10**9, bytes_accessed=20 * 2**20, transcendentals=0),
    )(lens, expert, gains, *arrays)


def choose_kernel(expert, up_in, down_in, up_out, down_out, up_v, down_v, in_sems, out_sems):
    e = expert[0, 0]
    parts = in_sems.shape[1]
    steps = []
    for p in range(parts):
        for n, (src, mid, dst) in enumerate(((up_in, up_v, up_out), (down_in, down_v, down_out))):
            rows = mid.shape[0] // parts
            at = pl.ds(p * rows, rows)
            steps.append((pltpu.make_async_copy(src.at[e, at], mid.at[at], in_sems.at[n, p]),
                          pltpu.make_async_copy(mid.at[at], dst.at[at], out_sems.at[n, p])))
    for first, _ in steps:
        first.start()
    for first, second in steps:
        first.wait()
        second.start()
    for _, second in steps:
        second.wait()


def choose_expert(expert, w_up, w_down):
    return pl.pallas_call(
        choose_kernel,
        out_shape=(jax.ShapeDtypeStruct(w_up.shape[1:], BF16), jax.ShapeDtypeStruct(w_down.shape[1:], BF16)),
        in_specs=[IN_SMEM, IN_HBM, IN_HBM],
        out_specs=(IN_HBM, IN_HBM),
        scratch_shapes=[pltpu.VMEM(w_up.shape[1:], BF16), pltpu.VMEM(w_down.shape[1:], BF16),
                        pltpu.SemaphoreType.DMA((2, 8)), pltpu.SemaphoreType.DMA((2, 8))],
        compiler_params=pltpu.CompilerParams(vmem_limit_bytes=VMEM_BYTES),
    )(expert, w_up, w_down)


def place_kernel(
    ids_any, gains_any, e_any, a0_any, a1_any, a2_any, a3_any, a4_any, a5_any, gi_any, gm_any, lo_any,
    lo_out, gi_out, gm_out, gain_out, qkv_out, os_out, q_out, kv_out, oc_out, up_out, down_out,
    ids, ids_in, gains_in, e_in, a0_in, a1_in, a2_in, a3_in, a4_in, a5_in, gi_in, gm_in, lo_in, gi_v, gm_v, gain_v, qkv_v, os_v, q_v, kv_v, oc_v,
    ups, downs, in_sems, e_sems, up_sems, down_sems, out_sems,
):
    rows = e_in.shape[0]
    number = pltpu.make_async_copy(ids_any, ids, in_sems.at[0])
    number.start()
    pairs = ((gi_any, gi_in), (gm_any, gm_in), (lo_any, lo_in), (gains_any, gains_in), (a0_any, a0_in),
             (a1_any, a1_in), (a2_any, a2_in), (a3_any, a3_in), (a4_any, a4_in), (a5_any, a5_in))
    reads = [pltpu.make_async_copy(src, dst, in_sems.at[1 + n]) for n, (src, dst) in enumerate(pairs)]
    blocks = [pltpu.make_async_copy(e_any.at[r], e_in.at[r], e_sems.at[r]) for r in range(rows)]
    for copy in reads + blocks:
        copy.start()
    writes = []

    def write(src, dst, sem):
        writes.append(pltpu.make_async_copy(src, dst, sem))
        writes[-1].start()

    reads[0].wait()
    gi_v[...] = gi_in[...].astype(F32)
    write(gi_v, gi_out, out_sems.at[0])
    reads[1].wait()
    gm_v[...] = gm_in[...].astype(F32)
    write(gm_v, gm_out, out_sems.at[1])
    reads[2].wait()
    write(lo_in, lo_out, out_sems.at[2])
    for copy in reads[3:]:
        copy.wait()
    gain_v[...] = gains_in[0:3, 0:32]
    oc_v[...] = jnp.sum(a0_in[...].astype(F32), axis=0)
    os_v[...] = jnp.sum(a3_in[...].astype(F32), axis=0)
    for pair, (cross, own) in enumerate(((a1_in, a4_in), (a2_in, a5_in))):
        cols = slice(pair * 128, pair * 128 + 128)
        cross = jnp.sum(cross[...].astype(F32), axis=0)
        own = jnp.sum(own[...].astype(F32), axis=0)
        q_v[:, cols] = cross[:, 0:128]
        for n in range(2):
            kv_v[n, :, cols] = cross[:, 128 + n * 128:256 + n * 128]
        for n in range(3):
            qkv_v[n, :, cols] = own[:, n * 128:n * 128 + 128]
    small = ((gain_v, gain_out), (qkv_v, qkv_out), (os_v, os_out), (q_v, q_out), (kv_v, kv_out), (oc_v, oc_out))
    for n, (src, dst) in enumerate(small):
        write(src, dst, out_sems.at[3 + n])
    number.wait()
    for r in range(rows):
        blocks[r].wait()
        for f in range(TILES):
            ups[r, :, f * TILE:(f + 1) * TILE] = e_in[r, f, :, 0:TILE].astype(F32)
            downs[r, :, f * TILE:(f + 1) * TILE] = e_in[r, f, :, TILE:2 * TILE].astype(F32)
        e = ids[r, 0].astype(jnp.int32)
        write(ups.at[r], up_out.at[e], up_sems.at[r])
        write(downs.at[r], down_out.at[e], down_sems.at[r])
    for copy in writes:
        copy.wait()


def place_grads(experts, *arrays):
    shape = lambda *dims: jax.ShapeDtypeStruct(dims, F32)
    like = lambda array: pltpu.VMEM(array.shape, array.dtype)
    dma = lambda *dims: pltpu.SemaphoreType.DMA(dims)
    rows = arrays[2].shape[0]
    staged = pltpu.VMEM((rows, 32, HIDDEN), F32)
    half = pltpu.VMEM((HALF, WIDTH), F32)
    small = [pltpu.VMEM(dims, F32) for dims in ((3, 32), (3, 32, COLS), (32, COLS), (32, COLS), (2, 32, COLS), (32, COLS))]
    return pl.pallas_call(
        place_kernel,
        out_shape=(jax.ShapeDtypeStruct((HALF, WIDTH), BF16), shape(HALF, WIDTH), shape(HALF, WIDTH), shape(3, 32), shape(3, 32, COLS), shape(32, COLS),
                   shape(32, COLS), shape(2, 32, COLS), shape(32, COLS),
                   shape(experts, 32, HIDDEN), shape(experts, 32, HIDDEN)),
        in_specs=[IN_HBM] * 12,
        out_specs=(IN_HBM,) * 11,
        scratch_shapes=[pltpu.SMEM(arrays[0].shape, F32)] + [like(array) for array in arrays] + [
            half, half, *small, staged, staged, dma(11), dma(rows), dma(rows), dma(rows), dma(9)],
        compiler_params=pltpu.CompilerParams(vmem_limit_bytes=VMEM_BYTES),
    )(*arrays)


def per_device_paired(
    layer_input, memory, seg_lengths, expert_ids, ln_gains, w_qkv, w_out_self, w_query_cross, w_kv_cross,
    w_out_cross, w_up, w_down, cotangent,
):
    n_dp = lax.axis_size("dp")
    up, down = choose_expert(expert_ids, w_up, w_down)
    layer_output, grad_input, grad_memory, e_rows, *a_rows, gain_rows, numbers = paired_layer(
        n_dp, seg_lengths, expert_ids, ln_gains,
        layer_input[0], memory[0], cotangent[0], w_qkv, w_out_self, w_query_cross, w_kv_cross, w_out_cross, up, down,
    )
    layer_output, grad_input, grad_memory, gain_share, qkv, out_self, query, key_value, out_cross, grad_up, grad_down = place_grads(
        w_up.shape[0], numbers, gain_rows, e_rows, *a_rows, grad_input, grad_memory, layer_output)
    return (
        layer_output[None], grad_input[None], grad_memory[None], gain_share, qkv, out_self.T, query, key_value,
        out_cross.T, grad_up, jnp.swapaxes(grad_down, 1, 2),
    )


def fits_pairs(mesh, layer_input, seg_lengths, w_up):
    return (
        mesh.shape["tp"] == 2
        and mesh.shape["dp"] == 16
        and layer_input.shape == (mesh.shape["dp"], LEN, WIDTH)
        and w_up.shape == (mesh.shape["dp"], WIDTH, 2 * HIDDEN)
    )


def solution(mesh):
    in_specs = (
        P("dp", "tp", None),
        P("dp", "tp", None),
        P("dp", None),
        P("dp", None),
        P(),
        P(None, None, "tp"),
        P("tp", None),
        P(None, "tp"),
        P(None, None, "tp"),
        P("tp", None),
        P(None, None, "tp"),
        P(None, "tp", None),
        P("dp", "tp", None),
    )
    out_specs = (
        P("dp", "tp", None),
        P("dp", "tp", None),
        P("dp", "tp", None),
        P(None, "dp"),
        P(None, "dp", "tp"),
        P("tp", "dp"),
        P("dp", "tp"),
        P(None, "dp", "tp"),
        P("tp", "dp"),
        P(None, "dp", "tp"),
        P(None, "tp", "dp"),
    )

    def run(*args):
        layer_input, seg_lengths, w_up = args[0], args[2], args[10]
        paired = fits_pairs(mesh, layer_input, seg_lengths, w_up)
        return jax.shard_map(
            per_device_paired if paired else per_device,
            mesh=mesh, in_specs=in_specs, out_specs=out_specs, check_vma=False,
        )(*args)

    return run
```

```python
import math
from functools import partial

import jax
import jax.numpy as jnp
from jax import lax
from jax.experimental import pallas as pl
from jax.experimental.pallas import tpu as pltpu
from jax.sharding import PartitionSpec as P

HEAD_DIM = 64


epsilon = 1e-05


def layer_norm(values, gain):
    centered = values - jnp.mean(values, axis=-1, keepdims=True)
    spread = jnp.mean(centered * centered, axis=-1, keepdims=True)
    return centered * lax.rsqrt(spread + epsilon) * gain


def norm_backward(state, gain, grad_normed, grad_state):
    unused, pullback = jax.vjp(layer_norm, state, gain)
    grad_values, grad_gain = pullback(grad_normed)
    return (grad_state + grad_values, grad_gain)


def segment_mask(lengths, length, count):
    seg_ends = jnp.cumsum(lengths, dtype=jnp.int32)
    places = jnp.arange(length, dtype=jnp.int32)
    labels = jnp.sum((places[:, None] >= seg_ends[None, :]).astype(jnp.int32), axis=1)
    row_places = jnp.arange(count, dtype=jnp.int32)
    return (labels[:, None] == labels[None, :]) & (row_places[:, None] >= places[None, :])


def to_heads(block):
    return block.reshape(block.shape[:-1] + (block.shape[-1] // HEAD_DIM, HEAD_DIM))


def softmax_rows(queries, key_rows, allowed):
    scores = jnp.einsum(
        "qhd,khd->hqk", queries, key_rows, preferred_element_type=jnp.float32
    ) * HEAD_DIM ** (-0.5)
    if allowed is not None:
        scores = jnp.where(allowed[None], scores, -1e30)
    row_max = jnp.max(scores, axis=-1, keepdims=True)
    weights = jnp.exp(scores - row_max)
    return weights / jnp.sum(weights, axis=-1, keepdims=True)


def attend_both(queries, key_rows, value_rows, allowed, grad_heads):
    row_probs = softmax_rows(queries, key_rows, allowed)
    probs_low = row_probs.astype(jnp.bfloat16)
    heads_out = jnp.einsum(
        "hqk,khd->qhd", probs_low, value_rows, preferred_element_type=jnp.float32
    ).astype(jnp.bfloat16)
    grad_probs = jnp.einsum(
        "qhd,khd->hqk", grad_heads, value_rows, preferred_element_type=jnp.float32
    )
    inner_sum = jnp.sum(row_probs * grad_probs, axis=-1, keepdims=True)
    grad_scores = (row_probs * (grad_probs - inner_sum)).astype(jnp.bfloat16)
    grad_queries = jnp.einsum(
        "hqk,khd->qhd", grad_scores, key_rows, preferred_element_type=jnp.float32
    ) * HEAD_DIM ** (-0.5)
    grad_keys = jnp.einsum(
        "hqk,qhd->khd", grad_scores, queries, preferred_element_type=jnp.float32
    ) * HEAD_DIM ** (-0.5)
    grad_values = jnp.einsum(
        "hqk,qhd->khd", probs_low, grad_heads, preferred_element_type=jnp.float32
    )
    return (heads_out, grad_queries, grad_keys, grad_values)


def spread_tokens(normed):
    return lax.all_gather(normed, "tp", axis=1, tiled=True)


def sum_tokens(partial_out):
    return lax.psum_scatter(partial_out, "tp", scatter_dimension=1, tiled=True)


def gather_grads(grad_state):
    return lax.all_gather(grad_state.astype(jnp.bfloat16), "tp", axis=1, tiled=True)


def sum_grads(grad_normed):
    return lax.psum_scatter(grad_normed, "tp", scatter_dimension=1, tiled=True)


def self_partial(normed_all, seg_lengths, w_qkv, w_out_self):
    projected = jnp.einsum(
        "rld,cde->rcle", normed_all, w_qkv, preferred_element_type=jnp.float32
    ).astype(jnp.bfloat16)

    def one_row(items):
        row_proj, lengths = items
        split_heads = to_heads(row_proj)
        length = row_proj.shape[1]
        row_probs = softmax_rows(
            split_heads[0], split_heads[1], segment_mask(lengths, length, length)
        )
        heads_out = jnp.einsum(
            "hqk,khd->qhd",
            row_probs.astype(jnp.bfloat16),
            split_heads[2],
            preferred_element_type=jnp.float32,
        )
        return heads_out.reshape(row_proj.shape[1:]).astype(jnp.bfloat16)

    heads_all = lax.map(one_row, (projected, seg_lengths))
    return jnp.einsum("rle,ed->rld", heads_all, w_out_self, preferred_element_type=jnp.float32)


def self_backward(normed_all, seg_lengths, w_qkv, w_out_self, grad_branch):
    projected = jnp.einsum(
        "rld,cde->rcle", normed_all, w_qkv, preferred_element_type=jnp.float32
    ).astype(jnp.bfloat16)
    grad_heads = jnp.einsum(
        "rld,ed->rle", grad_branch, w_out_self, preferred_element_type=jnp.float32
    ).astype(jnp.bfloat16)

    def one_row(items):
        row_proj, lengths, row_grad = items
        split_heads = to_heads(row_proj)
        length = row_proj.shape[1]
        results = attend_both(
            split_heads[0],
            split_heads[1],
            split_heads[2],
            segment_mask(lengths, length, length),
            to_heads(row_grad),
        )
        return (
            results[0].reshape(length, -1),
            jnp.stack([piece.reshape(length, -1).astype(jnp.bfloat16) for piece in results[1:]]),
        )

    heads_all, grad_proj = lax.map(one_row, (projected, seg_lengths, grad_heads))
    grad_w_out = jnp.einsum(
        "rle,rld->ed", heads_all, grad_branch, preferred_element_type=jnp.float32
    )
    grad_w_qkv = jnp.einsum(
        "rld,rcle->cde", normed_all, grad_proj, preferred_element_type=jnp.float32
    )
    grad_normed = jnp.einsum("rcle,cde->rld", grad_proj, w_qkv, preferred_element_type=jnp.float32)
    return (grad_normed, grad_w_qkv, grad_w_out)


def cross_partial(normed_all, memory_all, w_query_cross, w_kv_cross, w_out_cross):
    queries = jnp.einsum(
        "rld,de->rle", normed_all, w_query_cross, preferred_element_type=jnp.float32
    ).astype(jnp.bfloat16)
    key_value = jnp.einsum(
        "rmd,cde->rcme", memory_all, w_kv_cross, preferred_element_type=jnp.float32
    ).astype(jnp.bfloat16)

    def one_row(items):
        row_query, row_kv = items
        split_kv = to_heads(row_kv)
        row_probs = softmax_rows(to_heads(row_query), split_kv[0], None)
        heads_out = jnp.einsum(
            "hqk,khd->qhd",
            row_probs.astype(jnp.bfloat16),
            split_kv[1],
            preferred_element_type=jnp.float32,
        )
        return heads_out.reshape(row_query.shape).astype(jnp.bfloat16)

    heads_all = lax.map(one_row, (queries, key_value))
    return jnp.einsum("rle,ed->rld", heads_all, w_out_cross, preferred_element_type=jnp.float32)


def cross_core(normed_all, memory_all, w_query_cross, w_kv_cross, w_out_cross, grad_branch):
    queries = jnp.einsum(
        "rld,de->rle", normed_all, w_query_cross, preferred_element_type=jnp.float32
    ).astype(jnp.bfloat16)
    key_value = jnp.einsum(
        "rmd,cde->rcme", memory_all, w_kv_cross, preferred_element_type=jnp.float32
    ).astype(jnp.bfloat16)
    grad_heads = jnp.einsum(
        "rld,ed->rle", grad_branch, w_out_cross, preferred_element_type=jnp.float32
    ).astype(jnp.bfloat16)

    def one_row(items):
        row_query, row_kv, row_grad = items
        split_kv = to_heads(row_kv)
        query_count = row_query.shape[0]
        memory_count = row_kv.shape[1]
        results = attend_both(
            to_heads(row_query), split_kv[0], split_kv[1], None, to_heads(row_grad)
        )
        grad_kv = jnp.stack(
            [results[2].reshape(memory_count, -1), results[3].reshape(memory_count, -1)]
        )
        return (results[0].reshape(query_count, -1), results[1].reshape(query_count, -1), grad_kv)

    heads_all, grad_queries, grad_kv = lax.map(one_row, (queries, key_value, grad_heads))
    grad_w_out = jnp.einsum(
        "rle,rld->ed", heads_all, grad_branch, preferred_element_type=jnp.float32
    )
    return (grad_queries, grad_kv, grad_w_out)


def cross_backward(normed_all, memory_all, w_query_cross, w_kv_cross, w_out_cross, grad_branch):
    grad_queries, grad_kv, grad_w_out = cross_core(
        normed_all, memory_all, w_query_cross, w_kv_cross, w_out_cross, grad_branch
    )
    grad_queries = grad_queries.astype(jnp.bfloat16)
    grad_kv = grad_kv.astype(jnp.bfloat16)
    grad_w_query = jnp.einsum(
        "rld,rle->de", normed_all, grad_queries, preferred_element_type=jnp.float32
    )
    grad_w_kv = jnp.einsum("rmd,rcme->cde", memory_all, grad_kv, preferred_element_type=jnp.float32)
    grad_normed = jnp.einsum(
        "rle,de->rld", grad_queries, w_query_cross, preferred_element_type=jnp.float32
    )
    grad_memory = jnp.einsum(
        "rcme,cde->rmd", grad_kv, w_kv_cross, preferred_element_type=jnp.float32
    )
    return (grad_normed, grad_memory, grad_w_query, grad_w_kv, grad_w_out)


def expert_rows(weights, expert):
    return lax.dynamic_index_in_dim(weights, expert, 0, keepdims=False)


def ffn_partial(normed_all, expert_ids, w_up, w_down):

    def one_row(items):
        normed_row, expert = items
        pre_act = jnp.dot(normed_row, expert_rows(w_up, expert), preferred_element_type=jnp.float32)
        hidden = jax.nn.gelu(pre_act, approximate=False).astype(jnp.bfloat16)
        return jnp.dot(hidden, expert_rows(w_down, expert), preferred_element_type=jnp.float32)

    return lax.map(one_row, (normed_all, expert_ids[:, 0]))


def ffn_backward(normed_all, expert_ids, w_up, w_down, grad_branch):

    def one_row(items):
        normed_row, expert, grad_row = items
        up_rows = expert_rows(w_up, expert)
        down_rows = expert_rows(w_down, expert)
        pre_act = jnp.dot(normed_row, up_rows, preferred_element_type=jnp.float32)
        activated, gelu_back = jax.vjp(partial(jax.nn.gelu, approximate=False), pre_act)
        hidden = activated.astype(jnp.bfloat16)
        grad_hidden = lax.dot_general(
            grad_row, down_rows, (((1,), (1,)), ((), ())), preferred_element_type=jnp.float32
        )
        grad_pre = gelu_back(grad_hidden)[0].astype(jnp.bfloat16)
        grad_down = lax.dot_general(
            hidden, grad_row, (((0,), (0,)), ((), ())), preferred_element_type=jnp.float32
        )
        grad_up = lax.dot_general(
            normed_row, grad_pre, (((0,), (0,)), ((), ())), preferred_element_type=jnp.float32
        )
        grad_normed = lax.dot_general(
            grad_pre, up_rows, (((1,), (1,)), ((), ())), preferred_element_type=jnp.float32
        )
        return (grad_normed, grad_up, grad_down)

    grad_normed, row_up, row_down = lax.map(one_row, (normed_all, expert_ids[:, 0], grad_branch))
    choose = (
        expert_ids[:, 0][:, None] == jnp.arange(w_up.shape[0], dtype=jnp.int32)[None, :]
    ).astype(jnp.float32)
    grad_w_up = jnp.einsum("re,rdf->edf", choose, row_up, precision=lax.Precision.HIGHEST)
    grad_w_down = jnp.einsum("re,rfd->efd", choose, row_down, precision=lax.Precision.HIGHEST)
    return (grad_normed, grad_w_up, grad_w_down)


def run_forward(layer_input, memory, seg_lengths, expert_ids, ln_gains, attn_weights, w_up, w_down):
    w_qkv, w_out_self, w_query_cross, w_kv_cross, w_out_cross = attn_weights
    state_zero = layer_input.astype(jnp.float32)
    normed_local = layer_norm(state_zero, ln_gains[0]).astype(jnp.bfloat16)
    memory_all = lax.all_gather(memory, "tp", axis=1, tiled=True)
    normed_self = spread_tokens(normed_local)
    state_one = state_zero + sum_tokens(self_partial(normed_self, seg_lengths, w_qkv, w_out_self))
    normed_cross = spread_tokens(layer_norm(state_one, ln_gains[1]).astype(jnp.bfloat16))
    state_two = state_one + sum_tokens(
        cross_partial(normed_cross, memory_all, w_query_cross, w_kv_cross, w_out_cross)
    )
    normed_ffn = spread_tokens(layer_norm(state_two, ln_gains[2]).astype(jnp.bfloat16))
    state_three = state_two + sum_tokens(ffn_partial(normed_ffn, expert_ids, w_up, w_down))
    return (
        state_three,
        (state_zero, state_one, state_two, normed_self, normed_cross, normed_ffn, memory_all),
    )


def per_device(
    layer_input,
    memory,
    seg_lengths,
    expert_ids,
    ln_gains,
    w_qkv,
    w_out_self,
    w_query_cross,
    w_kv_cross,
    w_out_cross,
    w_up,
    w_down,
    cotangent,
):
    attn_weights = (w_qkv, w_out_self, w_query_cross, w_kv_cross, w_out_cross)
    use_qkv, use_out_self, use_query, use_kv, use_out_cross = attn_weights
    state_three, kept = run_forward(
        layer_input, memory, seg_lengths, expert_ids, ln_gains, attn_weights, w_up, w_down
    )
    fresh = lax.optimization_barrier((layer_input, memory, state_three))
    unused, kept = run_forward(
        fresh[0], fresh[1], seg_lengths, expert_ids, ln_gains, attn_weights, w_up, w_down
    )
    state_zero, state_one, state_two, normed_self, normed_cross, normed_ffn, memory_all = kept
    grad_state = cotangent.astype(jnp.float32)
    grad_normed, grad_up, grad_down = ffn_backward(
        normed_ffn, expert_ids, w_up, w_down, gather_grads(grad_state)
    )
    grad_state, gain_ffn = norm_backward(state_two, ln_gains[2], sum_grads(grad_normed), grad_state)
    grad_normed, memory_part, grad_w_query, grad_w_kv, grad_w_out_cross = cross_backward(
        normed_cross, memory_all, use_query, use_kv, use_out_cross, gather_grads(grad_state)
    )
    grad_normed, grad_memory = (
        lax.psum_scatter(
            grad_normed.astype(jnp.bfloat16), "tp", scatter_dimension=1, tiled=True
        ).astype(jnp.float32),
        lax.psum_scatter(
            memory_part.astype(jnp.bfloat16), "tp", scatter_dimension=1, tiled=True
        ).astype(jnp.float32),
    )
    grad_state, gain_cross = norm_backward(state_one, ln_gains[1], grad_normed, grad_state)
    grad_normed, grad_w_qkv, grad_w_out_self = self_backward(
        normed_self, seg_lengths, use_qkv, use_out_self, gather_grads(grad_state)
    )
    grad_state, gain_self = norm_backward(
        state_zero, ln_gains[0], sum_grads(grad_normed), grad_state
    )
    summed = (
        lax.psum_scatter(
            grad_w_qkv.astype(jnp.bfloat16), "dp", scatter_dimension=1, tiled=True
        ).astype(jnp.float32),
        lax.psum_scatter(
            grad_w_out_self.astype(jnp.bfloat16), "dp", scatter_dimension=1, tiled=True
        ).astype(jnp.float32),
        lax.psum_scatter(
            grad_w_query.astype(jnp.bfloat16), "dp", scatter_dimension=0, tiled=True
        ).astype(jnp.float32),
        lax.psum_scatter(
            grad_w_kv.astype(jnp.bfloat16), "dp", scatter_dimension=1, tiled=True
        ).astype(jnp.float32),
        lax.psum_scatter(
            grad_w_out_cross.astype(jnp.bfloat16), "dp", scatter_dimension=1, tiled=True
        ).astype(jnp.float32),
        lax.psum_scatter(
            grad_up.astype(jnp.bfloat16), "dp", scatter_dimension=1, tiled=True
        ).astype(jnp.float32),
        lax.psum_scatter(
            grad_down.astype(jnp.bfloat16), "dp", scatter_dimension=2, tiled=True
        ).astype(jnp.float32),
    )
    grad_w_qkv, grad_w_out_self, grad_w_query, grad_w_kv, grad_w_out_cross, grad_up, grad_down = (
        summed
    )
    gain_total = lax.psum(jnp.stack([gain_self, gain_cross, gain_ffn]), ("dp", "tp"))
    share_width = gain_total.shape[1] // lax.axis_size("dp")
    gain_share = lax.dynamic_slice_in_dim(
        gain_total, lax.axis_index("dp") * share_width, share_width, 1
    )
    return (
        state_three.astype(jnp.bfloat16),
        grad_state,
        grad_memory,
        gain_share,
        grad_w_qkv,
        grad_w_out_self,
        grad_w_query,
        grad_w_kv,
        grad_w_out_cross,
        grad_up,
        grad_down,
    )


F32, BF16 = jnp.float32, jnp.bfloat16
MESH = pl.DeviceIdType.MESH
LOG2E = math.log2(math.e)
QSCALE = LOG2E * HEAD_DIM ** -0.5
NN = (((1,), (0,)), ((), ()))
NT = (((1,), (1,)), ((), ()))
TN = (((0,), (0,)), ((), ()))

LEN, WIDTH, COLS, HIDDEN, BLOCK, HALF = 1024, 512, 256, 1024, 256, 512
BLOCKS = LEN // BLOCK
TILE = 256
TILES = HIDDEN // TILE
PIECES = (COLS, 3 * COLS // 2, 3 * COLS // 2) * 2


def dot(left, right, dims=NN):
    return lax.dot_general(left, right, dims, preferred_element_type=F32)


def head_mask(block, side):
    lanes = lax.broadcasted_iota(jnp.int32, block.shape, 1)
    keep = (lanes >= HEAD_DIM) if side else (lanes < HEAD_DIM)
    return jnp.where(keep, block, jnp.zeros_like(block))


def window_bias(key_at, query_at, keys, queries, starts):
    key_place = key_at + lax.broadcasted_iota(jnp.int32, (keys, queries), 0)
    query_place = query_at + lax.broadcasted_iota(jnp.int32, (keys, queries), 1)
    return jnp.where((key_place >= starts) & (key_place <= query_place), 0.0, -1e30)


def add_up(total, part):
    return part if total is None else total + part


def kept_part(kept, slot, n, chunk):
    if kept.shape[2] == 2 * BLOCK:
        half = kept.shape[1] // chunk
        return kept.at[slot, (n % half) * chunk:(n % half + 1) * chunk, (n // half) * BLOCK:(n // half + 1) * BLOCK]
    return kept.at[slot, n * chunk:(n + 1) * chunk]


def attend(units, q, k, vt, kept, ht, inverse, q_len, k_len, chunk, before=None, after=None):
    def scores(unit):
        h, slot, q_at, k_at, bias = unit
        lanes = slice((h // 2) * 128, (h // 2) * 128 + 128)
        out, top = [], None
        queries = q[pl.ds(q_at, q_len), lanes]
        for j in range(0, k_len, chunk):
            s = dot(head_mask(k[pl.ds(k_at + j, chunk), lanes], h % 2), queries, NT)
            if bias is not None:
                s = s + bias[j:j + chunk]
            out.append(s)
            high = jnp.max(s.reshape(chunk // 8, 8, q_len), axis=0)
            top = high if top is None else jnp.maximum(top, high)
        return out, jnp.max(top, axis=0, keepdims=True)

    def values(unit, made):
        h, slot, q_at, k_at, bias = unit
        rows = slice(h * 64, h * 64 + 64)
        out, total = None, None
        for n, s in enumerate(made[0]):
            p = jnp.exp2(s - made[1])
            total = add_up(total, jnp.sum(p.reshape(chunk // 8, 8, q_len), axis=0))
            low = p.astype(BF16)
            kept_part(kept, slot, n, chunk)[...] = low
            out = add_up(out, dot(vt[rows, pl.ds(k_at + n * chunk, chunk)], low))
        inv = 1.0 / jnp.sum(total, axis=0, keepdims=True)
        ht[rows, pl.ds(q_at, q_len)] = (out * inv).astype(BF16)
        inverse[h:h + 1, pl.ds(q_at, q_len)] = inv

    made = None
    for n, unit in enumerate(units):
        if n == 0:
            made = scores(unit)
        following = scores(units[n + 1]) if n + 1 < len(units) else None
        values(unit, made)
        made = following


def attend_back(units, v, kt, qt, gh, ght, kept, inner, inverse, dqt, dkt, dvt, q_len, k_len, chunk):
    def first(unit):
        h, slot, q_at, k_at = unit
        lanes = slice((h // 2) * 128, (h // 2) * 128 + 128)
        grads = gh[pl.ds(q_at, q_len), lanes]
        return [dot(head_mask(v[pl.ds(k_at + j, chunk), lanes], h % 2), grads, NT) for j in range(0, k_len, chunk)]

    def second(unit, made):
        h, slot, q_at, k_at = unit
        rows = slice(h * 64, h * 64 + 64)
        cols = pl.ds(q_at, q_len)
        shift = inner[h:h + 1, cols]
        part_q = None
        for n, dp in enumerate(made):
            at = pl.ds(k_at + n * chunk, chunk)
            p = kept_part(kept, slot, n, chunk)[...]
            ds = (p.astype(F32) * (dp - shift)).astype(BF16)
            dvt[rows, at] += dot(ght[rows, cols], p, NT)
            dkt[rows, at] += dot(qt[rows, cols], ds, NT)
            part_q = add_up(part_q, dot(kt[rows, at], ds))
        dqt[rows, cols] = (part_q * (inverse[h:h + 1, cols] * HEAD_DIM ** -0.5)).astype(BF16)

    made = None
    for n, unit in enumerate(units):
        if n == 0:
            made = first(unit)
        following = first(units[n + 1]) if n + 1 < len(units) else None
        second(unit, made)
        made = following


def gelu_parts(pre):
    gauss = jnp.exp2(pre * pre * (-0.5 * LOG2E))
    t = 1.0 / (1.0 + (0.3275911 / math.sqrt(2.0)) * jnp.abs(pre))
    poly = t * (0.254829592 * 0.5 + t * (-0.284496736 * 0.5 + t * (
        1.421413741 * 0.5 + t * (-1.453152027 * 0.5 + t * (1.061405429 * 0.5)))))
    tail = poly * gauss
    phi = jnp.where(pre >= 0, 1.0 - tail, tail)
    return phi, phi + pre * (gauss * (1.0 / math.sqrt(2.0 * math.pi)))


def normalise(x):
    c = x - jnp.mean(x, axis=-1, keepdims=True)
    r = lax.rsqrt(jnp.mean(c * c, axis=-1, keepdims=True) + epsilon)
    return c * r, r


def norm_back(state, gain, grad):
    xhat, r = normalise(state)
    y = grad * gain
    m1 = jnp.mean(y, axis=-1, keepdims=True)
    m2 = jnp.mean(y * xhat, axis=-1, keepdims=True)
    return r * (y - m1 - xhat * m2), jnp.sum(grad * xhat, axis=0, keepdims=True)


def block_rows(i):
    return pl.ds(pl.multiple_of(i * BLOCK, BLOCK), BLOCK)


def each(count, body):
    def step(i, carry):
        body(i)
        return carry

    lax.fori_loop(0, count, step, 0)


def layer_kernel(
    n_dp,
    lens, expert, gains, x_in, mem_in, cot_in, wqkv_in, wos_in, wq_in, wkv_in, woc_in, up_in, down_in,
    lo_out, gi_out, gm_out, e_out, a0_out, a1_out, a2_out, a3_out, a4_out, a5_out, g_out, ids_out,
    x, mem, cot, wqkv, wos, wq, wkv, woc, up, down, starts,
    s1, s2, gs, n0, n1, n2, q0, k0, v0, q1, k1, v1, vt, ht0, ht1, inv0, inv1, inner,
    kept0, kept1, kept2, gb, dkt, dvt, work, nt, cot_t, eb,
    a0, a1, a2, a3, a4, a5, ax0, ax1, ax2, ax3, ax4, ax5, ay0, ay1, ay2, ay3, ay4, ay5,
    snd, rcv, sndh, rcvh, leaving, half_out, gain_sum, g_send, g_in,
    y_send, y_recv, w_send, w_recv, c_send, c_recv, x_send, x_recv, h_send, h_recv,
    e_send, e_recv, p_send, p_recv, a_send, a_recv, g_ssem, g_rsem, o_send, o_recv, pick_sem,
):
    d, t = lax.axis_index("dp"), lax.axis_index("tp")
    c = lax.rem(d, 2)
    k2 = d - c
    row = k2 + t
    lin = d * 2 + t
    n_all = n_dp * 2
    diag = (k2 + 1 - c, 1 - t)
    sib = (k2 + 1 - c, t)
    swaps = c != t
    stays = c == t

    def remote(src, dst, ssem, rsem, to):
        return pltpu.make_async_remote_copy(
            src_ref=src, dst_ref=dst, send_sem=ssem, recv_sem=rsem, device_id=to, device_id_type=MESH)

    own = pl.ds(pl.multiple_of(c * HALF, HALF), HALF)
    other = pl.ds(pl.multiple_of((1 - c) * HALF, HALF), HALF)
    theirs = pl.ds(pl.multiple_of(t * HALF, HALF), HALF)

    X, MEM, COT, UP, DOWN = 0, 1, 2, 3, 3 + TILES
    n_brought = 3 + 2 * TILES

    def tile(f):
        return pl.ds(pl.multiple_of(f * TILE, TILE), TILE)

    def bring(n, place):
        if n < UP:
            src, dst = ((x_in, x), (mem_in, mem), (cot_in, cot))[n]
            dst = dst.at[place]
        elif n < DOWN:
            f = n - UP
            src, dst = leaving.at[f // 2, :, (f % 2) * TILE:(f % 2 + 1) * TILE], up.at[:, f * TILE:(f + 1) * TILE]
        else:
            f = n - DOWN
            src, dst = gb.at[f * TILE:(f + 1) * TILE], down.at[f * TILE:(f + 1) * TILE]
        return (lambda: remote(src, dst, y_send.at[n], y_recv.at[n], diag),
                lambda: pltpu.make_async_copy(src, dst, y_recv.at[n]))

    def picking(n):
        src = up_in.at[:, :, (n // 2) * HALF:(n // 2 + 1) * HALF] if n % 2 == 0 else down_in.at[
            :, (n // 2) * HALF:(n // 2 + 1) * HALF]
        return pltpu.make_async_copy(src, kept2, pick_sem.at[n])

    def pick(n):
        h = n // 2
        picking(n).wait()

        @pl.when(stays)
        def _():
            chosen = kept2[expert[0, 0]]
            if n % 2 == 0:
                up[:, h * HALF:(h + 1) * HALF] = chosen
            else:
                down[h * HALF:(h + 1) * HALF, :] = chosen

        @pl.when(swaps)
        def _():
            chosen = kept2[expert[0, 0]]
            if n % 2 == 0:
                leaving[h] = chosen
            else:
                gb[h * HALF:(h + 1) * HALF, :] = chosen

        if n < 3:
            picking(n + 1).start()

    def start_bring(n):
        far, near = bring(n, theirs)

        @pl.when(swaps)
        def _():
            far().start()

    def start_near(n):
        far, near = bring(n, own)

        @pl.when(stays)
        def _():
            near().start()

    def wait_bring(n):
        far, near = bring(n, own)

        @pl.when(swaps)
        def _():
            far().wait_recv()

        @pl.when(stays)
        def _():
            near().wait()

    def share(n, buf):
        return remote(buf.at[own], buf.at[own], c_send.at[n], c_recv.at[n], sib)

    def share_starts():
        return remote(starts, starts, c_send.at[3], c_recv.at[3], sib)

    n_pairs = n_dp // 2
    pair = lax.div(d, 2)
    halves = [(wqkv_in.at[1:3], wqkv.at[1:3]), (wqkv_in.at[0:1], wqkv.at[0:1]), (wos_in, wos), (wkv_in, wkv),
              (wq_in, wq), (woc_in, woc)]
    WKV0, WQ0, WOS, WKV, WQ, WOC = range(6)
    zs = n_dp // 4
    side = lax.rem(pair, 2)
    z = lax.div(d, 4)
    across = (d + 2 - 4 * side, t)

    def piece(ref, p):
        if len(ref.shape) == 3:
            rows = ref.shape[1] // n_pairs
            return ref.at[:, pl.ds(pl.multiple_of(p * rows, rows), rows)]
        rows = ref.shape[0] // n_pairs
        return ref.at[pl.ds(pl.multiple_of(p * rows, rows), rows)]

    def first_piece(n):
        src, dst = halves[n]
        return remote(piece(src, pair), piece(dst, pair), w_send.at[n, 0], w_recv.at[n, pair], diag)

    def hand_along(n, s):
        dst = halves[n][1]
        to = lax.rem(z + s, zs)
        return remote(piece(dst, pair), piece(dst, pair), w_send.at[n, s], w_recv.at[n, pair], (d + 4 * (to - z), t))

    def hand_across(n, s):
        dst = halves[n][1]
        p = lax.rem(z + s, zs) * 2 + side
        return remote(piece(dst, p), piece(dst, p), w_send.at[n, zs + s], w_recv.at[n, p], across)

    def wait_piece(n, p):
        dst = halves[n][1]
        remote(piece(dst, p), piece(dst, p), w_send.at[n, 0], w_recv.at[n, p], diag).wait_recv()

    def near_weight(n):
        src, dst = halves[n]
        return pltpu.make_async_copy(src, dst, w_recv.at[n, 0])

    def hand_round(n):
        first_piece(n).wait_recv()
        each(zs - 1, lambda s: hand_along(n, s + 1).start())
        hand_across(n, 0).start()

    def hand_on(n):
        def one(s):
            wait_piece(n, lax.rem(z + s + 1, zs) * 2 + side)
            hand_across(n, s + 1).start()

        @pl.when(swaps)
        def _():
            each(zs - 1, one)

    def wait_weight(n):
        @pl.when(swaps)
        def _():
            each(zs, lambda s: wait_piece(n, lax.rem(z + s, zs) * 2 + 1 - side))

        @pl.when(stays)
        def _():
            near_weight(n).wait()

    picking(0).start()
    start_near(X)

    @pl.when(stays)
    def _():
        near_weight(WKV0).start()
        near_weight(WQ0).start()

    start_near(MEM)
    start_near(COT)

    @pl.when(stays)
    def _():
        for n in (WOS, WKV, WQ, WOC):
            near_weight(n).start()

    barrier = pltpu.get_barrier_semaphore()

    def greet(i):
        to = lax.rem(lin + 1 + i, n_all)
        pl.semaphore_signal(barrier, inc=1, device_id=(lax.div(to, 2), lax.rem(to, 2)), device_id_type=MESH)

    each(n_all - 1, greet)

    @pl.when(stays)
    def _():
        places = lax.broadcasted_iota(jnp.int32, (8, LEN), 1)
        start, level = jnp.int32(0), jnp.zeros((8, LEN), jnp.int32)
        for s in range(lens.shape[1]):
            level = jnp.where(places >= start, start, level)
            start = start + lens[0, s]
        starts[...] = level

    pl.semaphore_wait(barrier, n_all - 1)

    @pl.when(swaps)
    def _():
        first_piece(WKV0).start()
        first_piece(WQ0).start()

    start_bring(X)

    @pl.when(swaps)
    def _():
        for n in (WOS, WKV, WQ, WOC):
            first_piece(n).start()

    start_bring(MEM)

    pick(0)

    @pl.when(stays)
    def _():
        share_starts().start()

    @pl.when(swaps)
    def _():
        hand_round(WKV0)
        hand_round(WQ0)

    pick(1)
    start_bring(UP)
    start_bring(DOWN)
    start_bring(COT)
    start_bring(UP + 1)
    start_bring(DOWN + 1)
    hand_on(WKV0)
    hand_on(WQ0)
    pick(2)

    def wait_near(n):
        near = bring(n, own)[1]

        @pl.when(stays)
        def _():
            near().wait()

    def wait_swapped(n):
        far = bring(n, own)[0]

        @pl.when(swaps)
        def _():
            far().wait_recv()

    wait_bring(X)
    share(0, x).start()

    @pl.when(swaps)
    def _():
        for n in (WOS, WKV, WQ, WOC):
            hand_round(n)

    pick(3)
    for f in range(2, TILES):
        start_bring(UP + f)
        start_bring(DOWN + f)


    @pl.when(stays)
    def _():
        wait_near(MEM)
        share(1, mem).start()
        wait_near(COT)
        share(2, cot).start()

    def self_project(i):
        r = block_rows(i)
        xhat, _ = normalise(x[r, :].astype(F32))
        nn = (xhat * gains[0:1, :]).astype(BF16)
        n0[r, :] = nn
        q0[r, :] = (dot(nn, wqkv[0]) * QSCALE).astype(BF16)
        k0[r, :] = dot(nn, wqkv[1]).astype(BF16)
        v0[r, :] = dot(nn, wqkv[2]).astype(BF16)

    wait_weight(WKV0)
    wait_weight(WQ0)
    each(2, lambda i: self_project(c * 2 + i))
    share(0, x).wait_recv()
    each(2, lambda i: self_project((1 - c) * 2 + i))
    vt[...] = v0[...].T

    @pl.when(swaps)
    def _():
        share_starts().wait_recv()

    def exchange(e, i):
        r = block_rows(i)
        return remote(snd.at[e % 2, r], rcv.at[e % 2, r], x_send.at[e, i], x_recv.at[e, i], sib)

    def out_of(e, i, ht, w_out):
        r = block_rows(i)
        snd[e % 2, r, :] = dot(ht[:, r], w_out[...], TN).astype(BF16)
        exchange(e, i).start()

    everything = range(4)
    first_bias = window_bias(0, 0, 256, 256, starts[0:1, 0:256])
    attend([(h, h, 0, 0, first_bias) for h in everything], q0, k0, vt, kept0, ht0, inv0, 256, 256, 256)

    def self_block(j):
        i = j + 1
        bias = window_bias(j * 256, i * 256, 512, 256, starts[0:1, i * 256:(i + 1) * 256])
        attend([(h, j * 4 + h, i * 256, j * 256, bias) for h in everything],
               q0, k0, vt, kept1, ht0, inv0, 256, 512, 256)

    for j, n in enumerate((WOS, WKV, WQ)):
        hand_on(n)
        self_block(j)
    wait_weight(WOS)
    each(BLOCKS, lambda i: out_of(0, i, ht0, wos))
    hand_on(WOC)

    wait_swapped(MEM)

    @pl.when(swaps)
    def _():
        share(1, mem).start()

    wait_weight(WKV)

    def memory_project(i):
        r = block_rows(i)
        k1[r, :] = dot(mem[r, :], wkv[0]).astype(BF16)
        v1[r, :] = dot(mem[r, :], wkv[1]).astype(BF16)

    each(2, lambda i: memory_project(c * 2 + i))
    share(1, mem).wait_recv()
    each(2, lambda i: memory_project((1 - c) * 2 + i))
    vt[...] = v1[...].T
    wait_weight(WQ)

    def cross_norm(i):
        r = block_rows(i)
        exchange(0, i).wait_recv()
        state = x[r, :].astype(F32) + (snd[0, r, :].astype(F32) + rcv[0, r, :].astype(F32))
        s1[r, :] = state
        xhat, _ = normalise(state)
        nn = (xhat * gains[1:2, :]).astype(BF16)
        n1[r, :] = nn
        q1[r, :] = (dot(nn, wq[...]) * QSCALE).astype(BF16)

    each(BLOCKS, cross_norm)

    wait_weight(WOC)

    def cross_pair(j):
        units = []
        for i in range(2):
            for h in everything:
                at = pl.multiple_of((j * 2 + i) * 256, 256)
                units.append((h, (j * 2 + i) * 4 + h, at, 0, None))
        attend(units, q1, k1, vt, kept2, ht1, inv1, 256, LEN, 256)
        out_of(1, j * 2, ht1, woc)
        out_of(1, j * 2 + 1, ht1, woc)

    each(BLOCKS // 2, cross_pair)

    wait_swapped(COT)

    @pl.when(swaps)
    def _():
        share(2, cot).start()

    def half_exchange(e, i):
        r = block_rows(i)
        return remote(sndh.at[e, r], rcvh.at[e, r], h_send.at[e, i], h_recv.at[e, i], sib)

    def expert_norm(i):
        r = block_rows(i)
        exchange(1, i).wait_recv()
        state = s1[r, :] + (snd[1, r, :].astype(F32) + rcv[1, r, :].astype(F32))
        s2[r, :] = state
        xhat, _ = normalise(state)
        n2[r, :] = (xhat * gains[2:3, :]).astype(BF16)

    each(2, expert_norm)
    share(2, cot).wait_recv()
    cot_t[...] = cot[...].T
    each(2, lambda i: expert_norm(i + 2))

    def begin(copy):
        copy.start()

    def finish_send(copy):
        copy.wait_send()

    def share_rows(ref, to):
        return ref.at[pl.ds(pl.multiple_of(to * 32, 32), 32)]

    def scatter(f, action):
        src, dst = eb.at[f], e_out.at[row, f]

        def one(s):
            to = lax.rem(d + s + 1, n_dp)
            action(remote(share_rows(src, to), dst, e_send.at[f, s + 1], e_recv.at[f, row], (to, c)))

        each(n_dp - 1, one)

    def scatter_near(f):
        @pl.when(stays)
        def _():
            pltpu.make_async_copy(share_rows(eb.at[f], d), e_out.at[row, f], e_recv.at[f, row]).start()
            scatter(f, begin)

    def own_far(f):
        return remote(share_rows(eb.at[f], d), e_out.at[row, f], e_send.at[f, 0], e_recv.at[f, row], (d, c))

    def scatter_far(f):
        @pl.when(swaps)
        def _():
            own_far(f).start()
            scatter(f, begin)

    def collect(f):
        def one(i):
            src, dst = eb.at[f, pl.ds(0, 32)], e_out.at[i, f]

            @pl.when(stays & (i == row))
            def _():
                pltpu.make_async_copy(src, dst, e_recv.at[f, i]).wait()

            @pl.when(jnp.logical_not(stays & (i == row)))
            def _():
                remote(src, dst, e_send.at[f, 0], e_recv.at[f, i], diag).wait_recv()

        each(n_dp, one)

    hid, gpre = work.at[0:LEN], work.at[LEN:2 * LEN]

    def expert_tile(f):
        cols = slice(f * TILE, (f + 1) * TILE)

        def first(i):
            r = slice(i * BLOCK, (i + 1) * BLOCK)
            return dot(n2[r, :], up[:, cols]), dot(cot[r, :], down[cols, :], NT)

        def second(i, made):
            r = slice(i * BLOCK, (i + 1) * BLOCK)
            pre, grad = made
            phi, slope = gelu_parts(pre)
            hid[r, cols] = (pre * phi).astype(BF16)
            gpre[r, cols] = (grad * slope).astype(BF16)

        made = first(0)
        for i in range(BLOCKS):
            following = first(i + 1) if i + 1 < BLOCKS else None
            second(i, made)
            made = following

    def expert_back(i):
        r = block_rows(i)
        snd[0, r, :] = dot(gpre[r, :], up[...], NT).astype(BF16)
        exchange(2, i).start()

    def expert_out(i):
        r = block_rows(i)
        part = dot(hid[r, :], down[...])
        mine = lax.div(i, 2) == c
        rl = block_rows(lax.rem(i, 2))

        @pl.when(mine)
        def _():
            half_out[rl, :] = s2[r, :] + part

        @pl.when(jnp.logical_not(mine))
        def _():
            sndh[0, rl, :] = part.astype(BF16)
            half_exchange(0, lax.rem(i, 2)).start()

    def expert_grads(f):
        cols = slice(f * TILE, (f + 1) * TILE)
        eb[f, :, 0:TILE] = dot(nt[...], gpre[:, cols]).astype(BF16)
        eb[f, :, TILE:2 * TILE] = dot(cot_t[...], hid[:, cols]).astype(BF16)

    def done_sending(e):
        each(BLOCKS, lambda i: exchange(e, i).wait_send())

    done_sending(0)
    for f in range(TILES):
        wait_swapped(UP + f)
        wait_swapped(DOWN + f)
        expert_tile(f)
        if f == 0:
            nt[...] = n2[...].T
        if f + 1 < TILES:
            expert_grads(f)
            scatter_near(f)
        if f + 2 == TILES:
            scatter_far(0)

    @pl.when(swaps)
    def _():
        for n in range(UP, n_brought):
            bring(n, theirs)[0]().wait_send()

    each(BLOCKS, expert_back)
    scatter_far(1)
    expert_grads(TILES - 1)
    scatter_near(TILES - 1)
    scatter_far(2)
    scatter_far(3)
    each(BLOCKS, expert_out)

    def strip(n):
        return work.at[n * COLS:(n + 1) * COLS]

    dqt, dkb, dvb, ght = strip(0), strip(1), strip(2), strip(3)
    kt, qt = cot_t.at[0:COLS], cot_t.at[COLS:2 * COLS]
    dq, dk = down.at[:, 0:COLS], down.at[:, COLS:2 * COLS]
    gh, dv = n2.at[:, 0:COLS], n2.at[:, COLS:2 * COLS]
    gain_sum[...] = jnp.zeros_like(gain_sum)

    def branch_block(n, i, e, state, base, ht, inv, w_out):
        r = block_rows(i)
        exchange(e, i).wait_recv()
        grad = snd[e % 2, r, :].astype(F32) + rcv[e % 2, r, :].astype(F32)
        step, share_gain = norm_back(state[r, :], gains[n:n + 1, :], grad)
        moved = base[r, :].astype(F32) + step
        gs[r, :] = moved
        low = moved.astype(BF16)
        gb[r, :] = low
        gain_sum[n:n + 1, :] += jnp.where(lax.div(i, 2) == c, share_gain, 0.0)
        gh[r, :] = dot(low, w_out[...], NT).astype(BF16)
        turned = dot(w_out[...], low, NT).astype(BF16).astype(F32)
        prod = turned * ht[:, r].astype(F32)
        for h in everything:
            rows = slice(h * 64, h * 64 + 64)
            inner[h:h + 1, r] = jnp.sum(prod[rows], axis=0, keepdims=True)
            ght[rows, r] = (turned[rows] * inv[h:h + 1, r]).astype(BF16)

    def turn_queries(q, k, inv):
        kt[...] = k[...].T
        turned = q[...].T
        for h in everything:
            rows = slice(h * 64, h * 64 + 64)
            qt[rows, :] = (turned[rows].astype(F32) * inv[h:h + 1, :]).astype(BF16)
        dkt[...] = jnp.zeros_like(dkt)
        dvt[...] = jnp.zeros_like(dvt)

    pieces = tuple(zip((a0, a1, a2, a3, a4, a5), (ax0, ax1, ax2, ax3, ax4, ax5), (ay0, ay1, ay2, ay3, ay4, ay5),
                       (a0_out, a1_out, a2_out, a3_out, a4_out, a5_out)))
    n_pieces = len(pieces)

    def over_x(n):
        buf, place = pieces[n][:2]
        return remote(buf.at[:, 1 - side], place, p_send.at[0, n], p_recv.at[0, n], across)

    def over_y(n):
        buf, place = pieces[n][0], pieces[n][2]
        return remote(buf.at[:, side], place, p_send.at[1, n], p_recv.at[1, n], (d, c))

    def add_x(n):
        buf, place = pieces[n][:2]
        over_x(n).wait_recv()
        buf[:, side] = (buf[:, side].astype(F32) + place[...].astype(F32)).astype(BF16)

        @pl.when(swaps)
        def _():
            over_y(n).start()

    def owners(n, action):
        buf, out = pieces[n][0], pieces[n][3]

        def one(s):
            to = lax.rem(z * 2 + c + s + 1, 2 * zs)
            to_z, to_c = lax.div(to, 2), lax.rem(to, 2)
            src = buf.at[to_z, side, pl.ds(pl.multiple_of(to_c * 32, 32), 32)]
            action(remote(src, out.at[z], a_send.at[n, s], a_recv.at[n, z], (to_z * 4 + side * 2 + to_c, t)))

        each(2 * zs - 1, one)

    def own_share(n):
        src = pieces[n][0].at[z, side, pl.ds(pl.multiple_of(c * 32, 32), 32)]
        return pltpu.make_async_copy(src, pieces[n][3].at[z], a_recv.at[n, z])

    def add_y(n):
        @pl.when(stays)
        def _():
            buf, place = pieces[n][0], pieces[n][2]
            over_y(n).wait_recv()
            buf[:, side] = (buf[:, side].astype(F32) + place[...].astype(F32)).astype(BF16)
            own_share(n).start()
            owners(n, begin)

    def collect_piece(n):
        buf, out = pieces[n][0], pieces[n][3]

        def one(i):
            @pl.when(stays & (i == z))
            def _():
                own_share(n).wait()

            @pl.when(jnp.logical_not(stays & (i == z)))
            def _():
                remote(buf.at[0, 0, pl.ds(0, 32)], out.at[i], a_send.at[n, 0], a_recv.at[n, i], diag).wait_recv()

        each(zs, one)

        @pl.when(stays)
        def _():
            owners(n, finish_send)

        @pl.when(swaps)
        def _():
            over_y(n).wait_send()

        over_x(n).wait_send()

    def by_owner(grad):
        return grad.astype(BF16).T.reshape(zs, 2, WIDTH // (2 * zs), grad.shape[0])

    each(BLOCKS, lambda i: branch_block(2, i, 2, s2, cot, ht1, inv1, woc))
    def leave(n, out):
        buf = leaving.at[n]
        return (lambda: remote(buf, out, o_send.at[n], o_recv.at[n], diag),
                lambda: pltpu.make_async_copy(buf, out, o_recv.at[n]))

    def start_leave(n, out):
        far, near = leave(n, out)

        @pl.when(swaps)
        def _():
            far().start()

        @pl.when(stays)
        def _():
            near().start()

    def wait_leave(n, out):
        far, near = leave(n, out)

        @pl.when(swaps)
        def _():
            far().wait()

        @pl.when(stays)
        def _():
            near().wait()

    def half_done(n):
        def one(low):
            half_exchange(n, low).wait_recv()
            r = block_rows(low)
            leaving[n, r, :] = (half_out[r, :] + rcvh[n, r, :].astype(F32)).astype(BF16)

        each(2, one)

    half_done(0)
    start_leave(0, lo_out)
    a0[...] = by_owner(dot(ht1[...], gb[...]))
    over_x(0).start()
    turn_queries(q1, k1, inv1)

    def pair_grads(pair_of_heads, n, source_q, source_kv):
        rows = slice(pair_of_heads * 128, pair_of_heads * 128 + 128)
        dkb[rows, :] = (dkt[rows, :] * math.log(2.0)).astype(BF16)
        dvb[rows, :] = dvt[rows, :].astype(BF16)
        buf = pieces[n][0]
        for part, (grad, source) in enumerate(((dqt, source_q), (dkb, source_kv), (dvb, source_kv))):
            buf[:, :, :, part * 128:part * 128 + 128] = by_owner(dot(grad[rows, :], source[...]))
        over_x(n).start()

    def cross_back(pair_of_heads):
        heads = (2 * pair_of_heads, 2 * pair_of_heads + 1)
        units = [(h, i * 4 + h, i * 256, 0) for h in heads for i in range(BLOCKS)]
        attend_back(units, v1, kt, qt, gh, ght, kept2, inner, inv1, dqt, dkt, dvt, 256, LEN, 256)
        pair_grads(pair_of_heads, 1 + pair_of_heads, n1, mem)

    cross_back(0)
    cross_back(1)

    def settle():
        dq[...] = dqt[...].T
        dk[...] = dkb[...].T
        dv[...] = dvb[...].T

    add_x(0)
    settle()
    done_sending(1)

    def cross_grads(i):
        r = block_rows(i)
        snd[1, r, :] = dot(dq[r, :], wq[...], NT).astype(BF16)
        exchange(3, i).start()

    each(BLOCKS, cross_grads)
    def memory_grads(i):
        r = block_rows(i)
        part = dot(dk[r, :], wkv[0], NT) + dot(dv[r, :], wkv[1], NT)
        mine = lax.div(i, 2) == c
        rl = block_rows(lax.rem(i, 2))

        @pl.when(mine)
        def _():
            half_out[rl, :] = part

        @pl.when(jnp.logical_not(mine))
        def _():
            sndh[1, rl, :] = part.astype(BF16)
            half_exchange(1, lax.rem(i, 2)).start()

    each(BLOCKS, memory_grads)
    add_x(1)

    each(BLOCKS, lambda i: branch_block(1, i, 3, s1, gs, ht0, inv0, wos))
    half_done(1)
    start_leave(1, gm_out)
    turn_queries(q0, k0, inv0)

    def self_back(pair_of_heads):
        heads = (2 * pair_of_heads, 2 * pair_of_heads + 1)
        attend_back([(h, h, 0, 0) for h in heads], v0, kt, qt, gh, ght, kept0, inner, inv0, dqt, dkt, dvt, 256, 256, 256)
        units = [(h, j * 4 + h, (j + 1) * 256, j * 256) for h in heads for j in range(BLOCKS - 1)]
        attend_back(units, v0, kt, qt, gh, ght, kept1, inner, inv0, dqt, dkt, dvt, 256, 512, 256)
        pair_grads(pair_of_heads, 4 + pair_of_heads, n0, n0)

    a3[...] = by_owner(dot(ht0[...], gb[...]))
    over_x(3).start()
    self_back(0)
    add_x(2)
    self_back(1)
    settle()

    def input_grads(i):
        r = block_rows(i)
        return dot(dq[r, :], wqkv[0], NT) + dot(dk[r, :], wqkv[1], NT) + dot(dv[r, :], wqkv[2], NT)

    def input_send(low):
        sndh[2, block_rows(low), :] = input_grads((1 - c) * 2 + low).astype(BF16)
        half_exchange(2, low).start()

    each(2, input_send)

    def input_keep(low):
        half_out[block_rows(low), :] = input_grads(c * 2 + low)

    each(2, input_keep)

    def input_done(low):
        half_exchange(2, low).wait_recv()
        rl = block_rows(low)
        r = block_rows(c * 2 + low)
        grad = half_out[rl, :] + rcvh[2, rl, :].astype(F32)
        step, share_gain = norm_back(x[r, :].astype(F32), gains[0:1, :], grad)
        gain_sum[0:1, :] += share_gain
        leaving[2, rl, :] = (gs[r, :] + step).astype(BF16)

    each(2, input_done)
    start_leave(2, gi_out)
    add_y(0)
    add_x(3)

    number = jnp.full((1, 128), expert[0, 0].astype(F32))
    for j in range(n_dp):
        turned = gain_sum[...] if j == 0 else pltpu.roll(gain_sum[...], (WIDTH - 32 * j) % WIDTH, 1)
        g_send[j] = turned[:, :128]
        g_send[j, 3:4, :] = number

    def gain_copy(s):
        to = lax.rem(lin + s, n_all)
        to_dp = lax.div(to, 2)
        return remote(g_send.at[to_dp], g_in.at[lin], g_ssem.at[s], g_rsem.at[lin], (to_dp, lax.rem(to, 2)))

    each(n_all - 1, lambda s: gain_copy(s + 1).start())
    keep_gain = pltpu.make_async_copy(g_send.at[d], g_in.at[lin], g_rsem.at[lin])
    keep_gain.start()

    add_y(1)
    add_x(4)
    add_y(2)
    add_x(5)
    add_y(3)
    add_y(4)
    add_y(5)

    wait_leave(0, lo_out)
    wait_leave(1, gm_out)
    wait_leave(2, gi_out)
    for f in range(TILES):
        collect(f)
        scatter(f, finish_send)

        @pl.when(swaps)
        def _():
            own_far(f).wait_send()

    for n in range(n_pieces):
        collect_piece(n)
    keep_gain.wait()

    def gain_wait(s):
        gain_copy(s + 1).wait_send()
        who = lax.rem(lin + s + 1, n_all)
        remote(g_send.at[0], g_in.at[who], g_ssem.at[0], g_rsem.at[who], diag).wait_recv()

    each(n_all - 1, gain_wait)
    g_out[...] = jnp.sum(g_in[...], axis=0)
    for r in range(n_dp):
        ids_out[r:r + 1, :] = g_in[2 * r, 3:4, :]

    @pl.when(swaps)
    def _():
        for n in range(UP):
            bring(n, theirs)[0]().wait_send()
        for n in range(6):
            first_piece(n).wait_send()
            each(zs - 1, lambda s: hand_along(n, s + 1).wait_send())
            each(zs, lambda s: hand_across(n, s).wait_send())

    for n, buf in enumerate((x, mem, cot)):
        share(n, buf).wait_send()

    @pl.when(stays)
    def _():
        share_starts().wait_send()

    done_sending(2)
    done_sending(3)
    for e in range(3):
        each(2, lambda i: half_exchange(e, i).wait_send())


VMEM_BYTES = 63 * 2**20
ANY_PLACE = pl.BlockSpec(memory_space=pl.ANY)
IN_HBM = pl.BlockSpec(memory_space=pltpu.HBM)
IN_SMEM = pl.BlockSpec(memory_space=pltpu.SMEM)
IN_VMEM = pl.BlockSpec(memory_space=pltpu.VMEM)


def paired_layer(n_dp, lens, expert, gains, *arrays):
    bf = lambda *shape: pltpu.VMEM(shape, BF16)
    fl = lambda *shape: pltpu.VMEM(shape, F32)
    dma = lambda *shape: pltpu.SemaphoreType.DMA(shape)
    tokens = bf(LEN, WIDTH)
    heads = bf(LEN, COLS)
    turned = bf(COLS, LEN)
    half = jax.ShapeDtypeStruct((HALF, WIDTH), BF16)
    zs = n_dp // 4
    sizes = PIECES
    split = [bf(zs, 2, WIDTH // (2 * zs), size) for size in sizes]
    x_parts = [bf(zs, WIDTH // (2 * zs), size) for size in sizes]
    return pl.pallas_call(
        partial(layer_kernel, n_dp),
        out_shape=(half, half, half, jax.ShapeDtypeStruct((n_dp, TILES, 32, 2 * TILE), BF16),
                   *[jax.ShapeDtypeStruct((zs, 32, size), BF16) for size in sizes],
                   jax.ShapeDtypeStruct((8, 128), F32), jax.ShapeDtypeStruct((n_dp, 128), F32)),
        in_specs=[IN_SMEM] * 2 + [IN_VMEM] + [ANY_PLACE] * 10,
        out_specs=(ANY_PLACE,) * (4 + len(sizes)) + (IN_VMEM,) * 2,
        scratch_shapes=[
            tokens, tokens, tokens, bf(3, WIDTH, COLS), bf(COLS, WIDTH), bf(WIDTH, COLS), bf(2, WIDTH, COLS),
            bf(COLS, WIDTH), bf(WIDTH, HIDDEN), bf(HIDDEN, WIDTH), pltpu.VMEM((8, LEN), jnp.int32),
            fl(LEN, WIDTH), fl(LEN, WIDTH), fl(LEN, WIDTH), tokens, tokens, tokens,
            heads, heads, heads, heads, heads, heads, turned, turned, turned, fl(8, LEN), fl(8, LEN), fl(8, LEN),
            bf(4, 256, 256), bf(12, 512, 256), bf(n_dp, WIDTH, WIDTH), tokens, fl(COLS, LEN), fl(COLS, LEN),
            bf(2 * LEN, HIDDEN), bf(WIDTH, LEN), bf(WIDTH, LEN), bf(TILES, WIDTH, 2 * TILE), *split, *x_parts, *x_parts,
            bf(2, LEN, WIDTH), bf(2, LEN, WIDTH), bf(3, HALF, WIDTH), bf(3, HALF, WIDTH), bf(3, HALF, WIDTH),
            fl(HALF, WIDTH), fl(8, WIDTH), fl(n_dp, 8, 128), fl(2 * n_dp, 8, 128),
            dma(3 + 2 * TILES), dma(3 + 2 * TILES), dma(6, n_dp // 2), dma(6, n_dp // 2), dma(4), dma(4),
            dma(4, 4), dma(4, 4), dma(3, 2), dma(3, 2),
            dma(TILES, n_dp), dma(TILES, n_dp), dma(2, len(sizes)), dma(2, len(sizes)), dma(len(sizes), 2 * zs), dma(len(sizes), zs),
            dma(2 * n_dp), dma(2 * n_dp), dma(3), dma(3), dma(4),
        ],
        compiler_params=pltpu.CompilerParams(
            collective_id=0, has_side_effects=True, vmem_limit_bytes=VMEM_BYTES),
        cost_estimate=pl.CostEstimate(flops=20 * 10**9, bytes_accessed=20 * 2**20, transcendentals=0),
    )(lens, expert, gains, *arrays)


def place_kernel(
    ids_any, gains_any, e_any, a0_any, a1_any, a2_any, a3_any, a4_any, a5_any, gi_any, gm_any, lo_any,
    lo_out, gi_out, gm_out, gain_out, qkv_out, os_out, q_out, kv_out, oc_out, up_out, down_out,
    ids, ids_in, gains_in, e_in, a0_in, a1_in, a2_in, a3_in, a4_in, a5_in, gi_in, gm_in, lo_in, gi_v, gm_v, gain_v, qkv_v, os_v, q_v, kv_v, oc_v,
    ups, downs, in_sems, e_sems, up_sems, down_sems, out_sems,
):
    rows = e_in.shape[0]
    number = pltpu.make_async_copy(ids_any, ids, in_sems.at[0])
    number.start()
    pairs = ((gi_any, gi_in), (gm_any, gm_in), (lo_any, lo_in), (gains_any, gains_in), (a0_any, a0_in),
             (a1_any, a1_in), (a2_any, a2_in), (a3_any, a3_in), (a4_any, a4_in), (a5_any, a5_in))
    reads = [pltpu.make_async_copy(src, dst, in_sems.at[1 + n]) for n, (src, dst) in enumerate(pairs)]
    blocks = [pltpu.make_async_copy(e_any.at[r], e_in.at[r], e_sems.at[r]) for r in range(rows)]
    for copy in reads + blocks:
        copy.start()
    writes = []

    def write(src, dst, sem):
        writes.append(pltpu.make_async_copy(src, dst, sem))
        writes[-1].start()

    reads[0].wait()
    gi_v[...] = gi_in[...].astype(F32)
    write(gi_v, gi_out, out_sems.at[0])
    reads[1].wait()
    gm_v[...] = gm_in[...].astype(F32)
    write(gm_v, gm_out, out_sems.at[1])
    reads[2].wait()
    write(lo_in, lo_out, out_sems.at[2])
    for copy in reads[3:]:
        copy.wait()
    gain_v[...] = gains_in[0:3, 0:32]
    oc_v[...] = jnp.sum(a0_in[...].astype(F32), axis=0)
    os_v[...] = jnp.sum(a3_in[...].astype(F32), axis=0)
    for pair, (cross, own) in enumerate(((a1_in, a4_in), (a2_in, a5_in))):
        cols = slice(pair * 128, pair * 128 + 128)
        cross = jnp.sum(cross[...].astype(F32), axis=0)
        own = jnp.sum(own[...].astype(F32), axis=0)
        q_v[:, cols] = cross[:, 0:128]
        for n in range(2):
            kv_v[n, :, cols] = cross[:, 128 + n * 128:256 + n * 128]
        for n in range(3):
            qkv_v[n, :, cols] = own[:, n * 128:n * 128 + 128]
    small = ((gain_v, gain_out), (qkv_v, qkv_out), (os_v, os_out), (q_v, q_out), (kv_v, kv_out), (oc_v, oc_out))
    for n, (src, dst) in enumerate(small):
        write(src, dst, out_sems.at[3 + n])
    number.wait()
    for r in range(rows):
        blocks[r].wait()
        for f in range(TILES):
            ups[r, :, f * TILE:(f + 1) * TILE] = e_in[r, f, :, 0:TILE].astype(F32)
            downs[r, :, f * TILE:(f + 1) * TILE] = e_in[r, f, :, TILE:2 * TILE].astype(F32)
        e = ids[r, 0].astype(jnp.int32)
        write(ups.at[r], up_out.at[e], up_sems.at[r])
        write(downs.at[r], down_out.at[e], down_sems.at[r])
    for copy in writes:
        copy.wait()


def place_grads(experts, *arrays):
    shape = lambda *dims: jax.ShapeDtypeStruct(dims, F32)
    like = lambda array: pltpu.VMEM(array.shape, array.dtype)
    dma = lambda *dims: pltpu.SemaphoreType.DMA(dims)
    rows = arrays[2].shape[0]
    staged = pltpu.VMEM((rows, 32, HIDDEN), F32)
    half = pltpu.VMEM((HALF, WIDTH), F32)
    small = [pltpu.VMEM(dims, F32) for dims in ((3, 32), (3, 32, COLS), (32, COLS), (32, COLS), (2, 32, COLS), (32, COLS))]
    return pl.pallas_call(
        place_kernel,
        out_shape=(jax.ShapeDtypeStruct((HALF, WIDTH), BF16), shape(HALF, WIDTH), shape(HALF, WIDTH), shape(3, 32), shape(3, 32, COLS), shape(32, COLS),
                   shape(32, COLS), shape(2, 32, COLS), shape(32, COLS),
                   shape(experts, 32, HIDDEN), shape(experts, 32, HIDDEN)),
        in_specs=[IN_HBM] * 12,
        out_specs=(IN_HBM,) * 11,
        scratch_shapes=[pltpu.SMEM(arrays[0].shape, F32)] + [like(array) for array in arrays] + [
            half, half, *small, staged, staged, dma(11), dma(rows), dma(rows), dma(rows), dma(9)],
        compiler_params=pltpu.CompilerParams(vmem_limit_bytes=VMEM_BYTES),
    )(*arrays)


def per_device_paired(
    layer_input, memory, seg_lengths, expert_ids, ln_gains, w_qkv, w_out_self, w_query_cross, w_kv_cross,
    w_out_cross, w_up, w_down, cotangent,
):
    n_dp = lax.axis_size("dp")
    layer_output, grad_input, grad_memory, e_rows, *a_rows, gain_rows, numbers = paired_layer(
        n_dp, seg_lengths, expert_ids, ln_gains,
        layer_input[0], memory[0], cotangent[0], w_qkv, w_out_self, w_query_cross, w_kv_cross, w_out_cross, w_up, w_down,
    )
    layer_output, grad_input, grad_memory, gain_share, qkv, out_self, query, key_value, out_cross, grad_up, grad_down = place_grads(
        w_up.shape[0], numbers, gain_rows, e_rows, *a_rows, grad_input, grad_memory, layer_output)
    return (
        layer_output[None], grad_input[None], grad_memory[None], gain_share, qkv, out_self.T, query, key_value,
        out_cross.T, grad_up, jnp.swapaxes(grad_down, 1, 2),
    )


def fits_pairs(mesh, layer_input, seg_lengths, w_up):
    return (
        mesh.shape["tp"] == 2
        and mesh.shape["dp"] == 16
        and layer_input.shape == (mesh.shape["dp"], LEN, WIDTH)
        and w_up.shape == (mesh.shape["dp"], WIDTH, 2 * HIDDEN)
    )


def solution(mesh):
    in_specs = (
        P("dp", "tp", None),
        P("dp", "tp", None),
        P("dp", None),
        P("dp", None),
        P(),
        P(None, None, "tp"),
        P("tp", None),
        P(None, "tp"),
        P(None, None, "tp"),
        P("tp", None),
        P(None, None, "tp"),
        P(None, "tp", None),
        P("dp", "tp", None),
    )
    out_specs = (
        P("dp", "tp", None),
        P("dp", "tp", None),
        P("dp", "tp", None),
        P(None, "dp"),
        P(None, "dp", "tp"),
        P("tp", "dp"),
        P("dp", "tp"),
        P(None, "dp", "tp"),
        P("tp", "dp"),
        P(None, "dp", "tp"),
        P(None, "tp", "dp"),
    )

    def run(*args):
        layer_input, seg_lengths, w_up = args[0], args[2], args[10]
        paired = fits_pairs(mesh, layer_input, seg_lengths, w_up)
        return jax.shard_map(
            per_device_paired if paired else per_device,
            mesh=mesh, in_specs=in_specs, out_specs=out_specs, check_vma=False,
        )(*args)

    return run
```
